32 devices in a mesh: blk: 8 (over z, x), rep: 4 (over y, core).
Axes of the slice: x: 2, y: 2, z: 4, core: 2. Of those that a mesh axis runs over, the one named last changes fastest.
Arguments:
- node_feats: bfloat16 [16384, 128], P(('blk', 'rep')), may hold values from -6 to 6
- adj_tiles: bfloat16 [128, 4, 4, 128, 128], P('blk', 'rep'), as said below
- col_index: int32 [128, 4, 4], P('blk', 'rep'), may hold values from 0 to 31, as said below
- w_in: bfloat16 [128, 512], replicated, may hold values from -0.5 to 0.5
- b_in: float32 [512], replicated, may hold values from -3 to 3
- w_out: bfloat16 [512, 128], replicated, may hold values from -0.25 to 0.25
- b_out: float32 [128], replicated, may hold values from -3 to 3
- cot_out: bfloat16 [16384, 128], P(('blk', 'rep')), may hold values from -6 to 6
Outputs:
- out_feats: bfloat16 [16384, 128], P(('blk', 'rep'))
- grad_feats: bfloat16 [16384, 128], P(('blk', 'rep'))
The draws below stay inside these ranges and needn't reach their ends.
Inputs may be any that keep to these rules, and one draw needn't show every extreme that they name: The matrix A described by adj_tiles and col_index is symmetric (A equals its transpose). `col_index`: column block numbers within a quarter.
All inputs are finite; a program needn't handle non-finite values.
Results may differ from the reference program's by a relative error of at most 0.0045.
Values may be sent and summed in bfloat16 or wider, within the bound.
No kernel may reach another device: no remote copies, remote signals or barrier semaphores. Data moves between devices by JAX's collectives and lax.ppermute only.
A program may use at most 128 MiB of HBM per device.

```python
import jax
import jax.numpy as jnp
from jax import lax

WIDTH = 128
MLP_UNITS = 512
BLOCK = 128
KQ = 4
ROWS_DEV = 2048
NODES = 16384
NBLOCKS = 128
N_BLK = 8


def pairing(key):
    half = KQ // 2
    quarter_blocks = NODES // (4 * BLOCK)
    per_shard = ROWS_DEV // (4 * BLOCK)
    keys = jax.random.split(jax.random.fold_in(key, 11), half * 16)
    perms = jax.vmap(lambda one_key: jax.random.permutation(one_key, quarter_blocks))(keys)
    perms = perms.reshape(half, 4, 4, quarter_blocks).astype(jnp.int32)
    inverse = jnp.argsort(perms, axis=-1, stable=True).astype(jnp.int32)
    rows = jnp.arange(NBLOCKS, dtype=jnp.int32)
    own_quarter = rows // per_shard % 4
    position = rows // (4 * per_shard) * per_shard + rows % per_shard
    quarters = jnp.arange(4, dtype=jnp.int32)
    forward = perms[:, own_quarter[:, None], quarters[None, :], position[:, None]]
    backward = inverse[:, quarters[None, :], own_quarter[:, None], position[:, None]]
    forward = jnp.transpose(forward, (1, 2, 0))
    backward = jnp.transpose(backward, (1, 2, 0))
    source = backward // per_shard * 4 * per_shard + quarters[None, :, None] * per_shard + backward % per_shard
    columns = jnp.concatenate([forward, backward], axis=-1).astype(jnp.int32)
    return (columns, source.astype(jnp.int32), own_quarter)


def draw_col_index(key, part):
    columns, source, own_quarter = pairing(key)
    return columns


def draw_adj_tiles(key, part):
    columns, source, own_quarter = pairing(key)
    half = KQ // 2
    scale = (BLOCK * 4 * KQ) ** (-0.5)
    shape = (NBLOCKS, 4, half, BLOCK, BLOCK)
    base = jax.random.normal(jax.random.fold_in(key, 12), shape, jnp.float32) * scale
    slots = jnp.arange(half, dtype=jnp.int32)
    mirrored = base[source, own_quarter[:, None, None], slots[None, None, :]]
    mirrored = jnp.swapaxes(mirrored, -1, -2)
    return jnp.concatenate([base, mirrored], axis=2).astype(jnp.bfloat16)


def level_of(key, shape, cuts, low, top_value):
    factor_of = 1.0
    for axis_at, blocks in cuts:
        heights = jax.random.uniform(jax.random.fold_in(jax.random.fold_in(key, 6), axis_at), (blocks,), jnp.float32, low / len(cuts), top_value / len(cuts))
        factor_of = factor_of * jnp.repeat(jnp.exp(heights), shape[axis_at] // blocks).reshape((-1,) + (1,) * (len(shape) - 1 - axis_at))
    return factor_of


def normal_values(own_key, shape, deviation, most, cuts=(), kind=jnp.bfloat16):
    factor_of = level_of(own_key, shape, cuts, -0.22, 0.18) if cuts else 1.0
    array = jax.random.normal(own_key, shape, jnp.float32) * deviation * factor_of
    return jnp.minimum(jnp.maximum(array, -most), most).astype(kind)


def setup_inputs(seed: int = 0) -> dict:
    arg_keys = jax.random.split(jax.random.key(seed), 9)
    return {
        "node_feats": normal_values(arg_keys[0], (NODES, WIDTH), 1.0, 6.0, ((0, 32),)),
        "adj_tiles": draw_adj_tiles(jax.random.fold_in(arg_keys[8], 71), 0),
        "col_index": draw_col_index(jax.random.fold_in(arg_keys[8], 71), 0),
        "w_in": normal_values(arg_keys[3], (WIDTH, MLP_UNITS), WIDTH ** -0.5, 0.5),
        "b_in": normal_values(arg_keys[4], (MLP_UNITS,), 0.5, 3.0, (), jnp.float32),
        "w_out": normal_values(arg_keys[5], (MLP_UNITS, WIDTH), MLP_UNITS ** -0.5, 0.25),
        "b_out": normal_values(arg_keys[6], (WIDTH,), 0.5, 3.0, (), jnp.float32),
        "cot_out": normal_values(arg_keys[7], (NODES, WIDTH), 1.0, 6.0, ((0, 32),)),
    }


def quarter_panel(feats, quarter):
    return feats.reshape(N_BLK, 4, ROWS_DEV // 4, WIDTH)[:, quarter].reshape(-1, BLOCK, WIDTH)


def aggregate(feats, adj_tiles, col_index):
    def one_quarter(quarter):
        grouped = quarter_panel(feats, quarter)
        picked = grouped[col_index[:, quarter, :]].astype(jnp.float32)
        tiles_here = adj_tiles[:, quarter].astype(jnp.float32)
        return jnp.einsum("gkij,gkjh->gih", tiles_here, picked)

    parts = lax.map(one_quarter, jnp.arange(4, dtype=jnp.int32))
    return jnp.sum(parts, axis=0).reshape(NODES, WIDTH)


def adjoint(grads, adj_tiles, col_index):
    blocks = grads.reshape(NBLOCKS, BLOCK, WIDTH).astype(jnp.float32)

    def one_quarter(quarter):
        tiles_here = adj_tiles[:, quarter].astype(jnp.float32)
        contrib = jnp.einsum("gkij,gih->gkjh", tiles_here, blocks)
        return jax.ops.segment_sum(contrib.reshape(-1, BLOCK, WIDTH), col_index[:, quarter, :].reshape(-1), num_segments=NODES // (4 * BLOCK))

    parts = lax.map(one_quarter, jnp.arange(4, dtype=jnp.int32))
    parts = parts.reshape(4, N_BLK, ROWS_DEV // 4, WIDTH)
    return jnp.transpose(parts, (1, 0, 2, 3)).reshape(NODES, WIDTH)


def reference(node_feats, adj_tiles, col_index, w_in, b_in, w_out, b_out, cot_out):
    agg = aggregate(node_feats, adj_tiles, col_index)
    agg_b = agg.astype(jnp.bfloat16)
    pre = jnp.dot(agg_b, w_in, preferred_element_type=jnp.float32) + b_in
    hidden = jax.nn.silu(pre).astype(jnp.bfloat16)
    projected = jnp.dot(hidden, w_out, preferred_element_type=jnp.float32) + b_out
    out_feats = (node_feats.astype(jnp.float32) + projected).astype(jnp.bfloat16)
    g_hidden = jnp.dot(cot_out, w_out.T, preferred_element_type=jnp.float32)
    sigma = jax.nn.sigmoid(pre)
    g_pre = (g_hidden * sigma * (1.0 + pre * (1.0 - sigma))).astype(jnp.bfloat16)
    g_agg = jnp.dot(g_pre, w_in.T, preferred_element_type=jnp.float32).astype(jnp.bfloat16)
    back_rows = adjoint(g_agg, adj_tiles, col_index)
    grad_feats = (cot_out.astype(jnp.float32) + back_rows).astype(jnp.bfloat16)
    return (out_feats, grad_feats)
```

```python
import functools

import jax
import jax.numpy as jnp
from jax import lax
from jax.experimental import pallas as pl
from jax.experimental.pallas import tpu as pltpu
from jax.sharding import PartitionSpec as P

BLOCK = 128
VMEM = pl.BlockSpec(memory_space=pltpu.VMEM)
SMEM = pl.BlockSpec(memory_space=pltpu.SMEM)


DIRECT = 8


def gather_blocks(rows):
    n = lax.axis_size("blk")
    if n > DIRECT:
        return [lax.all_gather(rows, "blk", axis=0, tiled=True)]
    got = [rows]
    for d in range(1, n):
        pairs = [((i + d) % n, i) for i in range(n)]
        got.append(lax.ppermute(rows, "blk", pairs))
    return got


def product_kernel(n_pieces, where, columns, tiles, *refs):
    pieces, outs, panel = refs[:n_pieces], refs[n_pieces:-1], refs[-1]
    blk, rep = where[0], where[1]
    reps = len(outs)
    rows = outs[0].shape[0]
    total = panel.shape[0] // BLOCK
    if n_pieces == 1:
        blk, panel = 0, pieces[0]
    else:
        for d, piece in enumerate(pieces):
            panel[pl.ds(d * rows, rows), :] = piece[...]
    per_shard = rows // BLOCK
    for d, out in enumerate(outs):
        quarter = lax.rem(rep + d, reps)
        for i in range(per_shard):
            g = quarter * per_shard + i
            picked = []
            for k in range(tiles.shape[2]):
                c = columns[g, k] - blk * per_shard
                c = jnp.where(c < 0, c + total, c)
                start = pl.multiple_of(c * BLOCK, BLOCK)
                picked.append(panel[pl.ds(start, BLOCK), :])
            left = jnp.concatenate([tiles[g, 0, k] for k in range(tiles.shape[2])], axis=1)
            right = jnp.concatenate(picked, axis=0)
            summed = jnp.dot(left, right, preferred_element_type=jnp.float32)
            out[pl.ds(i * BLOCK, BLOCK), :] = summed.astype(out.dtype)


def tile_products(pieces, adj_tiles, columns, where):
    reps = lax.axis_size("rep")
    width = pieces[0].shape[1]
    rows = adj_tiles.shape[0] * BLOCK // reps
    length = sum(piece.shape[0] for piece in pieces)
    kinds = [jnp.float32] + [jnp.bfloat16] * (reps - 1)
    return pl.pallas_call(
        functools.partial(product_kernel, len(pieces)),
        out_shape=[jax.ShapeDtypeStruct((rows, width), kind) for kind in kinds],
        in_specs=[SMEM, SMEM, VMEM] + [VMEM] * len(pieces),
        out_specs=[VMEM] * reps,
        scratch_shapes=[pltpu.VMEM((length, width), jnp.bfloat16)],
        compiler_params=pltpu.CompilerParams(vmem_limit_bytes=32 * 1024 * 1024),
        cost_estimate=pl.CostEstimate(
            flops=2 * adj_tiles.size * width, bytes_accessed=4 * adj_tiles.size, transcendentals=0
        ),
        name="tile_products",
    )(where, columns, adj_tiles, *pieces)


def sum_parts(parts):
    n = lax.axis_size("rep")
    terms = [parts[0]]
    for d in range(1, n):
        pairs = [(i, (i + d) % n) for i in range(n)]
        terms.append(lax.ppermute(parts[d], "rep", pairs))
    return terms


def contract(a, b, dims):
    return lax.dot_general(a, b, ((dims[:1], dims[1:]), ((), ())), preferred_element_type=jnp.float32)


def node_kernel(n_terms, *refs):
    terms = refs[:n_terms]
    feats, cot, w_in, b_in, w_out, b_out, out, g_out = refs[n_terms:]
    agg = terms[0][...]
    for term in terms[1:]:
        agg = agg + term[...].astype(jnp.float32)
    agg_b = agg.astype(jnp.bfloat16)
    pre = contract(agg_b, w_in[...], (1, 0)) + b_in[...]
    sigma = 1.0 / (1.0 + jnp.exp(-pre))
    g_hidden = contract(cot[...], w_out[...], (1, 1))
    g_pre = (g_hidden * sigma * (1.0 + pre * (1.0 - sigma))).astype(jnp.bfloat16)
    g_out[...] = contract(g_pre, w_in[...], (1, 1)).astype(jnp.bfloat16)
    hidden = (pre * sigma).astype(jnp.bfloat16)
    projected = contract(hidden, w_out[...], (1, 0)) + b_out[...]
    out[...] = (feats[...].astype(jnp.float32) + projected).astype(jnp.bfloat16)


def node_update(terms, node_feats, cot_out, w_in, b_in, w_out, b_out):
    rows, width = node_feats.shape
    units = w_in.shape[1]
    like = jax.ShapeDtypeStruct((rows, width), jnp.bfloat16)
    return pl.pallas_call(
        functools.partial(node_kernel, len(terms)),
        out_shape=[like, like],
        in_specs=[VMEM] * (len(terms) + 6),
        out_specs=[VMEM] * 2,
        compiler_params=pltpu.CompilerParams(vmem_limit_bytes=32 * 1024 * 1024),
        cost_estimate=pl.CostEstimate(
            flops=8 * rows * width * units, bytes_accessed=12 * rows * width, transcendentals=rows * units
        ),
        name="node_update",
    )(*terms, node_feats, cot_out, w_in, b_in.reshape(1, -1), w_out, b_out.reshape(1, -1))


def close_kernel(n_terms, *refs):
    cot, out = refs[n_terms:]
    total = refs[0][...]
    for term in refs[1:n_terms]:
        total = total + term[...].astype(jnp.float32)
    out[...] = (cot[...].astype(jnp.float32) + total).astype(jnp.bfloat16)


def close_grad(terms, cot_out):
    return pl.pallas_call(
        functools.partial(close_kernel, len(terms)),
        out_shape=jax.ShapeDtypeStruct(cot_out.shape, jnp.bfloat16),
        in_specs=[VMEM] * (len(terms) + 1),
        out_specs=VMEM,
        compiler_params=pltpu.CompilerParams(vmem_limit_bytes=32 * 1024 * 1024),
        name="close_grad",
    )(*terms, cot_out)


def local(node_feats, adj_tiles, col_index, w_in, b_in, w_out, b_out, cot_out):
    where = jnp.stack([lax.axis_index("blk"), lax.axis_index("rep")]).astype(jnp.int32)
    columns = col_index[:, 0, :]
    panel = gather_blocks(node_feats)
    terms = sum_parts(tile_products(panel, adj_tiles, columns, where))
    out_feats, g_agg = node_update(terms, node_feats, cot_out, w_in, b_in, w_out, b_out)
    panel = gather_blocks(g_agg)
    terms = sum_parts(tile_products(panel, adj_tiles, columns, where))
    return (out_feats, close_grad(terms, cot_out))


def solution(mesh):
    placed = (
        P(("blk", "rep"), None),
        P("blk", "rep", None, None, None),
        P("blk", "rep", None),
        P(),
        P(),
        P(),
        P(),
        P(("blk", "rep"), None),
    )
    return jax.shard_map(
        local,
        mesh=mesh,
        in_specs=placed,
        out_specs=(P(("blk", "rep"), None), P(("blk", "rep"), None)),
        check_vma=False,
    )
```

```python
import functools

import jax
import jax.numpy as jnp
from jax import lax
from jax.experimental import pallas as pl
from jax.experimental.pallas import tpu as pltpu
from jax.sharding import PartitionSpec as P

BLOCK = 128
VMEM = pl.BlockSpec(memory_space=pltpu.VMEM)
SMEM = pl.BlockSpec(memory_space=pltpu.SMEM)


LINE = 8


def slots(n):
    pairs = n // 2
    steps = sorted(range(1, pairs), key=lambda k: (-min(k, pairs - k), -k))
    return [2 * k + s for k in [0] + steps for s in range(2)]


def gather_blocks(rows):
    n = lax.axis_size("blk")
    if n > LINE:
        return [lax.all_gather(rows, "blk", axis=0, tiled=True)]
    other = [(i, i ^ 1) for i in range(n)]
    got = []
    for slot in slots(n):
        if slot == 1:
            got.append(lax.ppermute(rows, "blk", other))
        elif slot % 2:
            got.append(lax.ppermute(got[-1], "blk", other))
        elif slot:
            got.append(lax.ppermute(rows, "blk", [((i + slot) % n, i) for i in range(n)]))
        else:
            got.append(rows)
    return got


def product_kernel(n_pieces, where, columns, tiles, *refs):
    pieces, outs, panel = refs[:n_pieces], refs[n_pieces:-1], refs[-1]
    blk, rep = where[0], where[1]
    reps = len(outs)
    rows = outs[0].shape[0]
    side = lax.rem(blk, 2)
    base = blk - side
    if n_pieces == 1:
        panel = pieces[0]
    else:
        for slot, piece in zip(slots(n_pieces), pieces):
            panel[pl.ds(slot * rows, rows), :] = piece[...]
    per_shard = rows // BLOCK
    for d, out in enumerate(outs):
        quarter = lax.bitwise_xor(rep, d)
        for i in range(per_shard):
            g = quarter * per_shard + i
            picked = []
            for k in range(tiles.shape[2]):
                c = columns[g, k]
                if n_pieces > 1:
                    shard = lax.rem(lax.bitwise_xor(c // per_shard, side) - base + n_pieces, n_pieces)
                    c = shard * per_shard + lax.rem(c, per_shard)
                start = pl.multiple_of(c * BLOCK, BLOCK)
                picked.append(panel[pl.ds(start, BLOCK), :])
            left = jnp.concatenate([tiles[g, 0, k] for k in range(tiles.shape[2])], axis=1)
            right = jnp.concatenate(picked, axis=0)
            summed = jnp.dot(left, right, preferred_element_type=jnp.float32)
            out[pl.ds(i * BLOCK, BLOCK), :] = summed.astype(out.dtype)


def tile_products(pieces, adj_tiles, columns, where):
    reps = lax.axis_size("rep")
    width = pieces[0].shape[1]
    rows = adj_tiles.shape[0] * BLOCK // reps
    length = sum(piece.shape[0] for piece in pieces)
    kinds = [jnp.float32] + [jnp.bfloat16] * (reps - 1)
    return pl.pallas_call(
        functools.partial(product_kernel, len(pieces)),
        out_shape=[jax.ShapeDtypeStruct((rows, width), kind) for kind in kinds],
        in_specs=[SMEM, SMEM, VMEM] + [VMEM] * len(pieces),
        out_specs=[VMEM] * reps,
        scratch_shapes=[pltpu.VMEM((length, width), jnp.bfloat16)],
        compiler_params=pltpu.CompilerParams(vmem_limit_bytes=32 * 1024 * 1024),
        cost_estimate=pl.CostEstimate(
            flops=2 * adj_tiles.size * width, bytes_accessed=4 * adj_tiles.size, transcendentals=0
        ),
        name="tile_products",
    )(where, columns, adj_tiles, *pieces)


def sum_parts(parts):
    n = lax.axis_size("rep")
    terms = [parts[0]]
    for d in range(1, n):
        pairs = [(i, i ^ d) for i in range(n)]
        terms.append(lax.ppermute(parts[d], "rep", pairs))
    return terms


def contract(a, b, dims):
    return lax.dot_general(a, b, ((dims[:1], dims[1:]), ((), ())), preferred_element_type=jnp.float32)


def early_kernel(cot, w_out, tiles, feats, g_hidden):
    g_hidden[...] = contract(cot[...], w_out[...], (1, 1))


def early(cot_out, w_out, adj_tiles, node_feats):
    rows, width = cot_out.shape
    units = w_out.shape[0]
    return pl.pallas_call(
        early_kernel,
        out_shape=jax.ShapeDtypeStruct((rows, units), jnp.float32),
        in_specs=[VMEM] * 4,
        out_specs=VMEM,
        compiler_params=pltpu.CompilerParams(vmem_limit_bytes=32 * 1024 * 1024),
        cost_estimate=pl.CostEstimate(
            flops=2 * rows * width * units, bytes_accessed=8 * rows * units, transcendentals=0
        ),
        name="early",
    )(cot_out, w_out, adj_tiles, node_feats)


def node_kernel(n_terms, *refs):
    terms = refs[:n_terms]
    g_hidden, w_in, b_in, g_out, hidden_out = refs[n_terms:]
    agg = terms[0][...]
    for term in terms[1:]:
        agg = agg + term[...].astype(jnp.float32)
    agg_b = agg.astype(jnp.bfloat16)
    pre = contract(agg_b, w_in[...], (1, 0)) + b_in[...]
    sigma = 1.0 / (1.0 + jnp.exp(-pre))
    g_pre = (g_hidden[...] * sigma * (1.0 + pre * (1.0 - sigma))).astype(jnp.bfloat16)
    g_out[...] = contract(g_pre, w_in[...], (1, 1)).astype(jnp.bfloat16)
    hidden_out[...] = (pre * sigma).astype(jnp.bfloat16)


def node_update(terms, g_hidden, w_in, b_in):
    rows, units = g_hidden.shape
    width = w_in.shape[0]
    return pl.pallas_call(
        functools.partial(node_kernel, len(terms)),
        out_shape=[
            jax.ShapeDtypeStruct((rows, width), jnp.bfloat16),
            jax.ShapeDtypeStruct((rows, units), jnp.bfloat16),
        ],
        in_specs=[VMEM] * (len(terms) + 3),
        out_specs=[VMEM] * 2,
        compiler_params=pltpu.CompilerParams(vmem_limit_bytes=32 * 1024 * 1024),
        cost_estimate=pl.CostEstimate(
            flops=4 * rows * width * units, bytes_accessed=8 * rows * units, transcendentals=rows * units
        ),
        name="node_update",
    )(*terms, g_hidden, w_in, b_in.reshape(1, -1))


def project_kernel(hidden, feats, w_out, b_out, out):
    projected = contract(hidden[...], w_out[...], (1, 0)) + b_out[...]
    out[...] = (feats[...].astype(jnp.float32) + projected).astype(jnp.bfloat16)


def project(hidden, node_feats, w_out, b_out):
    rows, units = hidden.shape
    width = w_out.shape[1]
    return pl.pallas_call(
        project_kernel,
        out_shape=jax.ShapeDtypeStruct((rows, width), jnp.bfloat16),
        in_specs=[VMEM] * 4,
        out_specs=VMEM,
        compiler_params=pltpu.CompilerParams(vmem_limit_bytes=32 * 1024 * 1024),
        cost_estimate=pl.CostEstimate(
            flops=2 * rows * width * units, bytes_accessed=2 * rows * units, transcendentals=0
        ),
        name="project",
    )(hidden, node_feats, w_out, b_out.reshape(1, -1))


def close_kernel(n_terms, *refs):
    cot, out = refs[n_terms:]
    total = refs[0][...]
    for term in refs[1:n_terms]:
        total = total + term[...].astype(jnp.float32)
    out[...] = (cot[...].astype(jnp.float32) + total).astype(jnp.bfloat16)


def close_grad(terms, cot_out):
    return pl.pallas_call(
        functools.partial(close_kernel, len(terms)),
        out_shape=jax.ShapeDtypeStruct(cot_out.shape, jnp.bfloat16),
        in_specs=[VMEM] * (len(terms) + 1),
        out_specs=VMEM,
        compiler_params=pltpu.CompilerParams(vmem_limit_bytes=32 * 1024 * 1024),
        name="close_grad",
    )(*terms, cot_out)


def local(node_feats, adj_tiles, col_index, w_in, b_in, w_out, b_out, cot_out):
    where = jnp.stack([lax.axis_index("blk"), lax.axis_index("rep")]).astype(jnp.int32)
    columns = col_index[:, 0, :]
    g_hidden = early(cot_out, w_out, adj_tiles, node_feats)
    where, g_hidden = lax.optimization_barrier((where, g_hidden))
    panel = gather_blocks(node_feats)
    terms = sum_parts(tile_products(panel, adj_tiles, columns, where))
    g_agg, hidden = node_update(terms, g_hidden, w_in, b_in)
    out_feats = project(hidden, node_feats, w_out, b_out)
    panel = gather_blocks(g_agg)
    terms = sum_parts(tile_products(panel, adj_tiles, columns, where))
    return (out_feats, close_grad(terms, cot_out))


def solution(mesh):
    placed = (
        P(("blk", "rep"), None),
        P("blk", "rep", None, None, None),
        P("blk", "rep", None),
        P(),
        P(),
        P(),
        P(),
        P(("blk", "rep"), None),
    )
    return jax.shard_map(
        local,
        mesh=mesh,
        in_specs=placed,
        out_specs=(P(("blk", "rep"), None), P(("blk", "rep"), None)),
        check_vma=False,
    )
```

```python
import functools

import jax
import jax.numpy as jnp
from jax import lax
from jax.experimental import pallas as pl
from jax.experimental.pallas import tpu as pltpu
from jax.sharding import PartitionSpec as P

BLOCK = 128
VMEM = pl.BlockSpec(memory_space=pltpu.VMEM)
SMEM = pl.BlockSpec(memory_space=pltpu.SMEM)


BESIDE = 2 * 10**10
LINE = 8


def slots(n):
    pairs = n // 2
    steps = sorted(range(1, pairs), key=lambda k: (-min(k, pairs - k), -k))
    return [2 * k + s for k in [0] + steps for s in range(2)]


def gather_blocks(rows):
    n = lax.axis_size("blk")
    if n > LINE:
        return [lax.all_gather(rows, "blk", axis=0, tiled=True)]
    other = [(i, i ^ 1) for i in range(n)]
    got = []
    for slot in slots(n):
        if slot == 1:
            got.append(lax.ppermute(rows, "blk", other))
        elif slot % 2:
            got.append(lax.ppermute(got[-1], "blk", other))
        elif slot:
            got.append(lax.ppermute(rows, "blk", [((i + slot) % n, i) for i in range(n)]))
        else:
            got.append(rows)
    return got


def partners(n):
    return [0] + [d for d in range(1, n) if d != 1] + [1] * (n > 1)


def product_kernel(n_pieces, where, columns, tiles, *refs):
    pieces, outs, panel = refs[:n_pieces], refs[n_pieces:-1], refs[-1]
    blk, rep = where[0], where[1]
    reps = len(outs)
    rows = outs[0].shape[0]
    side = lax.rem(blk, 2)
    base = blk - side
    if n_pieces == 1:
        panel = pieces[0]
    else:
        for slot, piece in zip(slots(n_pieces), pieces):
            panel[pl.ds(slot * rows, rows), :] = piece[...]
    per_shard = rows // BLOCK
    for d, out in zip(partners(reps), outs):
        quarter = lax.bitwise_xor(rep, d)
        for i in range(per_shard):
            g = quarter * per_shard + i
            picked = []
            for k in range(tiles.shape[2]):
                c = columns[g, k]
                if n_pieces > 1:
                    shard = lax.rem(lax.bitwise_xor(c // per_shard, side) - base + n_pieces, n_pieces)
                    c = shard * per_shard + lax.rem(c, per_shard)
                start = pl.multiple_of(c * BLOCK, BLOCK)
                picked.append(panel[pl.ds(start, BLOCK), :])
            left = jnp.concatenate([tiles[g, 0, k] for k in range(tiles.shape[2])], axis=1)
            right = jnp.concatenate(picked, axis=0)
            summed = jnp.dot(left, right, preferred_element_type=jnp.float32)
            out[pl.ds(i * BLOCK, BLOCK), :] = summed.astype(out.dtype)


def tile_products(pieces, adj_tiles, columns, where):
    reps = lax.axis_size("rep")
    width = pieces[0].shape[1]
    rows = adj_tiles.shape[0] * BLOCK // reps
    length = sum(piece.shape[0] for piece in pieces)
    kinds = [jnp.float32] + [jnp.bfloat16] * (reps - 1)
    return pl.pallas_call(
        functools.partial(product_kernel, len(pieces)),
        out_shape=[jax.ShapeDtypeStruct((rows, width), kind) for kind in kinds],
        in_specs=[SMEM, SMEM, VMEM] + [VMEM] * len(pieces),
        out_specs=[VMEM] * reps,
        scratch_shapes=[pltpu.VMEM((length, width), jnp.bfloat16)],
        compiler_params=pltpu.CompilerParams(vmem_limit_bytes=32 * 1024 * 1024),
        cost_estimate=pl.CostEstimate(
            flops=2 * adj_tiles.size * width, bytes_accessed=4 * adj_tiles.size, transcendentals=0
        ),
        name="tile_products",
    )(where, columns, adj_tiles, *pieces)


def sum_parts(parts):
    n = lax.axis_size("rep")
    terms = [parts[0]]
    for d, part in zip(partners(n)[1:], parts[1:]):
        terms.append(lax.ppermute(part, "rep", [(i, i ^ d) for i in range(n)]))
    return terms


def contract(a, b, dims):
    return lax.dot_general(a, b, ((dims[:1], dims[1:]), ((), ())), preferred_element_type=jnp.float32)


def early_kernel(cot, w_out, g_hidden):
    g_hidden[...] = contract(cot[...], w_out[...], (1, 1))


def early(cot_out, w_out):
    rows, width = cot_out.shape
    units = w_out.shape[0]
    return pl.pallas_call(
        early_kernel,
        out_shape=jax.ShapeDtypeStruct((rows, units), jnp.float32),
        in_specs=[VMEM] * 2,
        out_specs=VMEM,
        compiler_params=pltpu.CompilerParams(vmem_limit_bytes=32 * 1024 * 1024),
        cost_estimate=pl.CostEstimate(flops=BESIDE, bytes_accessed=8 * rows * units, transcendentals=0),
        name="early",
    )(cot_out, w_out)


def node_kernel(n_terms, *refs):
    terms = refs[:n_terms]
    g_hidden, w_in, b_in, g_out, hidden_out = refs[n_terms:]
    agg = terms[0][...]
    for term in terms[1:]:
        agg = agg + term[...].astype(jnp.float32)
    agg_b = agg.astype(jnp.bfloat16)
    pre = contract(agg_b, w_in[...], (1, 0)) + b_in[...]
    sigma = 1.0 / (1.0 + jnp.exp(-pre))
    g_pre = (g_hidden[...] * sigma * (1.0 + pre * (1.0 - sigma))).astype(jnp.bfloat16)
    g_out[...] = contract(g_pre, w_in[...], (1, 1)).astype(jnp.bfloat16)
    hidden_out[...] = (pre * sigma).astype(jnp.bfloat16)


def node_update(terms, g_hidden, w_in, b_in):
    rows, units = g_hidden.shape
    width = w_in.shape[0]
    return pl.pallas_call(
        functools.partial(node_kernel, len(terms)),
        out_shape=[
            jax.ShapeDtypeStruct((rows, width), jnp.bfloat16),
            jax.ShapeDtypeStruct((rows, units), jnp.bfloat16),
        ],
        in_specs=[VMEM] * (len(terms) + 3),
        out_specs=[VMEM] * 2,
        compiler_params=pltpu.CompilerParams(vmem_limit_bytes=32 * 1024 * 1024),
        cost_estimate=pl.CostEstimate(
            flops=4 * rows * width * units, bytes_accessed=8 * rows * units, transcendentals=rows * units
        ),
        name="node_update",
    )(*terms, g_hidden, w_in, b_in.reshape(1, -1))


def project_kernel(hidden, feats, w_out, b_out, out):
    projected = contract(hidden[...], w_out[...], (1, 0)) + b_out[...]
    out[...] = (feats[...].astype(jnp.float32) + projected).astype(jnp.bfloat16)


def project(hidden, node_feats, w_out, b_out):
    rows, units = hidden.shape
    width = w_out.shape[1]
    return pl.pallas_call(
        project_kernel,
        out_shape=jax.ShapeDtypeStruct((rows, width), jnp.bfloat16),
        in_specs=[VMEM] * 4,
        out_specs=VMEM,
        compiler_params=pltpu.CompilerParams(vmem_limit_bytes=32 * 1024 * 1024),
        cost_estimate=pl.CostEstimate(
            flops=2 * rows * width * units, bytes_accessed=2 * rows * units, transcendentals=0
        ),
        name="project",
    )(hidden, node_feats, w_out, b_out.reshape(1, -1))


def close_kernel(n_terms, *refs):
    cot, out = refs[n_terms:]
    total = refs[0][...]
    for term in refs[1:n_terms]:
        total = total + term[...].astype(jnp.float32)
    out[...] = (cot[...].astype(jnp.float32) + total).astype(jnp.bfloat16)


def close_grad(terms, cot_out):
    return pl.pallas_call(
        functools.partial(close_kernel, len(terms)),
        out_shape=jax.ShapeDtypeStruct(cot_out.shape, jnp.bfloat16),
        in_specs=[VMEM] * (len(terms) + 1),
        out_specs=VMEM,
        compiler_params=pltpu.CompilerParams(vmem_limit_bytes=32 * 1024 * 1024),
        name="close_grad",
    )(*terms, cot_out)


def local(node_feats, adj_tiles, col_index, w_in, b_in, w_out, b_out, cot_out):
    where = jnp.stack([lax.axis_index("blk"), lax.axis_index("rep")]).astype(jnp.int32)
    columns = col_index[:, 0, :]
    g_hidden = early(cot_out, w_out)
    where, g_hidden = lax.optimization_barrier((where, g_hidden))
    panel = gather_blocks(node_feats)
    terms = sum_parts(tile_products(panel, adj_tiles, columns, where))
    g_agg, hidden = node_update(terms, g_hidden, w_in, b_in)
    out_feats = project(hidden, node_feats, w_out, b_out)
    panel = gather_blocks(g_agg)
    terms = sum_parts(tile_products(panel, adj_tiles, columns, where))
    return (out_feats, close_grad(terms, cot_out))


def solution(mesh):
    placed = (
        P(("blk", "rep"), None),
        P("blk", "rep", None, None, None),
        P("blk", "rep", None),
        P(),
        P(),
        P(),
        P(),
        P(("blk", "rep"), None),
    )
    return jax.shard_map(
        local,
        mesh=mesh,
        in_specs=placed,
        out_specs=(P(("blk", "rep"), None), P(("blk", "rep"), None)),
        check_vma=False,
    )
```

```python
import functools

import jax
import jax.numpy as jnp
from jax import lax
from jax.experimental import pallas as pl
from jax.experimental.pallas import tpu as pltpu
from jax.sharding import PartitionSpec as P

BLOCK = 128
VMEM = pl.BlockSpec(memory_space=pltpu.VMEM)
SMEM = pl.BlockSpec(memory_space=pltpu.SMEM)


BESIDE = 2 * 10**10
LINE = 8


def slots(n):
    pairs = n // 2
    steps = sorted(range(1, pairs), key=lambda k: (-min(k, pairs - k), -k))
    return [2 * k + s for k in [0] + steps for s in range(2)]


def gather_blocks(rows):
    n = lax.axis_size("blk")
    if n > LINE:
        return [lax.all_gather(rows, "blk", axis=0, tiled=True)]
    other = [(i, i ^ 1) for i in range(n)]
    got = []
    for slot in slots(n):
        if slot == 1:
            got.append(lax.ppermute(rows, "blk", other))
        elif slot % 2:
            got.append(lax.ppermute(got[-1], "blk", other))
        elif slot:
            got.append(lax.ppermute(rows, "blk", [((i + slot) % n, i) for i in range(n)]))
        else:
            got.append(rows)
    return got


def add_blocks(columns, tiles, panel, out, owners):
    per_owner = out.shape[0] // (BLOCK * len(owners))
    for j, owner in enumerate(owners):
        for i in range(per_owner):
            g = owner * per_owner + i
            slots_here = range(tiles.shape[2])
            starts = [pl.multiple_of(columns[g, k] * BLOCK, BLOCK) for k in slots_here]
            left = jnp.concatenate([tiles[g, 0, k] for k in slots_here], axis=1)
            right = jnp.concatenate([panel[pl.ds(start, BLOCK), :] for start in starts], axis=0)
            summed = jnp.dot(left, right, preferred_element_type=jnp.float32)
            out[pl.ds((j * per_owner + i) * BLOCK, BLOCK), :] = summed.astype(out.dtype)


def other_core_kernel(n_pieces, reps, where, columns, tiles, *refs):
    pieces, panel, out = refs[:n_pieces], refs[-2], refs[-1]
    blk, rep = where[0], where[1]
    rows = pieces[0].shape[0]
    side = lax.rem(blk, 2)
    if n_pieces == 1:
        panel[...] = pieces[0][...]
    else:
        for slot, piece in zip(slots(n_pieces), pieces):
            shard = lax.rem(blk - side + slot // 2 * 2, n_pieces) + lax.bitwise_xor(side, slot % 2)
            panel[pl.ds(pl.multiple_of(shard * rows, rows), rows), :] = piece[...]
    add_blocks(columns, tiles, panel, out, [lax.bitwise_xor(rep, d) for d in range(1, reps, 2)])


def own_core_kernel(reps, where, columns, tiles, panel, out):
    rep = where[1]
    add_blocks(columns, tiles, panel, out, [lax.bitwise_xor(rep, d) for d in range(0, reps, 2)])


def product_cost(adj_tiles, width):
    return pl.CostEstimate(
        flops=adj_tiles.size * width, bytes_accessed=2 * adj_tiles.size, transcendentals=0
    )


def other_core(pieces, adj_tiles, columns, where):
    reps = lax.axis_size("rep")
    width = pieces[0].shape[1]
    length = sum(piece.shape[0] for piece in pieces)
    rows = adj_tiles.shape[0] * BLOCK // 2
    return pl.pallas_call(
        functools.partial(other_core_kernel, len(pieces), reps),
        out_shape=[
            jax.ShapeDtypeStruct((length, width), jnp.bfloat16),
            jax.ShapeDtypeStruct((rows, width), jnp.bfloat16),
        ],
        in_specs=[SMEM, SMEM, VMEM] + [VMEM] * len(pieces),
        out_specs=[VMEM] * 2,
        compiler_params=pltpu.CompilerParams(vmem_limit_bytes=32 * 1024 * 1024),
        cost_estimate=product_cost(adj_tiles, width),
        name="other_core",
    )(where, columns, adj_tiles, *pieces)


def own_core(panel, adj_tiles, columns, where):
    rows, width = adj_tiles.shape[0] * BLOCK // 2, panel.shape[1]
    return pl.pallas_call(
        functools.partial(own_core_kernel, lax.axis_size("rep")),
        out_shape=jax.ShapeDtypeStruct((rows, width), jnp.float32),
        in_specs=[SMEM, SMEM, VMEM, VMEM],
        out_specs=VMEM,
        compiler_params=pltpu.CompilerParams(vmem_limit_bytes=32 * 1024 * 1024),
        cost_estimate=product_cost(adj_tiles, width),
        name="own_core",
    )(where, columns, adj_tiles, panel)


def add_cores_kernel(own, core, *outs):
    rows = outs[0].shape[0]
    for j, out in enumerate(outs, 1):
        part = pl.ds(j * rows, rows)
        out[...] = (own[part, :] + core[part, :].astype(jnp.float32)).astype(jnp.bfloat16)


def add_cores(own, core, rows):
    width = own.shape[1]
    return pl.pallas_call(
        add_cores_kernel,
        out_shape=[jax.ShapeDtypeStruct((rows, width), jnp.bfloat16)] * (own.shape[0] // rows - 1),
        in_specs=[VMEM] * 2,
        out_specs=[VMEM] * (own.shape[0] // rows - 1),
        compiler_params=pltpu.CompilerParams(vmem_limit_bytes=32 * 1024 * 1024),
        name="add_cores",
    )(own, core)


def tile_products(pieces, adj_tiles, columns, where, rows):
    reps = lax.axis_size("rep")
    panel, across = other_core(pieces, adj_tiles, columns, where)
    core = lax.ppermute(across, "rep", [(i, i ^ 1) for i in range(reps)])
    own = own_core(panel, adj_tiles, columns, where)
    terms = [own, core]
    for j, part in enumerate(add_cores(own, core, rows), 1):
        terms.append(lax.ppermute(part, "rep", [(i, i ^ (2 * j)) for i in range(reps)]))
    return terms


def add_terms(terms, rows):
    total = terms[0][pl.ds(0, rows), :]
    for term in terms[1:]:
        total = total + term[pl.ds(0, rows), :].astype(jnp.float32)
    return total


def contract(a, b, dims):
    return lax.dot_general(a, b, ((dims[:1], dims[1:]), ((), ())), preferred_element_type=jnp.float32)


def early_kernel(cot, w_out, g_hidden):
    g_hidden[...] = contract(cot[...], w_out[...], (1, 1))


def early(cot_out, w_out):
    rows, width = cot_out.shape
    units = w_out.shape[0]
    return pl.pallas_call(
        early_kernel,
        out_shape=jax.ShapeDtypeStruct((rows, units), jnp.float32),
        in_specs=[VMEM] * 2,
        out_specs=VMEM,
        compiler_params=pltpu.CompilerParams(vmem_limit_bytes=32 * 1024 * 1024),
        cost_estimate=pl.CostEstimate(flops=BESIDE, bytes_accessed=8 * rows * units, transcendentals=0),
        name="early",
    )(cot_out, w_out)


def node_kernel(n_terms, *refs):
    terms = refs[:n_terms]
    g_hidden, w_in, b_in, g_out, hidden_out = refs[n_terms:]
    agg_b = add_terms(terms, g_out.shape[0]).astype(jnp.bfloat16)
    pre = contract(agg_b, w_in[...], (1, 0)) + b_in[...]
    sigma = 1.0 / (1.0 + jnp.exp(-pre))
    g_pre = (g_hidden[...] * sigma * (1.0 + pre * (1.0 - sigma))).astype(jnp.bfloat16)
    g_out[...] = contract(g_pre, w_in[...], (1, 1)).astype(jnp.bfloat16)
    hidden_out[...] = (pre * sigma).astype(jnp.bfloat16)


def node_update(terms, g_hidden, w_in, b_in):
    rows, units = g_hidden.shape
    width = w_in.shape[0]
    return pl.pallas_call(
        functools.partial(node_kernel, len(terms)),
        out_shape=[
            jax.ShapeDtypeStruct((rows, width), jnp.bfloat16),
            jax.ShapeDtypeStruct((rows, units), jnp.bfloat16),
        ],
        in_specs=[VMEM] * (len(terms) + 3),
        out_specs=[VMEM] * 2,
        compiler_params=pltpu.CompilerParams(vmem_limit_bytes=32 * 1024 * 1024),
        cost_estimate=pl.CostEstimate(
            flops=4 * rows * width * units, bytes_accessed=8 * rows * units, transcendentals=rows * units
        ),
        name="node_update",
    )(*terms, g_hidden, w_in, b_in.reshape(1, -1))


def project_kernel(hidden, feats, w_out, b_out, out):
    projected = contract(hidden[...], w_out[...], (1, 0)) + b_out[...]
    out[...] = (feats[...].astype(jnp.float32) + projected).astype(jnp.bfloat16)


def project(hidden, node_feats, w_out, b_out):
    rows, units = hidden.shape
    width = w_out.shape[1]
    return pl.pallas_call(
        project_kernel,
        out_shape=jax.ShapeDtypeStruct((rows, width), jnp.bfloat16),
        in_specs=[VMEM] * 4,
        out_specs=VMEM,
        compiler_params=pltpu.CompilerParams(vmem_limit_bytes=32 * 1024 * 1024),
        cost_estimate=pl.CostEstimate(
            flops=2 * rows * width * units, bytes_accessed=2 * rows * units, transcendentals=0
        ),
        name="project",
    )(hidden, node_feats, w_out, b_out.reshape(1, -1))


def close_kernel(n_terms, *refs):
    cot, out = refs[n_terms:]
    total = add_terms(refs[:n_terms], out.shape[0])
    out[...] = (cot[...].astype(jnp.float32) + total).astype(jnp.bfloat16)


def close_grad(terms, cot_out):
    return pl.pallas_call(
        functools.partial(close_kernel, len(terms)),
        out_shape=jax.ShapeDtypeStruct(cot_out.shape, jnp.bfloat16),
        in_specs=[VMEM] * (len(terms) + 1),
        out_specs=VMEM,
        compiler_params=pltpu.CompilerParams(vmem_limit_bytes=32 * 1024 * 1024),
        name="close_grad",
    )(*terms, cot_out)


def local(node_feats, adj_tiles, col_index, w_in, b_in, w_out, b_out, cot_out):
    where = jnp.stack([lax.axis_index("blk"), lax.axis_index("rep")]).astype(jnp.int32)
    columns = col_index[:, 0, :]
    g_hidden = early(cot_out, w_out)
    where, g_hidden = lax.optimization_barrier((where, g_hidden))
    panel = gather_blocks(node_feats)
    terms = tile_products(panel, adj_tiles, columns, where, node_feats.shape[0])
    g_agg, hidden = node_update(terms, g_hidden, w_in, b_in)
    out_feats = project(hidden, node_feats, w_out, b_out)
    panel = gather_blocks(g_agg)
    terms = tile_products(panel, adj_tiles, columns, where, node_feats.shape[0])
    return (out_feats, close_grad(terms, cot_out))


def solution(mesh):
    placed = (
        P(("blk", "rep"), None),
        P("blk", "rep", None, None, None),
        P("blk", "rep", None),
        P(),
        P(),
        P(),
        P(),
        P(("blk", "rep"), None),
    )
    return jax.shard_map(
        local,
        mesh=mesh,
        in_specs=placed,
        out_specs=(P(("blk", "rep"), None), P(("blk", "rep"), None)),
        check_vma=False,
    )
```

```python
import functools

import jax
import jax.numpy as jnp
from jax import lax
from jax.experimental import pallas as pl
from jax.experimental.pallas import tpu as pltpu
from jax.sharding import PartitionSpec as P

BLOCK = 128
VMEM = pl.BlockSpec(memory_space=pltpu.VMEM)
SMEM = pl.BlockSpec(memory_space=pltpu.SMEM)


BESIDE = 2 * 10**10
LINE = 8


def slots(n):
    pairs = n // 2
    steps = sorted(range(1, pairs), key=lambda k: (-min(k, pairs - k), -k))
    return [2 * k + s for k in [0] + steps for s in range(2)]


def gather_blocks(rows):
    n = lax.axis_size("blk")
    if n > LINE:
        return [lax.all_gather(rows, "blk", axis=0, tiled=True)]
    other = [(i, i ^ 1) for i in range(n)]
    got = []
    for slot in slots(n):
        if slot == 1:
            got.append(lax.ppermute(rows, "blk", other))
        elif slot % 2:
            got.append(lax.ppermute(got[-1], "blk", other))
        elif slot:
            got.append(lax.ppermute(rows, "blk", [((i + slot) % n, i) for i in range(n)]))
        else:
            got.append(rows)
    return got


def add_blocks(columns, tiles, panel, out, owners):
    per_owner = out.shape[0] // (BLOCK * len(owners))
    for j, owner in enumerate(owners):
        for i in range(per_owner):
            g = owner * per_owner + i
            slots_here = range(tiles.shape[2])
            starts = [pl.multiple_of(columns[g, k] * BLOCK, BLOCK) for k in slots_here]
            left = jnp.concatenate([tiles[g, 0, k] for k in slots_here], axis=1)
            right = jnp.concatenate([panel[pl.ds(start, BLOCK), :] for start in starts], axis=0)
            summed = jnp.dot(left, right, preferred_element_type=jnp.float32)
            out[pl.ds((j * per_owner + i) * BLOCK, BLOCK), :] = summed.astype(out.dtype)


def other_kernel(n_pieces, reps, where, columns, tiles, *refs):
    pieces, panel, out = refs[:n_pieces], refs[-2], refs[-1]
    blk, rep = where[0], where[1]
    rows = pieces[0].shape[0]
    side = lax.rem(blk, 2)
    if n_pieces == 1:
        panel[...] = pieces[0][...]
    else:
        for slot, piece in zip(slots(n_pieces), pieces):
            shard = lax.rem(blk - side + slot // 2 * 2, n_pieces) + lax.bitwise_xor(side, slot % 2)
            panel[pl.ds(pl.multiple_of(shard * rows, rows), rows), :] = piece[...]
    add_blocks(columns, tiles, panel, out, [lax.bitwise_xor(rep, d) for d in range(1, reps, 2)])


def other_sums(pieces, adj_tiles, columns, where):
    reps = lax.axis_size("rep")
    width = pieces[0].shape[1]
    length = sum(piece.shape[0] for piece in pieces)
    rows = adj_tiles.shape[0] * BLOCK // reps
    return pl.pallas_call(
        functools.partial(other_kernel, len(pieces), reps),
        out_shape=[
            jax.ShapeDtypeStruct((length, width), jnp.bfloat16),
            jax.ShapeDtypeStruct((rows * (reps // 2), width), jnp.bfloat16),
        ],
        in_specs=[SMEM, SMEM, VMEM] + [VMEM] * len(pieces),
        out_specs=[VMEM] * 2,
        compiler_params=pltpu.CompilerParams(vmem_limit_bytes=32 * 1024 * 1024),
        cost_estimate=product_cost(adj_tiles, width, reps),
        name="other_sums",
    )(where, columns, adj_tiles, *pieces)


def sums_kernel(owners, where, columns, tiles, panel, out):
    add_blocks(columns, tiles, panel, out, [lax.bitwise_xor(where[1], d) for d in owners])


def sums(panel, adj_tiles, columns, where, owners, kind, name):
    reps = lax.axis_size("rep")
    rows, width = adj_tiles.shape[0] * BLOCK // reps * len(owners), panel.shape[1]
    return pl.pallas_call(
        functools.partial(sums_kernel, owners),
        out_shape=jax.ShapeDtypeStruct((rows, width), kind),
        in_specs=[SMEM, SMEM, VMEM, VMEM],
        out_specs=VMEM,
        compiler_params=pltpu.CompilerParams(vmem_limit_bytes=32 * 1024 * 1024),
        cost_estimate=product_cost(adj_tiles, width, reps),
        name=name,
    )(where, columns, adj_tiles, panel)


def product_cost(adj_tiles, width, reps):
    size = adj_tiles.size // reps
    return pl.CostEstimate(flops=2 * size * width, bytes_accessed=2 * size, transcendentals=0)


def add_cores_kernel(own, core, *outs):
    rows = outs[0].shape[0]
    for j, out in enumerate(outs):
        here, there = pl.ds(j * rows, rows), pl.ds((j + 1) * rows, rows)
        out[...] = (own[here, :] + core[there, :].astype(jnp.float32)).astype(jnp.bfloat16)


def add_cores(own, core, rows):
    width = own.shape[1]
    return pl.pallas_call(
        add_cores_kernel,
        out_shape=[jax.ShapeDtypeStruct((rows, width), jnp.bfloat16)] * (own.shape[0] // rows),
        in_specs=[VMEM] * 2,
        out_specs=[VMEM] * (own.shape[0] // rows),
        compiler_params=pltpu.CompilerParams(vmem_limit_bytes=32 * 1024 * 1024),
        name="add_cores",
    )(own, core)


def tile_products(pieces, adj_tiles, columns, where, rows):
    reps = lax.axis_size("rep")
    panel, across = other_sums(pieces, adj_tiles, columns, where)
    core = lax.ppermute(across, "rep", [(i, i ^ 1) for i in range(reps)])
    own = sums(panel, adj_tiles, columns, where, range(2, reps, 2), jnp.float32, "own_far")
    parts = add_cores(own, core, rows)
    panel, parts = lax.optimization_barrier((panel, parts))
    near = sums(panel, adj_tiles, columns, where, [0], jnp.float32, "own_near")
    terms = [near, core]
    for j, part in enumerate(parts, 1):
        terms.append(lax.ppermute(part, "rep", [(i, i ^ (2 * j)) for i in range(reps)]))
    return terms


def add_terms(terms, rows):
    total = terms[0][pl.ds(0, rows), :]
    for term in terms[1:]:
        total = total + term[pl.ds(0, rows), :].astype(jnp.float32)
    return total


def contract(a, b, dims):
    return lax.dot_general(a, b, ((dims[:1], dims[1:]), ((), ())), preferred_element_type=jnp.float32)


def early_kernel(cot, w_out, g_hidden):
    g_hidden[...] = contract(cot[...], w_out[...], (1, 1))


def early(cot_out, w_out):
    rows, width = cot_out.shape
    units = w_out.shape[0]
    return pl.pallas_call(
        early_kernel,
        out_shape=jax.ShapeDtypeStruct((rows, units), jnp.float32),
        in_specs=[VMEM] * 2,
        out_specs=VMEM,
        compiler_params=pltpu.CompilerParams(vmem_limit_bytes=32 * 1024 * 1024),
        cost_estimate=pl.CostEstimate(flops=BESIDE, bytes_accessed=8 * rows * units, transcendentals=0),
        name="early",
    )(cot_out, w_out)


def node_kernel(n_terms, *refs):
    terms = refs[:n_terms]
    g_hidden, w_in, b_in, g_out, hidden_out = refs[n_terms:]
    agg_b = add_terms(terms, g_out.shape[0]).astype(jnp.bfloat16)
    pre = contract(agg_b, w_in[...], (1, 0)) + b_in[...]
    sigma = 1.0 / (1.0 + jnp.exp(-pre))
    g_pre = (g_hidden[...] * sigma * (1.0 + pre * (1.0 - sigma))).astype(jnp.bfloat16)
    g_out[...] = contract(g_pre, w_in[...], (1, 1)).astype(jnp.bfloat16)
    hidden_out[...] = (pre * sigma).astype(jnp.bfloat16)


def node_update(terms, g_hidden, w_in, b_in):
    rows, units = g_hidden.shape
    width = w_in.shape[0]
    return pl.pallas_call(
        functools.partial(node_kernel, len(terms)),
        out_shape=[
            jax.ShapeDtypeStruct((rows, width), jnp.bfloat16),
            jax.ShapeDtypeStruct((rows, units), jnp.bfloat16),
        ],
        in_specs=[VMEM] * (len(terms) + 3),
        out_specs=[VMEM] * 2,
        compiler_params=pltpu.CompilerParams(vmem_limit_bytes=32 * 1024 * 1024),
        cost_estimate=pl.CostEstimate(
            flops=4 * rows * width * units, bytes_accessed=8 * rows * units, transcendentals=rows * units
        ),
        name="node_update",
    )(*terms, g_hidden, w_in, b_in.reshape(1, -1))


def project_kernel(hidden, feats, w_out, b_out, out):
    projected = contract(hidden[...], w_out[...], (1, 0)) + b_out[...]
    out[...] = (feats[...].astype(jnp.float32) + projected).astype(jnp.bfloat16)


def project(hidden, node_feats, w_out, b_out):
    rows, units = hidden.shape
    width = w_out.shape[1]
    return pl.pallas_call(
        project_kernel,
        out_shape=jax.ShapeDtypeStruct((rows, width), jnp.bfloat16),
        in_specs=[VMEM] * 4,
        out_specs=VMEM,
        compiler_params=pltpu.CompilerParams(vmem_limit_bytes=32 * 1024 * 1024),
        cost_estimate=pl.CostEstimate(
            flops=2 * rows * width * units, bytes_accessed=2 * rows * units, transcendentals=0
        ),
        name="project",
    )(hidden, node_feats, w_out, b_out.reshape(1, -1))


def close_kernel(n_terms, *refs):
    cot, out = refs[n_terms:]
    total = add_terms(refs[:n_terms], out.shape[0])
    out[...] = (cot[...].astype(jnp.float32) + total).astype(jnp.bfloat16)


def close_grad(terms, cot_out):
    return pl.pallas_call(
        functools.partial(close_kernel, len(terms)),
        out_shape=jax.ShapeDtypeStruct(cot_out.shape, jnp.bfloat16),
        in_specs=[VMEM] * (len(terms) + 1),
        out_specs=VMEM,
        compiler_params=pltpu.CompilerParams(vmem_limit_bytes=32 * 1024 * 1024),
        name="close_grad",
    )(*terms, cot_out)


def local(node_feats, adj_tiles, col_index, w_in, b_in, w_out, b_out, cot_out):
    where = jnp.stack([lax.axis_index("blk"), lax.axis_index("rep")]).astype(jnp.int32)
    columns = col_index[:, 0, :]
    g_hidden = early(cot_out, w_out)
    where, g_hidden = lax.optimization_barrier((where, g_hidden))
    panel = gather_blocks(node_feats)
    terms = tile_products(panel, adj_tiles, columns, where, node_feats.shape[0])
    g_agg, hidden = node_update(terms, g_hidden, w_in, b_in)
    out_feats = project(hidden, node_feats, w_out, b_out)
    panel = gather_blocks(g_agg)
    terms = tile_products(panel, adj_tiles, columns, where, node_feats.shape[0])
    return (out_feats, close_grad(terms, cot_out))


def solution(mesh):
    placed = (
        P(("blk", "rep"), None),
        P("blk", "rep", None, None, None),
        P("blk", "rep", None),
        P(),
        P(),
        P(),
        P(),
        P(("blk", "rep"), None),
    )
    return jax.shard_map(
        local,
        mesh=mesh,
        in_specs=placed,
        out_specs=(P(("blk", "rep"), None), P(("blk", "rep"), None)),
        check_vma=False,
    )
```

```python
import functools

import jax
import jax.numpy as jnp
from jax import lax
from jax.experimental import pallas as pl
from jax.experimental.pallas import tpu as pltpu
from jax.sharding import PartitionSpec as P

BLOCK = 128
VMEM = pl.BlockSpec(memory_space=pltpu.VMEM)
SMEM = pl.BlockSpec(memory_space=pltpu.SMEM)


BESIDE = 2 * 10**10
LINE = 8


def slots(n):
    pairs = n // 2
    steps = sorted(range(1, pairs), key=lambda k: (-min(k, pairs - k), -k))
    return [2 * k + s for k in [0] + steps for s in range(2)]


def gather_blocks(rows):
    n = lax.axis_size("blk")
    if n > LINE:
        return [lax.all_gather(rows, "blk", axis=0, tiled=True)]
    other = [(i, i ^ 1) for i in range(n)]
    got = []
    for slot in slots(n):
        if slot == 1:
            got.append(lax.ppermute(rows, "blk", other))
        elif slot % 2:
            got.append(lax.ppermute(got[-1], "blk", other))
        elif slot:
            got.append(lax.ppermute(rows, "blk", [((i + slot) % n, i) for i in range(n)]))
        else:
            got.append(rows)
    return got


def position(table, tiles):
    count = tiles.shape[0] * tiles.shape[2]
    return table[count], table[count + 1]


def add_blocks(table, tiles, panel, out, owners):
    per_owner = out.shape[0] // (BLOCK * len(owners))
    for j, owner in enumerate(owners):
        for i in range(per_owner):
            g = owner * per_owner + i
            slots_here = range(tiles.shape[2])
            starts = [pl.multiple_of(table[g * tiles.shape[2] + k] * BLOCK, BLOCK) for k in slots_here]
            left = jnp.concatenate([tiles[g, 0, k] for k in slots_here], axis=1)
            right = jnp.concatenate([panel[pl.ds(start, BLOCK), :] for start in starts], axis=0)
            summed = jnp.dot(left, right, preferred_element_type=jnp.float32)
            out[pl.ds((j * per_owner + i) * BLOCK, BLOCK), :] = summed.astype(out.dtype)


def other_kernel(n_pieces, reps, table, tiles, *refs):
    pieces, panel, out = refs[:n_pieces], refs[-2], refs[-1]
    blk, rep = position(table, tiles)
    rows = pieces[0].shape[0]
    side = lax.rem(blk, 2)
    if n_pieces == 1:
        panel[...] = pieces[0][...]
    else:
        for slot, piece in zip(slots(n_pieces), pieces):
            shard = lax.rem(blk - side + slot // 2 * 2, n_pieces) + lax.bitwise_xor(side, slot % 2)
            panel[pl.ds(pl.multiple_of(shard * rows, rows), rows), :] = piece[...]
    add_blocks(table, tiles, panel, out, [lax.bitwise_xor(rep, d) for d in range(1, reps, 2)])


def other_sums(pieces, adj_tiles, table):
    reps = lax.axis_size("rep")
    width = pieces[0].shape[1]
    length = sum(piece.shape[0] for piece in pieces)
    rows = adj_tiles.shape[0] * BLOCK // reps
    return pl.pallas_call(
        functools.partial(other_kernel, len(pieces), reps),
        out_shape=[
            jax.ShapeDtypeStruct((length, width), jnp.bfloat16),
            jax.ShapeDtypeStruct((rows * (reps // 2), width), jnp.bfloat16),
        ],
        in_specs=[SMEM, VMEM] + [VMEM] * len(pieces),
        out_specs=[VMEM] * 2,
        compiler_params=pltpu.CompilerParams(vmem_limit_bytes=32 * 1024 * 1024),
        cost_estimate=product_cost(adj_tiles, width, reps),
        name="other_sums",
    )(table, adj_tiles, *pieces)


def sums_kernel(owners, table, tiles, panel, out):
    blk, rep = position(table, tiles)
    add_blocks(table, tiles, panel, out, [lax.bitwise_xor(rep, d) for d in owners])


def sums(panel, adj_tiles, table, owners, kind, name):
    reps = lax.axis_size("rep")
    rows, width = adj_tiles.shape[0] * BLOCK // reps * len(owners), panel.shape[1]
    return pl.pallas_call(
        functools.partial(sums_kernel, owners),
        out_shape=jax.ShapeDtypeStruct((rows, width), kind),
        in_specs=[SMEM, VMEM, VMEM],
        out_specs=VMEM,
        compiler_params=pltpu.CompilerParams(vmem_limit_bytes=32 * 1024 * 1024),
        cost_estimate=product_cost(adj_tiles, width, reps),
        name=name,
    )(table, adj_tiles, panel)


def product_cost(adj_tiles, width, reps):
    size = adj_tiles.size // reps
    return pl.CostEstimate(flops=2 * size * width, bytes_accessed=2 * size, transcendentals=0)


def add_cores_kernel(own, core, *outs):
    rows = outs[0].shape[0]
    for j, out in enumerate(outs):
        here, there = pl.ds(j * rows, rows), pl.ds((j + 1) * rows, rows)
        out[...] = (own[here, :] + core[there, :].astype(jnp.float32)).astype(jnp.bfloat16)


def add_cores(own, core, rows):
    width = own.shape[1]
    return pl.pallas_call(
        add_cores_kernel,
        out_shape=[jax.ShapeDtypeStruct((rows, width), jnp.bfloat16)] * (own.shape[0] // rows),
        in_specs=[VMEM] * 2,
        out_specs=[VMEM] * (own.shape[0] // rows),
        compiler_params=pltpu.CompilerParams(vmem_limit_bytes=32 * 1024 * 1024),
        name="add_cores",
    )(own, core)


def tile_products(pieces, adj_tiles, table, rows):
    reps = lax.axis_size("rep")
    panel, across = other_sums(pieces, adj_tiles, table)
    core = lax.ppermute(across, "rep", [(i, i ^ 1) for i in range(reps)])
    own = sums(panel, adj_tiles, table, range(2, reps, 2), jnp.float32, "own_far")
    parts = add_cores(own, core, rows)
    panel, parts = lax.optimization_barrier((panel, parts))
    near = sums(panel, adj_tiles, table, [0], jnp.float32, "own_near")
    terms = [near, core]
    for j, part in enumerate(parts, 1):
        terms.append(lax.ppermute(part, "rep", [(i, i ^ (2 * j)) for i in range(reps)]))
    return terms


def add_terms(terms, rows):
    total = terms[0][pl.ds(0, rows), :]
    for term in terms[1:]:
        total = total + term[pl.ds(0, rows), :].astype(jnp.float32)
    return total


def contract(a, b, dims):
    return lax.dot_general(a, b, ((dims[:1], dims[1:]), ((), ())), preferred_element_type=jnp.float32)


def early_kernel(cot, w_out, g_hidden):
    g_hidden[...] = contract(cot[...], w_out[...], (1, 1))


def early(cot_out, w_out):
    rows, width = cot_out.shape
    units = w_out.shape[0]
    return pl.pallas_call(
        early_kernel,
        out_shape=jax.ShapeDtypeStruct((rows, units), jnp.float32),
        in_specs=[VMEM] * 2,
        out_specs=VMEM,
        compiler_params=pltpu.CompilerParams(vmem_limit_bytes=32 * 1024 * 1024),
        cost_estimate=pl.CostEstimate(flops=BESIDE, bytes_accessed=8 * rows * units, transcendentals=0),
        name="early",
    )(cot_out, w_out)


def node_kernel(n_terms, *refs):
    terms = refs[:n_terms]
    g_hidden, w_in, b_in, g_out, hidden_out = refs[n_terms:]
    agg_b = add_terms(terms, g_out.shape[0]).astype(jnp.bfloat16)
    pre = contract(agg_b, w_in[...], (1, 0)) + b_in[...]
    sigma = 1.0 / (1.0 + jnp.exp(-pre))
    g_pre = (g_hidden[...] * sigma * (1.0 + pre * (1.0 - sigma))).astype(jnp.bfloat16)
    g_out[...] = contract(g_pre, w_in[...], (1, 1)).astype(jnp.bfloat16)
    hidden_out[...] = (pre * sigma).astype(jnp.bfloat16)


def node_update(terms, g_hidden, w_in, b_in):
    rows, units = g_hidden.shape
    width = w_in.shape[0]
    return pl.pallas_call(
        functools.partial(node_kernel, len(terms)),
        out_shape=[
            jax.ShapeDtypeStruct((rows, width), jnp.bfloat16),
            jax.ShapeDtypeStruct((rows, units), jnp.bfloat16),
        ],
        in_specs=[VMEM] * (len(terms) + 3),
        out_specs=[VMEM] * 2,
        compiler_params=pltpu.CompilerParams(vmem_limit_bytes=32 * 1024 * 1024),
        cost_estimate=pl.CostEstimate(
            flops=4 * rows * width * units, bytes_accessed=8 * rows * units, transcendentals=rows * units
        ),
        name="node_update",
    )(*terms, g_hidden, w_in, b_in.reshape(1, -1))


def project_kernel(hidden, feats, w_out, b_out, out):
    projected = contract(hidden[...], w_out[...], (1, 0)) + b_out[...]
    out[...] = (feats[...].astype(jnp.float32) + projected).astype(jnp.bfloat16)


def project(hidden, node_feats, w_out, b_out):
    rows, units = hidden.shape
    width = w_out.shape[1]
    return pl.pallas_call(
        project_kernel,
        out_shape=jax.ShapeDtypeStruct((rows, width), jnp.bfloat16),
        in_specs=[VMEM] * 4,
        out_specs=VMEM,
        compiler_params=pltpu.CompilerParams(vmem_limit_bytes=32 * 1024 * 1024),
        cost_estimate=pl.CostEstimate(
            flops=2 * rows * width * units, bytes_accessed=2 * rows * units, transcendentals=0
        ),
        name="project",
    )(hidden, node_feats, w_out, b_out.reshape(1, -1))


def close_kernel(n_terms, *refs):
    cot, out = refs[n_terms:]
    total = add_terms(refs[:n_terms], out.shape[0])
    out[...] = (cot[...].astype(jnp.float32) + total).astype(jnp.bfloat16)


def close_grad(terms, cot_out):
    return pl.pallas_call(
        functools.partial(close_kernel, len(terms)),
        out_shape=jax.ShapeDtypeStruct(cot_out.shape, jnp.bfloat16),
        in_specs=[VMEM] * (len(terms) + 1),
        out_specs=VMEM,
        compiler_params=pltpu.CompilerParams(vmem_limit_bytes=32 * 1024 * 1024),
        name="close_grad",
    )(*terms, cot_out)


def local(node_feats, adj_tiles, col_index, w_in, b_in, w_out, b_out, cot_out):
    where = jnp.stack([lax.axis_index("blk"), lax.axis_index("rep")]).astype(jnp.int32)
    table = jnp.concatenate([col_index.reshape(-1), where])
    g_hidden = early(cot_out, w_out)
    table, g_hidden = lax.optimization_barrier((table, g_hidden))
    panel = gather_blocks(node_feats)
    terms = tile_products(panel, adj_tiles, table, node_feats.shape[0])
    g_agg, hidden = node_update(terms, g_hidden, w_in, b_in)
    out_feats = project(hidden, node_feats, w_out, b_out)
    panel = gather_blocks(g_agg)
    terms = tile_products(panel, adj_tiles, table, node_feats.shape[0])
    return (out_feats, close_grad(terms, cot_out))


def solution(mesh):
    placed = (
        P(("blk", "rep"), None),
        P("blk", "rep", None, None, None),
        P("blk", "rep", None),
        P(),
        P(),
        P(),
        P(),
        P(("blk", "rep"), None),
    )
    return jax.shard_map(
        local,
        mesh=mesh,
        in_specs=placed,
        out_specs=(P(("blk", "rep"), None), P(("blk", "rep"), None)),
        check_vma=False,
    )
```

```python
import functools

import jax
import jax.numpy as jnp
from jax import lax
from jax.experimental import pallas as pl
from jax.experimental.pallas import tpu as pltpu
from jax.sharding import PartitionSpec as P

BLOCK = 128
VMEM = pl.BlockSpec(memory_space=pltpu.VMEM)
SMEM = pl.BlockSpec(memory_space=pltpu.SMEM)


BESIDE = 2 * 10**10
LINE = 8


def rotations(n):
    return sorted(range(2, n, 2), key=lambda slot: (min(slot, n - slot), -slot))


def gather_blocks(rows):
    n = lax.axis_size("blk")
    if n > LINE:
        return [(None, lax.all_gather(rows, "blk", axis=0, tiled=True))]
    other = [(i, i ^ 1) for i in range(n)]
    got = [(0, rows), (1, lax.ppermute(rows, "blk", other))]
    for slot in reversed(rotations(n)):
        column = lax.ppermute(rows, "blk", [((i + slot) % n, i) for i in range(n)])
        got += [(slot, column), (slot + 1, lax.ppermute(column, "blk", other))]
    return got


def position(table, tiles):
    count = tiles.shape[0] * tiles.shape[2]
    return table[count], table[count + 1]


def add_blocks(table, tiles, panel, out, owners):
    per_owner = out.shape[0] // (BLOCK * len(owners))
    for j, owner in enumerate(owners):
        for i in range(per_owner):
            g = owner * per_owner + i
            slots_here = range(tiles.shape[2])
            starts = [pl.multiple_of(table[g * tiles.shape[2] + k] * BLOCK, BLOCK) for k in slots_here]
            left = jnp.concatenate([tiles[g, 0, k] for k in slots_here], axis=1)
            right = jnp.concatenate([panel[pl.ds(start, BLOCK), :] for start in starts], axis=0)
            summed = jnp.dot(left, right, preferred_element_type=jnp.float32)
            out[pl.ds((j * per_owner + i) * BLOCK, BLOCK), :] = summed.astype(out.dtype)


def other_kernel(places, reps, table, tiles, *refs):
    pieces, panel, out = refs[: len(places)], refs[-2], refs[-1]
    blk, rep = position(table, tiles)
    shard_rows = tiles.shape[0] * BLOCK // reps
    shards = panel.shape[0] // shard_rows
    side = lax.rem(blk, 2)
    for slot, piece in zip(places, pieces):
        if slot is None:
            panel[...] = piece[...]
        else:
            shard = lax.rem(blk - side + slot // 2 * 2, shards) + lax.bitwise_xor(side, slot % 2)
            panel[pl.ds(pl.multiple_of(shard * shard_rows, shard_rows), shard_rows), :] = piece[...]
    add_blocks(table, tiles, panel, out, [lax.bitwise_xor(rep, d) for d in range(1, reps, 2)])


def other_sums(gathered, adj_tiles, table):
    reps = lax.axis_size("rep")
    pieces = [piece for _, piece in gathered]
    width = pieces[0].shape[1]
    rows = adj_tiles.shape[0] * BLOCK // reps
    length = lax.axis_size("blk") * rows
    return pl.pallas_call(
        functools.partial(other_kernel, [slot for slot, _ in gathered], reps),
        out_shape=[
            jax.ShapeDtypeStruct((length, width), jnp.bfloat16),
            jax.ShapeDtypeStruct((rows * (reps // 2), width), jnp.bfloat16),
        ],
        in_specs=[SMEM, VMEM] + [VMEM] * len(pieces),
        out_specs=[VMEM] * 2,
        compiler_params=pltpu.CompilerParams(vmem_limit_bytes=32 * 1024 * 1024),
        cost_estimate=product_cost(adj_tiles, width, reps),
        name="other_sums",
    )(table, adj_tiles, *pieces)


def sums_kernel(owners, table, tiles, panel, out):
    blk, rep = position(table, tiles)
    add_blocks(table, tiles, panel, out, [lax.bitwise_xor(rep, d) for d in owners])


def sums(panel, adj_tiles, table, owners, kind, name):
    reps = lax.axis_size("rep")
    rows, width = adj_tiles.shape[0] * BLOCK // reps * len(owners), panel.shape[1]
    return pl.pallas_call(
        functools.partial(sums_kernel, owners),
        out_shape=jax.ShapeDtypeStruct((rows, width), kind),
        in_specs=[SMEM, VMEM, VMEM],
        out_specs=VMEM,
        compiler_params=pltpu.CompilerParams(vmem_limit_bytes=32 * 1024 * 1024),
        cost_estimate=product_cost(adj_tiles, width, reps),
        name=name,
    )(table, adj_tiles, panel)


def product_cost(adj_tiles, width, reps):
    size = adj_tiles.size // reps
    return pl.CostEstimate(flops=2 * size * width, bytes_accessed=2 * size, transcendentals=0)


def add_cores_kernel(own, core, *outs):
    rows = outs[0].shape[0]
    skip = core.shape[0] - own.shape[0]
    for j, out in enumerate(outs):
        here, there = pl.ds(j * rows, rows), pl.ds(skip + j * rows, rows)
        out[...] = (own[here, :] + core[there, :].astype(jnp.float32)).astype(jnp.bfloat16)


def add_cores(own, core, rows):
    width = own.shape[1]
    return pl.pallas_call(
        add_cores_kernel,
        out_shape=[jax.ShapeDtypeStruct((rows, width), jnp.bfloat16)] * (own.shape[0] // rows),
        in_specs=[VMEM] * 2,
        out_specs=[VMEM] * (own.shape[0] // rows),
        compiler_params=pltpu.CompilerParams(vmem_limit_bytes=32 * 1024 * 1024),
        name="add_cores",
    )(own, core)


def tile_products(gathered, adj_tiles, table):
    reps = lax.axis_size("rep")
    panel, across = other_sums(gathered, adj_tiles, table)
    core = lax.ppermute(across, "rep", [(i, i ^ 1) for i in range(reps)])
    own = sums(panel, adj_tiles, table, range(2, reps, 2), jnp.float32, "own_far")
    rows = adj_tiles.shape[0] * BLOCK // reps
    sent = add_cores(own, core, rows)
    panel, sent = lax.optimization_barrier((panel, sent))
    near = sums(panel, adj_tiles, table, [0], jnp.float32, "own_near")
    terms = [near, core]
    for j, piece in enumerate(sent, 1):
        terms.append(lax.ppermute(piece, "rep", [(i, i ^ (2 * j)) for i in range(reps)]))
    return terms


def add_terms(terms, rows):
    total = terms[0][pl.ds(0, rows), :]
    for term in terms[1:]:
        total = total + term[pl.ds(0, rows), :].astype(jnp.float32)
    return total


def contract(a, b, dims):
    return lax.dot_general(a, b, ((dims[:1], dims[1:]), ((), ())), preferred_element_type=jnp.float32)


def early_kernel(cot, w_out, g_hidden):
    g_hidden[...] = contract(cot[...], w_out[...], (1, 1))


def early(cot_out, w_out):
    rows, width = cot_out.shape
    units = w_out.shape[0]
    return pl.pallas_call(
        early_kernel,
        out_shape=jax.ShapeDtypeStruct((rows, units), jnp.float32),
        in_specs=[VMEM] * 2,
        out_specs=VMEM,
        compiler_params=pltpu.CompilerParams(vmem_limit_bytes=32 * 1024 * 1024),
        cost_estimate=pl.CostEstimate(flops=BESIDE, bytes_accessed=8 * rows * units, transcendentals=0),
        name="early",
    )(cot_out, w_out)


def node_kernel(n_terms, *refs):
    terms = refs[:n_terms]
    g_hidden, w_in, b_in, g_out, hidden_out = refs[n_terms:]
    rows = g_out.shape[0]
    agg_b = add_terms(terms, rows).astype(jnp.bfloat16)
    pre = contract(agg_b, w_in[...], (1, 0)) + b_in[...]
    sigma = 1.0 / (1.0 + jnp.exp(-pre))
    g_pre = (g_hidden[...] * sigma * (1.0 + pre * (1.0 - sigma))).astype(jnp.bfloat16)
    g_out[...] = contract(g_pre, w_in[...], (1, 1)).astype(jnp.bfloat16)
    hidden_out[...] = (pre * sigma).astype(jnp.bfloat16)


def node_update(terms, g_hidden, w_in, b_in):
    rows, units = g_hidden.shape
    width = w_in.shape[0]
    return pl.pallas_call(
        functools.partial(node_kernel, len(terms)),
        out_shape=[
            jax.ShapeDtypeStruct((rows, width), jnp.bfloat16),
            jax.ShapeDtypeStruct((rows, units), jnp.bfloat16),
        ],
        in_specs=[VMEM] * (len(terms) + 3),
        out_specs=[VMEM] * 2,
        compiler_params=pltpu.CompilerParams(vmem_limit_bytes=32 * 1024 * 1024),
        cost_estimate=pl.CostEstimate(
            flops=4 * rows * width * units, bytes_accessed=8 * rows * units, transcendentals=rows * units
        ),
        name="node_update",
    )(*terms, g_hidden, w_in, b_in.reshape(1, -1))


def project_kernel(hidden, feats, w_out, b_out, out):
    projected = contract(hidden[...], w_out[...], (1, 0)) + b_out[...]
    out[...] = (feats[...].astype(jnp.float32) + projected).astype(jnp.bfloat16)


def project(hidden, node_feats, w_out, b_out):
    rows, units = hidden.shape
    width = w_out.shape[1]
    return pl.pallas_call(
        project_kernel,
        out_shape=jax.ShapeDtypeStruct((rows, width), jnp.bfloat16),
        in_specs=[VMEM] * 4,
        out_specs=VMEM,
        compiler_params=pltpu.CompilerParams(vmem_limit_bytes=32 * 1024 * 1024),
        cost_estimate=pl.CostEstimate(
            flops=2 * rows * width * units, bytes_accessed=2 * rows * units, transcendentals=0
        ),
        name="project",
    )(hidden, node_feats, w_out, b_out.reshape(1, -1))


def close_kernel(*refs):
    terms, cot, out = refs[:-2], refs[-2], refs[-1]
    total = add_terms(terms, out.shape[0])
    out[...] = (cot[...].astype(jnp.float32) + total).astype(jnp.bfloat16)


def close_grad(terms, cot_out):
    return pl.pallas_call(
        close_kernel,
        out_shape=jax.ShapeDtypeStruct(cot_out.shape, jnp.bfloat16),
        in_specs=[VMEM] * (len(terms) + 1),
        out_specs=VMEM,
        compiler_params=pltpu.CompilerParams(vmem_limit_bytes=32 * 1024 * 1024),
        name="close_grad",
    )(*terms, cot_out)


def local(node_feats, adj_tiles, col_index, w_in, b_in, w_out, b_out, cot_out):
    where = jnp.stack([lax.axis_index("blk"), lax.axis_index("rep")]).astype(jnp.int32)
    table = jnp.concatenate([col_index.reshape(-1), where])
    g_hidden = early(cot_out, w_out)
    table, g_hidden = lax.optimization_barrier((table, g_hidden))
    terms = tile_products(gather_blocks(node_feats), adj_tiles, table)
    g_agg, hidden = node_update(terms, g_hidden, w_in, b_in)
    out_feats = project(hidden, node_feats, w_out, b_out)
    terms = tile_products(gather_blocks(g_agg), adj_tiles, table)
    return (out_feats, close_grad(terms, cot_out))


def solution(mesh):
    placed = (
        P(("blk", "rep"), None),
        P("blk", "rep", None, None, None),
        P("blk", "rep", None),
        P(),
        P(),
        P(),
        P(),
        P(("blk", "rep"), None),
    )
    return jax.shard_map(
        local,
        mesh=mesh,
        in_specs=placed,
        out_specs=(P(("blk", "rep"), None), P(("blk", "rep"), None)),
        check_vma=False,
    )
```

```python
import functools

import jax
import jax.numpy as jnp
from jax import lax
from jax.experimental import pallas as pl
from jax.experimental.pallas import tpu as pltpu
from jax.sharding import PartitionSpec as P

BLOCK = 128
VMEM = pl.BlockSpec(memory_space=pltpu.VMEM)
SMEM = pl.BlockSpec(memory_space=pltpu.SMEM)


BESIDE = 2 * 10**10
PAIRS = 4


def after(pair):
    return (3 * pair + 2) % (PAIRS + 1)


def before(pair):
    return (2 * pair + 1) % (PAIRS + 1)


def gather_blocks(rows):
    n = lax.axis_size("blk")
    if n != 2 * PAIRS:
        return [("all", lax.all_gather(rows, "blk", axis=0, tiled=True))]

    def beside(piece):
        return lax.ppermute(piece, "blk", [(i, i ^ 1) for i in range(n)])

    def step(piece, hop):
        return lax.ppermute(piece, "blk", [(i, 2 * hop(i // 2) + i % 2) for i in range(n)])

    first = step(rows, after)
    second = step(rows, before)
    third = step(first, after)
    own_beside = beside(rows)
    onward, _ = lax.optimization_barrier((first, own_beside))
    return [
        ("own", rows),
        ("own beside", own_beside),
        ("second", second),
        ("second beside", beside(second)),
        ("third", third),
        ("third beside", beside(third)),
        ("first", first),
        ("first beside", beside(onward)),
    ]


def place_pieces(panel, blk, rows, names, pieces):
    got = dict(zip(names, pieces))
    if "all" in got:
        panel[...] = got["all"][...]
        return
    pair, side = blk // 2, lax.rem(blk, 2)
    came = {"own": pair, "first": before(pair), "second": after(pair), "third": before(before(pair))}
    for name, source in came.items():
        for which, other in ((name, 0), (name + " beside", 1)):
            start = (2 * source + lax.bitwise_xor(side, other)) * rows
            panel[pl.ds(pl.multiple_of(start, rows), rows), :] = got[which][...]


def position(table, tiles):
    count = tiles.shape[0] * tiles.shape[2]
    return table[count], table[count + 1]


def add_blocks(table, tiles, panel, out, owners):
    per_owner = out.shape[0] // (BLOCK * len(owners))
    for j, owner in enumerate(owners):
        for i in range(per_owner):
            g = owner * per_owner + i
            slots_here = range(tiles.shape[2])
            starts = [pl.multiple_of(table[g * tiles.shape[2] + k] * BLOCK, BLOCK) for k in slots_here]
            left = jnp.concatenate([tiles[g, 0, k] for k in slots_here], axis=1)
            right = jnp.concatenate([panel[pl.ds(start, BLOCK), :] for start in starts], axis=0)
            summed = jnp.dot(left, right, preferred_element_type=jnp.float32)
            out[pl.ds((j * per_owner + i) * BLOCK, BLOCK), :] = summed.astype(out.dtype)


def other_kernel(names, reps, table, tiles, *refs):
    pieces, panel, out = refs[: len(names)], refs[-2], refs[-1]
    blk, rep = position(table, tiles)
    place_pieces(panel, blk, tiles.shape[0] * BLOCK // reps, names, pieces)
    add_blocks(table, tiles, panel, out, [lax.bitwise_xor(rep, d) for d in range(1, reps, 2)])


def other_sums(gathered, adj_tiles, table):
    reps = lax.axis_size("rep")
    names, pieces = zip(*gathered)
    width = pieces[0].shape[1]
    rows = adj_tiles.shape[0] * BLOCK // reps
    length = lax.axis_size("blk") * rows
    return pl.pallas_call(
        functools.partial(other_kernel, names, reps),
        out_shape=[
            jax.ShapeDtypeStruct((length, width), jnp.bfloat16),
            jax.ShapeDtypeStruct((rows * (reps // 2), width), jnp.bfloat16),
        ],
        in_specs=[SMEM, VMEM] + [VMEM] * len(pieces),
        out_specs=[VMEM] * 2,
        compiler_params=pltpu.CompilerParams(vmem_limit_bytes=32 * 1024 * 1024),
        cost_estimate=product_cost(adj_tiles, width, reps),
        name="other_sums",
    )(table, adj_tiles, *pieces)


def sums_kernel(owners, table, tiles, panel, out):
    blk, rep = position(table, tiles)
    add_blocks(table, tiles, panel, out, [lax.bitwise_xor(rep, d) for d in owners])


def sums(panel, adj_tiles, table, owners, kind, name):
    reps = lax.axis_size("rep")
    rows, width = adj_tiles.shape[0] * BLOCK // reps * len(owners), panel.shape[1]
    return pl.pallas_call(
        functools.partial(sums_kernel, owners),
        out_shape=jax.ShapeDtypeStruct((rows, width), kind),
        in_specs=[SMEM, VMEM, VMEM],
        out_specs=VMEM,
        compiler_params=pltpu.CompilerParams(vmem_limit_bytes=32 * 1024 * 1024),
        cost_estimate=product_cost(adj_tiles, width, reps),
        name=name,
    )(table, adj_tiles, panel)


def product_cost(adj_tiles, width, reps):
    size = adj_tiles.size // reps
    return pl.CostEstimate(flops=2 * size * width, bytes_accessed=2 * size, transcendentals=0)


def add_cores_kernel(own, core, *outs):
    rows = outs[0].shape[0]
    for j, out in enumerate(outs):
        here, there = pl.ds(j * rows, rows), pl.ds((j + 1) * rows, rows)
        out[...] = (own[here, :] + core[there, :].astype(jnp.float32)).astype(jnp.bfloat16)


def add_cores(own, core, rows):
    width = own.shape[1]
    return pl.pallas_call(
        add_cores_kernel,
        out_shape=[jax.ShapeDtypeStruct((rows, width), jnp.bfloat16)] * (own.shape[0] // rows),
        in_specs=[VMEM] * 2,
        out_specs=[VMEM] * (own.shape[0] // rows),
        compiler_params=pltpu.CompilerParams(vmem_limit_bytes=32 * 1024 * 1024),
        name="add_cores",
    )(own, core)


def tile_products(pieces, adj_tiles, table, rows):
    reps = lax.axis_size("rep")
    panel, across = other_sums(pieces, adj_tiles, table)
    core = lax.ppermute(across, "rep", [(i, i ^ 1) for i in range(reps)])
    own = sums(panel, adj_tiles, table, range(2, reps, 2), jnp.float32, "own_far")
    parts = add_cores(own, core, rows)
    panel, parts = lax.optimization_barrier((panel, parts))
    near = sums(panel, adj_tiles, table, [0], jnp.float32, "own_near")
    terms = [near, core]
    for j, part in enumerate(parts, 1):
        terms.append(lax.ppermute(part, "rep", [(i, i ^ (2 * j)) for i in range(reps)]))
    return terms


def add_terms(terms, rows):
    total = terms[0][pl.ds(0, rows), :]
    for term in terms[1:]:
        total = total + term[pl.ds(0, rows), :].astype(jnp.float32)
    return total


def contract(a, b, dims):
    return lax.dot_general(a, b, ((dims[:1], dims[1:]), ((), ())), preferred_element_type=jnp.float32)


def early_kernel(cot, w_out, g_hidden):
    g_hidden[...] = contract(cot[...], w_out[...], (1, 1))


def early(cot_out, w_out):
    rows, width = cot_out.shape
    units = w_out.shape[0]
    return pl.pallas_call(
        early_kernel,
        out_shape=jax.ShapeDtypeStruct((rows, units), jnp.float32),
        in_specs=[VMEM] * 2,
        out_specs=VMEM,
        compiler_params=pltpu.CompilerParams(vmem_limit_bytes=32 * 1024 * 1024),
        cost_estimate=pl.CostEstimate(flops=BESIDE, bytes_accessed=8 * rows * units, transcendentals=0),
        name="early",
    )(cot_out, w_out)


def node_kernel(n_terms, *refs):
    terms = refs[:n_terms]
    g_hidden, w_in, b_in, g_out, hidden_out = refs[n_terms:]
    agg_b = add_terms(terms, g_out.shape[0]).astype(jnp.bfloat16)
    pre = contract(agg_b, w_in[...], (1, 0)) + b_in[...]
    sigma = 1.0 / (1.0 + jnp.exp(-pre))
    g_pre = (g_hidden[...] * sigma * (1.0 + pre * (1.0 - sigma))).astype(jnp.bfloat16)
    g_out[...] = contract(g_pre, w_in[...], (1, 1)).astype(jnp.bfloat16)
    hidden_out[...] = (pre * sigma).astype(jnp.bfloat16)


def node_update(terms, g_hidden, w_in, b_in):
    rows, units = g_hidden.shape
    width = w_in.shape[0]
    return pl.pallas_call(
        functools.partial(node_kernel, len(terms)),
        out_shape=[
            jax.ShapeDtypeStruct((rows, width), jnp.bfloat16),
            jax.ShapeDtypeStruct((rows, units), jnp.bfloat16),
        ],
        in_specs=[VMEM] * (len(terms) + 3),
        out_specs=[VMEM] * 2,
        compiler_params=pltpu.CompilerParams(vmem_limit_bytes=32 * 1024 * 1024),
        cost_estimate=pl.CostEstimate(
            flops=4 * rows * width * units, bytes_accessed=8 * rows * units, transcendentals=rows * units
        ),
        name="node_update",
    )(*terms, g_hidden, w_in, b_in.reshape(1, -1))


def project_kernel(hidden, feats, w_out, b_out, out):
    projected = contract(hidden[...], w_out[...], (1, 0)) + b_out[...]
    out[...] = (feats[...].astype(jnp.float32) + projected).astype(jnp.bfloat16)


def project(hidden, node_feats, w_out, b_out):
    rows, units = hidden.shape
    width = w_out.shape[1]
    return pl.pallas_call(
        project_kernel,
        out_shape=jax.ShapeDtypeStruct((rows, width), jnp.bfloat16),
        in_specs=[VMEM] * 4,
        out_specs=VMEM,
        compiler_params=pltpu.CompilerParams(vmem_limit_bytes=32 * 1024 * 1024),
        cost_estimate=pl.CostEstimate(
            flops=2 * rows * width * units, bytes_accessed=2 * rows * units, transcendentals=0
        ),
        name="project",
    )(hidden, node_feats, w_out, b_out.reshape(1, -1))


def close_kernel(n_terms, *refs):
    cot, out = refs[n_terms:]
    total = add_terms(refs[:n_terms], out.shape[0])
    out[...] = (cot[...].astype(jnp.float32) + total).astype(jnp.bfloat16)


def close_grad(terms, cot_out):
    return pl.pallas_call(
        functools.partial(close_kernel, len(terms)),
        out_shape=jax.ShapeDtypeStruct(cot_out.shape, jnp.bfloat16),
        in_specs=[VMEM] * (len(terms) + 1),
        out_specs=VMEM,
        compiler_params=pltpu.CompilerParams(vmem_limit_bytes=32 * 1024 * 1024),
        name="close_grad",
    )(*terms, cot_out)


def local(node_feats, adj_tiles, col_index, w_in, b_in, w_out, b_out, cot_out):
    where = jnp.stack([lax.axis_index("blk"), lax.axis_index("rep")]).astype(jnp.int32)
    table = jnp.concatenate([col_index.reshape(-1), where])
    g_hidden = early(cot_out, w_out)
    table, g_hidden = lax.optimization_barrier((table, g_hidden))
    panel = gather_blocks(node_feats)
    terms = tile_products(panel, adj_tiles, table, node_feats.shape[0])
    g_agg, hidden = node_update(terms, g_hidden, w_in, b_in)
    out_feats = project(hidden, node_feats, w_out, b_out)
    panel = gather_blocks(g_agg)
    terms = tile_products(panel, adj_tiles, table, node_feats.shape[0])
    return (out_feats, close_grad(terms, cot_out))


def solution(mesh):
    placed = (
        P(("blk", "rep"), None),
        P("blk", "rep", None, None, None),
        P("blk", "rep", None),
        P(),
        P(),
        P(),
        P(),
        P(("blk", "rep"), None),
    )
    return jax.shard_map(
        local,
        mesh=mesh,
        in_specs=placed,
        out_specs=(P(("blk", "rep"), None), P(("blk", "rep"), None)),
        check_vma=False,
    )
```

```python
import functools

import jax
import jax.numpy as jnp
from jax import lax
from jax.experimental import pallas as pl
from jax.experimental.pallas import tpu as pltpu
from jax.sharding import PartitionSpec as P

BLOCK = 128
VMEM = pl.BlockSpec(memory_space=pltpu.VMEM)
SMEM = pl.BlockSpec(memory_space=pltpu.SMEM)


BESIDE = 2 * 10**10
PAIRS = 4


def after(pair):
    return (3 * pair + 2) % (PAIRS + 1)


def before(pair):
    return (2 * pair + 1) % (PAIRS + 1)


def gather_blocks(rows):
    n = lax.axis_size("blk")
    if n != 2 * PAIRS:
        return [("all", lax.all_gather(rows, "blk", axis=0, tiled=True))]

    def beside(piece):
        return lax.ppermute(piece, "blk", [(i, i ^ 1) for i in range(n)])

    def step(piece, hop):
        return lax.ppermute(piece, "blk", [(i, 2 * hop(i // 2) + i % 2) for i in range(n)])

    first, second, own_beside = step(rows, after), step(rows, before), beside(rows)
    first_beside = beside(first)
    third = step(lax.optimization_barrier((first, own_beside))[0], after)
    second_beside = beside(second)
    third_beside = beside(lax.optimization_barrier((third, first_beside))[0])
    return [
        ("own", rows),
        ("own beside", own_beside),
        ("second", second),
        ("second beside", second_beside),
        ("third", third),
        ("third beside", third_beside),
        ("first", first),
        ("first beside", first_beside),
    ]


def place_pieces(panel, blk, rows, names, pieces):
    got = dict(zip(names, pieces))
    if "all" in got:
        panel[...] = got["all"][...]
        return
    pair, side = blk // 2, lax.rem(blk, 2)
    came = {"own": pair, "first": before(pair), "second": after(pair), "third": before(before(pair))}
    for name, source in came.items():
        for which, other in ((name, 0), (name + " beside", 1)):
            start = (2 * source + lax.bitwise_xor(side, other)) * rows
            panel[pl.ds(pl.multiple_of(start, rows), rows), :] = got[which][...]


def position(table, tiles):
    count = tiles.shape[0] * tiles.shape[2]
    return table[count], table[count + 1]


def add_blocks(table, tiles, panel, out, owners):
    per_owner = out.shape[0] // (BLOCK * len(owners))
    for j, owner in enumerate(owners):
        for i in range(per_owner):
            g = owner * per_owner + i
            slots_here = range(tiles.shape[2])
            starts = [pl.multiple_of(table[g * tiles.shape[2] + k] * BLOCK, BLOCK) for k in slots_here]
            left = jnp.concatenate([tiles[g, 0, k] for k in slots_here], axis=1)
            right = jnp.concatenate([panel[pl.ds(start, BLOCK), :] for start in starts], axis=0)
            summed = jnp.dot(left, right, preferred_element_type=jnp.float32)
            out[pl.ds((j * per_owner + i) * BLOCK, BLOCK), :] = summed.astype(out.dtype)


def other_kernel(names, reps, table, tiles, *refs):
    pieces, panel, out = refs[: len(names)], refs[-2], refs[-1]
    blk, rep = position(table, tiles)
    place_pieces(panel, blk, tiles.shape[0] * BLOCK // reps, names, pieces)
    add_blocks(table, tiles, panel, out, [lax.bitwise_xor(rep, d) for d in range(1, reps, 2)])


def other_sums(gathered, adj_tiles, table):
    reps = lax.axis_size("rep")
    names, pieces = zip(*gathered)
    width = pieces[0].shape[1]
    rows = adj_tiles.shape[0] * BLOCK // reps
    length = lax.axis_size("blk") * rows
    return pl.pallas_call(
        functools.partial(other_kernel, names, reps),
        out_shape=[
            jax.ShapeDtypeStruct((length, width), jnp.bfloat16),
            jax.ShapeDtypeStruct((rows * (reps // 2), width), jnp.bfloat16),
        ],
        in_specs=[SMEM, VMEM] + [VMEM] * len(pieces),
        out_specs=[VMEM] * 2,
        compiler_params=pltpu.CompilerParams(vmem_limit_bytes=32 * 1024 * 1024),
        cost_estimate=product_cost(adj_tiles, width, reps),
        name="other_sums",
    )(table, adj_tiles, *pieces)


def sums_kernel(owners, table, tiles, panel, out):
    blk, rep = position(table, tiles)
    add_blocks(table, tiles, panel, out, [lax.bitwise_xor(rep, d) for d in owners])


def sums(panel, adj_tiles, table, owners, kind, name):
    reps = lax.axis_size("rep")
    rows, width = adj_tiles.shape[0] * BLOCK // reps * len(owners), panel.shape[1]
    return pl.pallas_call(
        functools.partial(sums_kernel, owners),
        out_shape=jax.ShapeDtypeStruct((rows, width), kind),
        in_specs=[SMEM, VMEM, VMEM],
        out_specs=VMEM,
        compiler_params=pltpu.CompilerParams(vmem_limit_bytes=32 * 1024 * 1024),
        cost_estimate=product_cost(adj_tiles, width, reps),
        name=name,
    )(table, adj_tiles, panel)


def product_cost(adj_tiles, width, reps):
    size = adj_tiles.size // reps
    return pl.CostEstimate(flops=2 * size * width, bytes_accessed=2 * size, transcendentals=0)


def add_cores_kernel(own, core, *outs):
    rows = outs[0].shape[0]
    for j, out in enumerate(outs):
        here, there = pl.ds(j * rows, rows), pl.ds((j + 1) * rows, rows)
        out[...] = (own[here, :] + core[there, :].astype(jnp.float32)).astype(jnp.bfloat16)


def add_cores(own, core, rows):
    width = own.shape[1]
    return pl.pallas_call(
        add_cores_kernel,
        out_shape=[jax.ShapeDtypeStruct((rows, width), jnp.bfloat16)] * (own.shape[0] // rows),
        in_specs=[VMEM] * 2,
        out_specs=[VMEM] * (own.shape[0] // rows),
        compiler_params=pltpu.CompilerParams(vmem_limit_bytes=32 * 1024 * 1024),
        name="add_cores",
    )(own, core)


def tile_products(pieces, adj_tiles, table, rows):
    reps = lax.axis_size("rep")
    panel, across = other_sums(pieces, adj_tiles, table)
    core = lax.ppermute(across, "rep", [(i, i ^ 1) for i in range(reps)])
    own = sums(panel, adj_tiles, table, range(2, reps, 2), jnp.float32, "own_far")
    parts = add_cores(own, core, rows)
    panel, parts = lax.optimization_barrier((panel, parts))
    near = sums(panel, adj_tiles, table, [0], jnp.float32, "own_near")
    terms = [near, core]
    for j, part in enumerate(parts, 1):
        terms.append(lax.ppermute(part, "rep", [(i, i ^ (2 * j)) for i in range(reps)]))
    return terms


def add_terms(terms, rows):
    total = terms[0][pl.ds(0, rows), :]
    for term in terms[1:]:
        total = total + term[pl.ds(0, rows), :].astype(jnp.float32)
    return total


def contract(a, b, dims):
    return lax.dot_general(a, b, ((dims[:1], dims[1:]), ((), ())), preferred_element_type=jnp.float32)


def early_kernel(cot, w_out, g_hidden):
    g_hidden[...] = contract(cot[...], w_out[...], (1, 1))


def early(cot_out, w_out):
    rows, width = cot_out.shape
    units = w_out.shape[0]
    return pl.pallas_call(
        early_kernel,
        out_shape=jax.ShapeDtypeStruct((rows, units), jnp.float32),
        in_specs=[VMEM] * 2,
        out_specs=VMEM,
        compiler_params=pltpu.CompilerParams(vmem_limit_bytes=32 * 1024 * 1024),
        cost_estimate=pl.CostEstimate(flops=BESIDE, bytes_accessed=8 * rows * units, transcendentals=0),
        name="early",
    )(cot_out, w_out)


def node_kernel(n_terms, *refs):
    terms = refs[:n_terms]
    g_hidden, w_in, b_in, g_out, hidden_out = refs[n_terms:]
    agg_b = add_terms(terms, g_out.shape[0]).astype(jnp.bfloat16)
    pre = contract(agg_b, w_in[...], (1, 0)) + b_in[...]
    sigma = 1.0 / (1.0 + jnp.exp(-pre))
    g_pre = (g_hidden[...] * sigma * (1.0 + pre * (1.0 - sigma))).astype(jnp.bfloat16)
    g_out[...] = contract(g_pre, w_in[...], (1, 1)).astype(jnp.bfloat16)
    hidden_out[...] = (pre * sigma).astype(jnp.bfloat16)


def node_update(terms, g_hidden, w_in, b_in):
    rows, units = g_hidden.shape
    width = w_in.shape[0]
    return pl.pallas_call(
        functools.partial(node_kernel, len(terms)),
        out_shape=[
            jax.ShapeDtypeStruct((rows, width), jnp.bfloat16),
            jax.ShapeDtypeStruct((rows, units), jnp.bfloat16),
        ],
        in_specs=[VMEM] * (len(terms) + 3),
        out_specs=[VMEM] * 2,
        compiler_params=pltpu.CompilerParams(vmem_limit_bytes=32 * 1024 * 1024),
        cost_estimate=pl.CostEstimate(
            flops=4 * rows * width * units, bytes_accessed=8 * rows * units, transcendentals=rows * units
        ),
        name="node_update",
    )(*terms, g_hidden, w_in, b_in.reshape(1, -1))


def project_kernel(hidden, feats, w_out, b_out, out):
    projected = contract(hidden[...], w_out[...], (1, 0)) + b_out[...]
    out[...] = (feats[...].astype(jnp.float32) + projected).astype(jnp.bfloat16)


def project(hidden, node_feats, w_out, b_out):
    rows, units = hidden.shape
    width = w_out.shape[1]
    return pl.pallas_call(
        project_kernel,
        out_shape=jax.ShapeDtypeStruct((rows, width), jnp.bfloat16),
        in_specs=[VMEM] * 4,
        out_specs=VMEM,
        compiler_params=pltpu.CompilerParams(vmem_limit_bytes=32 * 1024 * 1024),
        cost_estimate=pl.CostEstimate(
            flops=2 * rows * width * units, bytes_accessed=2 * rows * units, transcendentals=0
        ),
        name="project",
    )(hidden, node_feats, w_out, b_out.reshape(1, -1))


def close_kernel(n_terms, *refs):
    cot, out = refs[n_terms:]
    total = add_terms(refs[:n_terms], out.shape[0])
    out[...] = (cot[...].astype(jnp.float32) + total).astype(jnp.bfloat16)


def close_grad(terms, cot_out):
    return pl.pallas_call(
        functools.partial(close_kernel, len(terms)),
        out_shape=jax.ShapeDtypeStruct(cot_out.shape, jnp.bfloat16),
        in_specs=[VMEM] * (len(terms) + 1),
        out_specs=VMEM,
        compiler_params=pltpu.CompilerParams(vmem_limit_bytes=32 * 1024 * 1024),
        name="close_grad",
    )(*terms, cot_out)


def local(node_feats, adj_tiles, col_index, w_in, b_in, w_out, b_out, cot_out):
    where = jnp.stack([lax.axis_index("blk"), lax.axis_index("rep")]).astype(jnp.int32)
    table = jnp.concatenate([col_index.reshape(-1), where])
    g_hidden = early(cot_out, w_out)
    table, g_hidden = lax.optimization_barrier((table, g_hidden))
    panel = gather_blocks(node_feats)
    terms = tile_products(panel, adj_tiles, table, node_feats.shape[0])
    g_agg, hidden = node_update(terms, g_hidden, w_in, b_in)
    out_feats = project(hidden, node_feats, w_out, b_out)
    panel = gather_blocks(g_agg)
    terms = tile_products(panel, adj_tiles, table, node_feats.shape[0])
    return (out_feats, close_grad(terms, cot_out))


def solution(mesh):
    placed = (
        P(("blk", "rep"), None),
        P("blk", "rep", None, None, None),
        P("blk", "rep", None),
        P(),
        P(),
        P(),
        P(),
        P(("blk", "rep"), None),
    )
    return jax.shard_map(
        local,
        mesh=mesh,
        in_specs=placed,
        out_specs=(P(("blk", "rep"), None), P(("blk", "rep"), None)),
        check_vma=False,
    )
```

```python
import functools

import jax
import jax.numpy as jnp
from jax import lax
from jax.experimental import pallas as pl
from jax.experimental.pallas import tpu as pltpu
from jax.sharding import PartitionSpec as P

BLOCK = 128
VMEM = pl.BlockSpec(memory_space=pltpu.VMEM)
SMEM = pl.BlockSpec(memory_space=pltpu.SMEM)


BESIDE = 2 * 10**10
PAIRS = 4


def after(pair):
    return (3 * pair + 2) % (PAIRS + 1)


def before(pair):
    return (2 * pair + 1) % (PAIRS + 1)


def gather_blocks(rows):
    n = lax.axis_size("blk")
    if n != 2 * PAIRS:
        return [("all", lax.all_gather(rows, "blk", axis=0, tiled=True))]

    def beside(piece):
        return lax.ppermute(piece, "blk", [(i, i ^ 1) for i in range(n)])

    def step(piece, hop):
        return lax.ppermute(piece, "blk", [(i, 2 * hop(i // 2) + i % 2) for i in range(n)])

    first, second, own_beside = step(rows, after), step(rows, before), beside(rows)
    first_beside = beside(lax.optimization_barrier((first, own_beside))[0])
    third, third_beside = step(first, after), step(first_beside, after)
    second_beside = beside(second)
    return [
        ("own", rows),
        ("own beside", own_beside),
        ("second", second),
        ("second beside", second_beside),
        ("third", third),
        ("third beside", third_beside),
        ("first", first),
        ("first beside", first_beside),
    ]


def place_pieces(panel, blk, rows, names, pieces):
    got = dict(zip(names, pieces))
    if "all" in got:
        panel[...] = got["all"][...]
        return
    pair, side = blk // 2, lax.rem(blk, 2)
    came = {"own": pair, "first": before(pair), "second": after(pair), "third": before(before(pair))}
    for name, source in came.items():
        for which, other in ((name, 0), (name + " beside", 1)):
            start = (2 * source + lax.bitwise_xor(side, other)) * rows
            panel[pl.ds(pl.multiple_of(start, rows), rows), :] = got[which][...]


def position(table, tiles):
    count = tiles.shape[0] * tiles.shape[2]
    return table[count], table[count + 1]


def add_blocks(table, tiles, panel, out, owners):
    per_owner = out.shape[0] // (BLOCK * len(owners))
    for j, owner in enumerate(owners):
        for i in range(per_owner):
            g = owner * per_owner + i
            slots_here = range(tiles.shape[2])
            starts = [pl.multiple_of(table[g * tiles.shape[2] + k] * BLOCK, BLOCK) for k in slots_here]
            left = jnp.concatenate([tiles[g, 0, k] for k in slots_here], axis=1)
            right = jnp.concatenate([panel[pl.ds(start, BLOCK), :] for start in starts], axis=0)
            summed = jnp.dot(left, right, preferred_element_type=jnp.float32)
            out[pl.ds((j * per_owner + i) * BLOCK, BLOCK), :] = summed.astype(out.dtype)


def other_kernel(names, reps, table, tiles, *refs):
    pieces, panel, out = refs[: len(names)], refs[-2], refs[-1]
    blk, rep = position(table, tiles)
    place_pieces(panel, blk, tiles.shape[0] * BLOCK // reps, names, pieces)
    add_blocks(table, tiles, panel, out, [lax.bitwise_xor(rep, d) for d in range(1, reps, 2)])


def other_sums(gathered, adj_tiles, table):
    reps = lax.axis_size("rep")
    names, pieces = zip(*gathered)
    width = pieces[0].shape[1]
    rows = adj_tiles.shape[0] * BLOCK // reps
    length = lax.axis_size("blk") * rows
    return pl.pallas_call(
        functools.partial(other_kernel, names, reps),
        out_shape=[
            jax.ShapeDtypeStruct((length, width), jnp.bfloat16),
            jax.ShapeDtypeStruct((rows * (reps // 2), width), jnp.bfloat16),
        ],
        in_specs=[SMEM, VMEM] + [VMEM] * len(pieces),
        out_specs=[VMEM] * 2,
        compiler_params=pltpu.CompilerParams(vmem_limit_bytes=32 * 1024 * 1024),
        cost_estimate=product_cost(adj_tiles, width, reps),
        name="other_sums",
    )(table, adj_tiles, *pieces)


def sums_kernel(owners, table, tiles, panel, out):
    blk, rep = position(table, tiles)
    add_blocks(table, tiles, panel, out, [lax.bitwise_xor(rep, d) for d in owners])


def sums(panel, adj_tiles, table, owners, kind, name):
    reps = lax.axis_size("rep")
    rows, width = adj_tiles.shape[0] * BLOCK // reps * len(owners), panel.shape[1]
    return pl.pallas_call(
        functools.partial(sums_kernel, owners),
        out_shape=jax.ShapeDtypeStruct((rows, width), kind),
        in_specs=[SMEM, VMEM, VMEM],
        out_specs=VMEM,
        compiler_params=pltpu.CompilerParams(vmem_limit_bytes=32 * 1024 * 1024),
        cost_estimate=product_cost(adj_tiles, width, reps),
        name=name,
    )(table, adj_tiles, panel)


def product_cost(adj_tiles, width, reps):
    size = adj_tiles.size // reps
    return pl.CostEstimate(flops=2 * size * width, bytes_accessed=2 * size, transcendentals=0)


def add_cores_kernel(own, core, *outs):
    rows = outs[0].shape[0]
    for j, out in enumerate(outs):
        here, there = pl.ds(j * rows, rows), pl.ds((j + 1) * rows, rows)
        out[...] = (own[here, :] + core[there, :].astype(jnp.float32)).astype(jnp.bfloat16)


def add_cores(own, core, rows):
    width = own.shape[1]
    return pl.pallas_call(
        add_cores_kernel,
        out_shape=[jax.ShapeDtypeStruct((rows, width), jnp.bfloat16)] * (own.shape[0] // rows),
        in_specs=[VMEM] * 2,
        out_specs=[VMEM] * (own.shape[0] // rows),
        compiler_params=pltpu.CompilerParams(vmem_limit_bytes=32 * 1024 * 1024),
        name="add_cores",
    )(own, core)


def tile_products(pieces, adj_tiles, table, rows):
    reps = lax.axis_size("rep")
    panel, across = other_sums(pieces, adj_tiles, table)
    core = lax.ppermute(across, "rep", [(i, i ^ 1) for i in range(reps)])
    own = sums(panel, adj_tiles, table, range(2, reps, 2), jnp.float32, "own_far")
    parts = add_cores(own, core, rows)
    panel, parts = lax.optimization_barrier((panel, parts))
    near = sums(panel, adj_tiles, table, [0], jnp.float32, "own_near")
    terms = [near, core]
    for j, part in enumerate(parts, 1):
        terms.append(lax.ppermute(part, "rep", [(i, i ^ (2 * j)) for i in range(reps)]))
    return terms


def add_terms(terms, rows):
    total = terms[0][pl.ds(0, rows), :]
    for term in terms[1:]:
        total = total + term[pl.ds(0, rows), :].astype(jnp.float32)
    return total


def contract(a, b, dims):
    return lax.dot_general(a, b, ((dims[:1], dims[1:]), ((), ())), preferred_element_type=jnp.float32)


def early_kernel(cot, w_out, g_hidden):
    g_hidden[...] = contract(cot[...], w_out[...], (1, 1))


def early(cot_out, w_out):
    rows, width = cot_out.shape
    units = w_out.shape[0]
    return pl.pallas_call(
        early_kernel,
        out_shape=jax.ShapeDtypeStruct((rows, units), jnp.float32),
        in_specs=[VMEM] * 2,
        out_specs=VMEM,
        compiler_params=pltpu.CompilerParams(vmem_limit_bytes=32 * 1024 * 1024),
        cost_estimate=pl.CostEstimate(flops=BESIDE, bytes_accessed=8 * rows * units, transcendentals=0),
        name="early",
    )(cot_out, w_out)


def node_kernel(n_terms, *refs):
    terms = refs[:n_terms]
    g_hidden, w_in, b_in, g_out, hidden_out = refs[n_terms:]
    agg_b = add_terms(terms, g_out.shape[0]).astype(jnp.bfloat16)
    pre = contract(agg_b, w_in[...], (1, 0)) + b_in[...]
    sigma = 1.0 / (1.0 + jnp.exp(-pre))
    g_pre = (g_hidden[...] * sigma * (1.0 + pre * (1.0 - sigma))).astype(jnp.bfloat16)
    g_out[...] = contract(g_pre, w_in[...], (1, 1)).astype(jnp.bfloat16)
    hidden_out[...] = (pre * sigma).astype(jnp.bfloat16)


def node_update(terms, g_hidden, w_in, b_in):
    rows, units = g_hidden.shape
    width = w_in.shape[0]
    return pl.pallas_call(
        functools.partial(node_kernel, len(terms)),
        out_shape=[
            jax.ShapeDtypeStruct((rows, width), jnp.bfloat16),
            jax.ShapeDtypeStruct((rows, units), jnp.bfloat16),
        ],
        in_specs=[VMEM] * (len(terms) + 3),
        out_specs=[VMEM] * 2,
        compiler_params=pltpu.CompilerParams(vmem_limit_bytes=32 * 1024 * 1024),
        cost_estimate=pl.CostEstimate(
            flops=4 * rows * width * units, bytes_accessed=8 * rows * units, transcendentals=rows * units
        ),
        name="node_update",
    )(*terms, g_hidden, w_in, b_in.reshape(1, -1))


def project_kernel(hidden, feats, w_out, b_out, out):
    projected = contract(hidden[...], w_out[...], (1, 0)) + b_out[...]
    out[...] = (feats[...].astype(jnp.float32) + projected).astype(jnp.bfloat16)


def project(hidden, node_feats, w_out, b_out):
    rows, units = hidden.shape
    width = w_out.shape[1]
    return pl.pallas_call(
        project_kernel,
        out_shape=jax.ShapeDtypeStruct((rows, width), jnp.bfloat16),
        in_specs=[VMEM] * 4,
        out_specs=VMEM,
        compiler_params=pltpu.CompilerParams(vmem_limit_bytes=32 * 1024 * 1024),
        cost_estimate=pl.CostEstimate(
            flops=2 * rows * width * units, bytes_accessed=2 * rows * units, transcendentals=0
        ),
        name="project",
    )(hidden, node_feats, w_out, b_out.reshape(1, -1))


def close_kernel(n_terms, *refs):
    cot, out = refs[n_terms:]
    total = add_terms(refs[:n_terms], out.shape[0])
    out[...] = (cot[...].astype(jnp.float32) + total).astype(jnp.bfloat16)


def close_grad(terms, cot_out):
    return pl.pallas_call(
        functools.partial(close_kernel, len(terms)),
        out_shape=jax.ShapeDtypeStruct(cot_out.shape, jnp.bfloat16),
        in_specs=[VMEM] * (len(terms) + 1),
        out_specs=VMEM,
        compiler_params=pltpu.CompilerParams(vmem_limit_bytes=32 * 1024 * 1024),
        name="close_grad",
    )(*terms, cot_out)


def local(node_feats, adj_tiles, col_index, w_in, b_in, w_out, b_out, cot_out):
    where = jnp.stack([lax.axis_index("blk"), lax.axis_index("rep")]).astype(jnp.int32)
    table = jnp.concatenate([col_index.reshape(-1), where])
    g_hidden = early(cot_out, w_out)
    table, g_hidden = lax.optimization_barrier((table, g_hidden))
    panel = gather_blocks(node_feats)
    terms = tile_products(panel, adj_tiles, table, node_feats.shape[0])
    g_agg, hidden = node_update(terms, g_hidden, w_in, b_in)
    out_feats = project(hidden, node_feats, w_out, b_out)
    panel = gather_blocks(g_agg)
    terms = tile_products(panel, adj_tiles, table, node_feats.shape[0])
    return (out_feats, close_grad(terms, cot_out))


def solution(mesh):
    placed = (
        P(("blk", "rep"), None),
        P("blk", "rep", None, None, None),
        P("blk", "rep", None),
        P(),
        P(),
        P(),
        P(),
        P(("blk", "rep"), None),
    )
    return jax.shard_map(
        local,
        mesh=mesh,
        in_specs=placed,
        out_specs=(P(("blk", "rep"), None), P(("blk", "rep"), None)),
        check_vma=False,
    )
```

```python
import functools

import jax
import jax.numpy as jnp
from jax import lax
from jax.experimental import pallas as pl
from jax.experimental.pallas import tpu as pltpu
from jax.sharding import PartitionSpec as P

BLOCK = 128
VMEM = pl.BlockSpec(memory_space=pltpu.VMEM)
SMEM = pl.BlockSpec(memory_space=pltpu.SMEM)


BESIDE = 2 * 10**10
PAIRS = 4
STEPS = ((0, -1, -1), (0, 1, 0), (0, 0, 1), (1, -1, 0), (1, 0, -1), (3, 1, 0), (4, 0, -1))
AFTER = {5: 2}


def after(pair):
    return (3 * pair + 2) % (PAIRS + 1)


def before(pair):
    return (2 * pair + 1) % (PAIRS + 1)


def source(blk, move):
    if move == 0:
        return 2 * (blk // 2) + 1 - blk % 2
    return 2 * (after if move > 0 else before)(blk // 2) + blk % 2


def gather_blocks(rows):
    n, reps = lax.axis_size("blk"), lax.axis_size("rep")
    if n != 2 * PAIRS:
        return [lax.all_gather(rows, "blk", axis=0, tiled=True)]
    pieces = [rows]
    for step, (sent, odd, even) in enumerate(STEPS, 1):
        pairs = []
        for blk in range(n):
            for rep in range(reps):
                pairs.append((source(blk, odd if rep % 2 else even) * reps + rep, blk * reps + rep))
        piece = pieces[sent]
        if step in AFTER:
            piece, _ = lax.optimization_barrier((piece, pieces[AFTER[step]]))
        pieces.append(lax.ppermute(piece, ("blk", "rep"), pairs))
    return pieces


def place_pieces(panel, blk, rep, pieces):
    if len(pieces) == 1:
        panel[...] = pieces[0][...]
        return
    rows = pieces[0].shape[0]

    for parity in range(2):

        @pl.when(lax.rem(rep, 2) == parity)
        def _(parity=parity):
            turns = [(0, 0)]
            for sent, odd, even in STEPS:
                move = odd if parity else even
                turn, side = turns[sent]
                turns.append(((turn + move) % PAIRS, side ^ (move == 0)))
            for (turn, side), piece in zip(turns, pieces):
                pair = blk // 2
                for _ in range(turn):
                    pair = after(pair)
                start = (2 * pair + lax.bitwise_xor(lax.rem(blk, 2), int(side))) * rows
                panel[pl.ds(pl.multiple_of(start, rows), rows), :] = piece[...]


def position(table, tiles):
    count = tiles.shape[0] * tiles.shape[2]
    return table[count], table[count + 1]


def add_blocks(table, tiles, panel, out, owners):
    per_owner = out.shape[0] // (BLOCK * len(owners))
    for j, owner in enumerate(owners):
        for i in range(per_owner):
            g = owner * per_owner + i
            slots_here = range(tiles.shape[2])
            starts = [pl.multiple_of(table[g * tiles.shape[2] + k] * BLOCK, BLOCK) for k in slots_here]
            left = jnp.concatenate([tiles[g, 0, k] for k in slots_here], axis=1)
            right = jnp.concatenate([panel[pl.ds(start, BLOCK), :] for start in starts], axis=0)
            summed = jnp.dot(left, right, preferred_element_type=jnp.float32)
            out[pl.ds((j * per_owner + i) * BLOCK, BLOCK), :] = summed.astype(out.dtype)


def other_kernel(reps, table, tiles, *refs):
    pieces, panel, out = refs[:-2], refs[-2], refs[-1]
    blk, rep = position(table, tiles)
    place_pieces(panel, blk, rep, pieces)
    add_blocks(table, tiles, panel, out, [lax.bitwise_xor(rep, d) for d in range(1, reps, 2)])


def other_sums(pieces, adj_tiles, table):
    reps = lax.axis_size("rep")
    width = pieces[0].shape[1]
    rows = adj_tiles.shape[0] * BLOCK // reps
    length = lax.axis_size("blk") * rows
    return pl.pallas_call(
        functools.partial(other_kernel, reps),
        out_shape=[
            jax.ShapeDtypeStruct((length, width), jnp.bfloat16),
            jax.ShapeDtypeStruct((rows * (reps // 2), width), jnp.bfloat16),
        ],
        in_specs=[SMEM, VMEM] + [VMEM] * len(pieces),
        out_specs=[VMEM] * 2,
        compiler_params=pltpu.CompilerParams(vmem_limit_bytes=32 * 1024 * 1024),
        cost_estimate=product_cost(adj_tiles, width, reps),
        name="other_sums",
    )(table, adj_tiles, *pieces)


def sums_kernel(owners, table, tiles, panel, out):
    blk, rep = position(table, tiles)
    add_blocks(table, tiles, panel, out, [lax.bitwise_xor(rep, d) for d in owners])


def sums(panel, adj_tiles, table, owners, kind, name):
    reps = lax.axis_size("rep")
    rows, width = adj_tiles.shape[0] * BLOCK // reps * len(owners), panel.shape[1]
    return pl.pallas_call(
        functools.partial(sums_kernel, owners),
        out_shape=jax.ShapeDtypeStruct((rows, width), kind),
        in_specs=[SMEM, VMEM, VMEM],
        out_specs=VMEM,
        compiler_params=pltpu.CompilerParams(vmem_limit_bytes=32 * 1024 * 1024),
        cost_estimate=product_cost(adj_tiles, width, reps),
        name=name,
    )(table, adj_tiles, panel)


def product_cost(adj_tiles, width, reps):
    size = adj_tiles.size // reps
    return pl.CostEstimate(flops=2 * size * width, bytes_accessed=2 * size, transcendentals=0)


def add_cores_kernel(own, core, *outs):
    rows = outs[0].shape[0]
    for j, out in enumerate(outs):
        here, there = pl.ds(j * rows, rows), pl.ds((j + 1) * rows, rows)
        out[...] = (own[here, :] + core[there, :].astype(jnp.float32)).astype(jnp.bfloat16)


def add_cores(own, core, rows):
    width = own.shape[1]
    return pl.pallas_call(
        add_cores_kernel,
        out_shape=[jax.ShapeDtypeStruct((rows, width), jnp.bfloat16)] * (own.shape[0] // rows),
        in_specs=[VMEM] * 2,
        out_specs=[VMEM] * (own.shape[0] // rows),
        compiler_params=pltpu.CompilerParams(vmem_limit_bytes=32 * 1024 * 1024),
        name="add_cores",
    )(own, core)


def tile_products(pieces, adj_tiles, table, rows):
    reps = lax.axis_size("rep")
    panel, across = other_sums(pieces, adj_tiles, table)
    core = lax.ppermute(across, "rep", [(i, i ^ 1) for i in range(reps)])
    own = sums(panel, adj_tiles, table, range(2, reps, 2), jnp.float32, "own_far")
    parts = add_cores(own, core, rows)
    panel, parts = lax.optimization_barrier((panel, parts))
    near = sums(panel, adj_tiles, table, [0], jnp.float32, "own_near")
    terms = [near, core]
    for j, part in enumerate(parts, 1):
        terms.append(lax.ppermute(part, "rep", [(i, i ^ (2 * j)) for i in range(reps)]))
    return terms


def add_terms(terms, rows):
    total = terms[0][pl.ds(0, rows), :]
    for term in terms[1:]:
        total = total + term[pl.ds(0, rows), :].astype(jnp.float32)
    return total


def contract(a, b, dims):
    return lax.dot_general(a, b, ((dims[:1], dims[1:]), ((), ())), preferred_element_type=jnp.float32)


def early_kernel(cot, w_out, g_hidden):
    g_hidden[...] = contract(cot[...], w_out[...], (1, 1))


def early(cot_out, w_out):
    rows, width = cot_out.shape
    units = w_out.shape[0]
    return pl.pallas_call(
        early_kernel,
        out_shape=jax.ShapeDtypeStruct((rows, units), jnp.float32),
        in_specs=[VMEM] * 2,
        out_specs=VMEM,
        compiler_params=pltpu.CompilerParams(vmem_limit_bytes=32 * 1024 * 1024),
        cost_estimate=pl.CostEstimate(flops=BESIDE, bytes_accessed=8 * rows * units, transcendentals=0),
        name="early",
    )(cot_out, w_out)


def node_kernel(n_terms, *refs):
    terms = refs[:n_terms]
    g_hidden, w_in, b_in, g_out, hidden_out = refs[n_terms:]
    agg_b = add_terms(terms, g_out.shape[0]).astype(jnp.bfloat16)
    pre = contract(agg_b, w_in[...], (1, 0)) + b_in[...]
    sigma = 1.0 / (1.0 + jnp.exp(-pre))
    g_pre = (g_hidden[...] * sigma * (1.0 + pre * (1.0 - sigma))).astype(jnp.bfloat16)
    g_out[...] = contract(g_pre, w_in[...], (1, 1)).astype(jnp.bfloat16)
    hidden_out[...] = (pre * sigma).astype(jnp.bfloat16)


def node_update(terms, g_hidden, w_in, b_in):
    rows, units = g_hidden.shape
    width = w_in.shape[0]
    return pl.pallas_call(
        functools.partial(node_kernel, len(terms)),
        out_shape=[
            jax.ShapeDtypeStruct((rows, width), jnp.bfloat16),
            jax.ShapeDtypeStruct((rows, units), jnp.bfloat16),
        ],
        in_specs=[VMEM] * (len(terms) + 3),
        out_specs=[VMEM] * 2,
        compiler_params=pltpu.CompilerParams(vmem_limit_bytes=32 * 1024 * 1024),
        cost_estimate=pl.CostEstimate(
            flops=4 * rows * width * units, bytes_accessed=8 * rows * units, transcendentals=rows * units
        ),
        name="node_update",
    )(*terms, g_hidden, w_in, b_in.reshape(1, -1))


def project_kernel(hidden, feats, w_out, b_out, out):
    projected = contract(hidden[...], w_out[...], (1, 0)) + b_out[...]
    out[...] = (feats[...].astype(jnp.float32) + projected).astype(jnp.bfloat16)


def project(hidden, node_feats, w_out, b_out):
    rows, units = hidden.shape
    width = w_out.shape[1]
    return pl.pallas_call(
        project_kernel,
        out_shape=jax.ShapeDtypeStruct((rows, width), jnp.bfloat16),
        in_specs=[VMEM] * 4,
        out_specs=VMEM,
        compiler_params=pltpu.CompilerParams(vmem_limit_bytes=32 * 1024 * 1024),
        cost_estimate=pl.CostEstimate(
            flops=2 * rows * width * units, bytes_accessed=2 * rows * units, transcendentals=0
        ),
        name="project",
    )(hidden, node_feats, w_out, b_out.reshape(1, -1))


def close_kernel(n_terms, *refs):
    cot, out = refs[n_terms:]
    total = add_terms(refs[:n_terms], out.shape[0])
    out[...] = (cot[...].astype(jnp.float32) + total).astype(jnp.bfloat16)


def close_grad(terms, cot_out):
    return pl.pallas_call(
        functools.partial(close_kernel, len(terms)),
        out_shape=jax.ShapeDtypeStruct(cot_out.shape, jnp.bfloat16),
        in_specs=[VMEM] * (len(terms) + 1),
        out_specs=VMEM,
        compiler_params=pltpu.CompilerParams(vmem_limit_bytes=32 * 1024 * 1024),
        name="close_grad",
    )(*terms, cot_out)


def local(node_feats, adj_tiles, col_index, w_in, b_in, w_out, b_out, cot_out):
    where = jnp.stack([lax.axis_index("blk"), lax.axis_index("rep")]).astype(jnp.int32)
    table = jnp.concatenate([col_index.reshape(-1), where])
    g_hidden = early(cot_out, w_out)
    table, g_hidden = lax.optimization_barrier((table, g_hidden))
    panel = gather_blocks(node_feats)
    terms = tile_products(panel, adj_tiles, table, node_feats.shape[0])
    g_agg, hidden = node_update(terms, g_hidden, w_in, b_in)
    out_feats = project(hidden, node_feats, w_out, b_out)
    panel = gather_blocks(g_agg)
    terms = tile_products(panel, adj_tiles, table, node_feats.shape[0])
    return (out_feats, close_grad(terms, cot_out))


def solution(mesh):
    placed = (
        P(("blk", "rep"), None),
        P("blk", "rep", None, None, None),
        P("blk", "rep", None),
        P(),
        P(),
        P(),
        P(),
        P(("blk", "rep"), None),
    )
    return jax.shard_map(
        local,
        mesh=mesh,
        in_specs=placed,
        out_specs=(P(("blk", "rep"), None), P(("blk", "rep"), None)),
        check_vma=False,
    )
```

```python
import functools

import jax
import jax.numpy as jnp
from jax import lax
from jax.experimental import pallas as pl
from jax.experimental.pallas import tpu as pltpu
from jax.sharding import PartitionSpec as P

BLOCK = 128
VMEM = pl.BlockSpec(memory_space=pltpu.VMEM)
SMEM = pl.BlockSpec(memory_space=pltpu.SMEM)


BESIDE = 2 * 10**10
PAIRS = 4


def after(pair):
    return (3 * pair + 2) % (PAIRS + 1)


def before(pair):
    return (2 * pair + 1) % (PAIRS + 1)


def gather_blocks(rows):
    n = lax.axis_size("blk")
    if n != 2 * PAIRS:
        return [("all", lax.all_gather(rows, "blk", axis=0, tiled=True))]

    def beside(piece):
        return lax.ppermute(piece, "blk", [(i, i ^ 1) for i in range(n)])

    def step(piece, hop):
        return lax.ppermute(piece, "blk", [(i, 2 * hop(i // 2) + i % 2) for i in range(n)])

    first, second, own_beside = step(rows, after), step(rows, before), beside(rows)
    first_beside = beside(lax.optimization_barrier((first, own_beside))[0])
    third, third_beside = step(first, after), step(first_beside, after)
    second_beside = beside(second)
    return [
        ("own", rows),
        ("own beside", own_beside),
        ("second", second),
        ("second beside", second_beside),
        ("third", third),
        ("third beside", third_beside),
        ("first", first),
        ("first beside", first_beside),
    ]


def place_pieces(panel, blk, rows, names, pieces):
    got = dict(zip(names, pieces))
    if "all" in got:
        panel[...] = got["all"][...]
        return
    pair, side = blk // 2, lax.rem(blk, 2)
    came = {"own": pair, "first": before(pair), "second": after(pair), "third": before(before(pair))}
    for name, source in came.items():
        for which, other in ((name, 0), (name + " beside", 1)):
            start = (2 * source + lax.bitwise_xor(side, other)) * rows
            panel[pl.ds(pl.multiple_of(start, rows), rows), :] = got[which][...]


def add_blocks(columns, tiles, panel, out, owners):
    per_owner = out.shape[0] // (BLOCK * len(owners))
    for j, owner in enumerate(owners):
        for i in range(per_owner):
            g = owner * per_owner + i
            slots_here = range(tiles.shape[2])
            starts = [pl.multiple_of(columns[k, g] * BLOCK, BLOCK) for k in slots_here]
            left = jnp.concatenate([tiles[g, 0, k] for k in slots_here], axis=1)
            right = jnp.concatenate([panel[pl.ds(start, BLOCK), :] for start in starts], axis=0)
            summed = jnp.dot(left, right, preferred_element_type=jnp.float32)
            out[pl.ds((j * per_owner + i) * BLOCK, BLOCK), :] = summed.astype(out.dtype)


def other_kernel(names, reps, columns, tiles, *refs):
    pieces, panel, out = refs[: len(names)], refs[-2], refs[-1]
    blk, rep = lax.axis_index("blk"), lax.axis_index("rep")
    place_pieces(panel, blk, tiles.shape[0] * BLOCK // reps, names, pieces)
    add_blocks(columns, tiles, panel, out, [lax.bitwise_xor(rep, d) for d in range(1, reps, 2)])


def other_sums(gathered, adj_tiles, columns):
    reps = lax.axis_size("rep")
    names, pieces = zip(*gathered)
    width = pieces[0].shape[1]
    rows = adj_tiles.shape[0] * BLOCK // reps
    length = lax.axis_size("blk") * rows
    return pl.pallas_call(
        functools.partial(other_kernel, names, reps),
        out_shape=[
            jax.ShapeDtypeStruct((length, width), jnp.bfloat16),
            jax.ShapeDtypeStruct((rows * (reps // 2), width), jnp.bfloat16),
        ],
        in_specs=[SMEM, VMEM] + [VMEM] * len(pieces),
        out_specs=[VMEM] * 2,
        compiler_params=pltpu.CompilerParams(vmem_limit_bytes=32 * 1024 * 1024),
        cost_estimate=product_cost(adj_tiles, width, reps),
        name="other_sums",
    )(columns, adj_tiles, *pieces)


def sums_kernel(owners, columns, tiles, panel, out):
    rep = lax.axis_index("rep")
    add_blocks(columns, tiles, panel, out, [lax.bitwise_xor(rep, d) for d in owners])


def sums(panel, adj_tiles, columns, owners, kind, name):
    reps = lax.axis_size("rep")
    rows, width = adj_tiles.shape[0] * BLOCK // reps * len(owners), panel.shape[1]
    return pl.pallas_call(
        functools.partial(sums_kernel, owners),
        out_shape=jax.ShapeDtypeStruct((rows, width), kind),
        in_specs=[SMEM, VMEM, VMEM],
        out_specs=VMEM,
        compiler_params=pltpu.CompilerParams(vmem_limit_bytes=32 * 1024 * 1024),
        cost_estimate=product_cost(adj_tiles, width, reps),
        name=name,
    )(columns, adj_tiles, panel)


def product_cost(adj_tiles, width, reps):
    size = adj_tiles.size // reps
    return pl.CostEstimate(flops=2 * size * width, bytes_accessed=2 * size, transcendentals=0)


def add_cores_kernel(own, core, *outs):
    rows = outs[0].shape[0]
    for j, out in enumerate(outs):
        here, there = pl.ds(j * rows, rows), pl.ds((j + 1) * rows, rows)
        out[...] = (own[here, :] + core[there, :].astype(jnp.float32)).astype(jnp.bfloat16)


def add_cores(own, core, rows):
    width = own.shape[1]
    return pl.pallas_call(
        add_cores_kernel,
        out_shape=[jax.ShapeDtypeStruct((rows, width), jnp.bfloat16)] * (own.shape[0] // rows),
        in_specs=[VMEM] * 2,
        out_specs=[VMEM] * (own.shape[0] // rows),
        compiler_params=pltpu.CompilerParams(vmem_limit_bytes=32 * 1024 * 1024),
        name="add_cores",
    )(own, core)


def tile_products(pieces, adj_tiles, columns, rows):
    reps = lax.axis_size("rep")
    panel, across = other_sums(pieces, adj_tiles, columns)
    core = lax.ppermute(across, "rep", [(i, i ^ 1) for i in range(reps)])
    own = sums(panel, adj_tiles, columns, range(2, reps, 2), jnp.float32, "own_far")
    parts = add_cores(own, core, rows)
    panel, parts = lax.optimization_barrier((panel, parts))
    near = sums(panel, adj_tiles, columns, [0], jnp.float32, "own_near")
    terms = [near, core]
    for j, part in enumerate(parts, 1):
        terms.append(lax.ppermute(part, "rep", [(i, i ^ (2 * j)) for i in range(reps)]))
    return terms


def add_terms(terms, rows):
    total = terms[0][pl.ds(0, rows), :]
    for term in terms[1:]:
        total = total + term[pl.ds(0, rows), :].astype(jnp.float32)
    return total


def contract(a, b, dims):
    return lax.dot_general(a, b, ((dims[:1], dims[1:]), ((), ())), preferred_element_type=jnp.float32)


def early_kernel(cot, w_out, g_hidden):
    g_hidden[...] = contract(cot[...], w_out[...], (1, 1))


def early(cot_out, w_out):
    rows, width = cot_out.shape
    units = w_out.shape[0]
    return pl.pallas_call(
        early_kernel,
        out_shape=jax.ShapeDtypeStruct((rows, units), jnp.float32),
        in_specs=[VMEM] * 2,
        out_specs=VMEM,
        compiler_params=pltpu.CompilerParams(vmem_limit_bytes=32 * 1024 * 1024),
        cost_estimate=pl.CostEstimate(flops=BESIDE, bytes_accessed=8 * rows * units, transcendentals=0),
        name="early",
    )(cot_out, w_out)


def node_kernel(n_terms, *refs):
    terms = refs[:n_terms]
    g_hidden, w_in, b_in, g_out, hidden_out = refs[n_terms:]
    agg_b = add_terms(terms, g_out.shape[0]).astype(jnp.bfloat16)
    pre = contract(agg_b, w_in[...], (1, 0)) + b_in[...]
    sigma = 1.0 / (1.0 + jnp.exp(-pre))
    g_pre = (g_hidden[...] * sigma * (1.0 + pre * (1.0 - sigma))).astype(jnp.bfloat16)
    g_out[...] = contract(g_pre, w_in[...], (1, 1)).astype(jnp.bfloat16)
    hidden_out[...] = (pre * sigma).astype(jnp.bfloat16)


def node_update(terms, g_hidden, w_in, b_in):
    rows, units = g_hidden.shape
    width = w_in.shape[0]
    return pl.pallas_call(
        functools.partial(node_kernel, len(terms)),
        out_shape=[
            jax.ShapeDtypeStruct((rows, width), jnp.bfloat16),
            jax.ShapeDtypeStruct((rows, units), jnp.bfloat16),
        ],
        in_specs=[VMEM] * (len(terms) + 3),
        out_specs=[VMEM] * 2,
        compiler_params=pltpu.CompilerParams(vmem_limit_bytes=32 * 1024 * 1024),
        cost_estimate=pl.CostEstimate(
            flops=4 * rows * width * units, bytes_accessed=8 * rows * units, transcendentals=rows * units
        ),
        name="node_update",
    )(*terms, g_hidden, w_in, b_in.reshape(1, -1))


def project_kernel(hidden, feats, w_out, b_out, out):
    projected = contract(hidden[...], w_out[...], (1, 0)) + b_out[...]
    out[...] = (feats[...].astype(jnp.float32) + projected).astype(jnp.bfloat16)


def project(hidden, node_feats, w_out, b_out):
    rows, units = hidden.shape
    width = w_out.shape[1]
    return pl.pallas_call(
        project_kernel,
        out_shape=jax.ShapeDtypeStruct((rows, width), jnp.bfloat16),
        in_specs=[VMEM] * 4,
        out_specs=VMEM,
        compiler_params=pltpu.CompilerParams(vmem_limit_bytes=32 * 1024 * 1024),
        cost_estimate=pl.CostEstimate(
            flops=2 * rows * width * units, bytes_accessed=2 * rows * units, transcendentals=0
        ),
        name="project",
    )(hidden, node_feats, w_out, b_out.reshape(1, -1))


def close_kernel(n_terms, *refs):
    cot, out = refs[n_terms:]
    total = add_terms(refs[:n_terms], out.shape[0])
    out[...] = (cot[...].astype(jnp.float32) + total).astype(jnp.bfloat16)


def close_grad(terms, cot_out):
    return pl.pallas_call(
        functools.partial(close_kernel, len(terms)),
        out_shape=jax.ShapeDtypeStruct(cot_out.shape, jnp.bfloat16),
        in_specs=[VMEM] * (len(terms) + 1),
        out_specs=VMEM,
        compiler_params=pltpu.CompilerParams(vmem_limit_bytes=32 * 1024 * 1024),
        name="close_grad",
    )(*terms, cot_out)


def local(node_feats, adj_tiles, col_index, w_in, b_in, w_out, b_out, cot_out):
    columns = jnp.transpose(col_index, (1, 2, 0))[0]
    g_hidden = early(cot_out, w_out)
    columns, g_hidden = lax.optimization_barrier((columns, g_hidden))
    panel = gather_blocks(node_feats)
    terms = tile_products(panel, adj_tiles, columns, node_feats.shape[0])
    g_agg, hidden = node_update(terms, g_hidden, w_in, b_in)
    out_feats = project(hidden, node_feats, w_out, b_out)
    panel = gather_blocks(g_agg)
    terms = tile_products(panel, adj_tiles, columns, node_feats.shape[0])
    return (out_feats, close_grad(terms, cot_out))


def solution(mesh):
    placed = (
        P(("blk", "rep"), None),
        P("blk", "rep", None, None, None),
        P("blk", "rep", None),
        P(),
        P(),
        P(),
        P(),
        P(("blk", "rep"), None),
    )
    return jax.shard_map(
        local,
        mesh=mesh,
        in_specs=placed,
        out_specs=(P(("blk", "rep"), None), P(("blk", "rep"), None)),
        check_vma=False,
    )
```

```python
import functools

import jax
import jax.numpy as jnp
from jax import lax
from jax.experimental import pallas as pl
from jax.experimental.pallas import tpu as pltpu
from jax.sharding import PartitionSpec as P

BLOCK = 128
VMEM = pl.BlockSpec(memory_space=pltpu.VMEM)


BESIDE = 2 * 10**10
PAIRS = 4


def after(pair):
    return (3 * pair + 2) % (PAIRS + 1)


def before(pair):
    return (2 * pair + 1) % (PAIRS + 1)


def gather_blocks(rows):
    n = lax.axis_size("blk")
    if n != 2 * PAIRS:
        return [("all", lax.all_gather(rows, "blk", axis=0, tiled=True))]

    def beside(piece):
        return lax.ppermute(piece, "blk", [(i, i ^ 1) for i in range(n)])

    def step(piece, hop):
        return lax.ppermute(piece, "blk", [(i, 2 * hop(i // 2) + i % 2) for i in range(n)])

    first, second, own_beside = step(rows, after), step(rows, before), beside(rows)
    first_beside = beside(lax.optimization_barrier((first, own_beside))[0])
    third, third_beside = step(first, after), step(first_beside, after)
    second_beside = beside(second)
    return [
        ("own", rows),
        ("own beside", own_beside),
        ("second", second),
        ("second beside", second_beside),
        ("third", third),
        ("third beside", third_beside),
        ("first", first),
        ("first beside", first_beside),
    ]


def place_pieces(panel, blk, rows, names, pieces):
    got = dict(zip(names, pieces))
    if "all" in got:
        panel[...] = got["all"][...]
        return
    pair, side = blk // 2, lax.rem(blk, 2)
    came = {"own": pair, "first": before(pair), "second": after(pair), "third": before(before(pair))}
    for name, source in came.items():
        for which, other in ((name, 0), (name + " beside", 1)):
            start = (2 * source + lax.bitwise_xor(side, other)) * rows
            panel[pl.ds(pl.multiple_of(start, rows), rows), :] = got[which][...]


def add_blocks(columns, tiles, panel, out, owners):
    per_owner = out.shape[0] // (BLOCK * len(owners))
    slots_here = range(tiles.shape[2])
    for j, owner in enumerate(owners):
        numbers = columns[pl.ds(owner * per_owner, per_owner), :]
        for i in range(per_owner):
            starts = [pl.multiple_of(numbers[i, k] * BLOCK, BLOCK) for k in slots_here]
            left = jnp.concatenate([tiles[owner * per_owner + i, 0, k] for k in slots_here], axis=1)
            right = jnp.concatenate([panel[pl.ds(start, BLOCK), :] for start in starts], axis=0)
            summed = jnp.dot(left, right, preferred_element_type=jnp.float32)
            out[pl.ds((j * per_owner + i) * BLOCK, BLOCK), :] = summed.astype(out.dtype)


def other_kernel(names, reps, columns, tiles, *refs):
    pieces, panel, out = refs[: len(names)], refs[-2], refs[-1]
    blk, rep = lax.axis_index("blk"), lax.axis_index("rep")
    place_pieces(panel, blk, tiles.shape[0] * BLOCK // reps, names, pieces)
    add_blocks(columns, tiles, panel, out, [lax.bitwise_xor(rep, d) for d in range(1, reps, 2)])


def other_sums(gathered, adj_tiles, columns):
    reps = lax.axis_size("rep")
    names, pieces = zip(*gathered)
    width = pieces[0].shape[1]
    rows = adj_tiles.shape[0] * BLOCK // reps
    length = lax.axis_size("blk") * rows
    return pl.pallas_call(
        functools.partial(other_kernel, names, reps),
        out_shape=[
            jax.ShapeDtypeStruct((length, width), jnp.bfloat16),
            jax.ShapeDtypeStruct((rows * (reps // 2), width), jnp.bfloat16),
        ],
        in_specs=[VMEM, VMEM] + [VMEM] * len(pieces),
        out_specs=[VMEM] * 2,
        compiler_params=pltpu.CompilerParams(vmem_limit_bytes=32 * 1024 * 1024),
        cost_estimate=product_cost(adj_tiles, width, reps),
        name="other_sums",
    )(columns, adj_tiles, *pieces)


def sums_kernel(owners, columns, tiles, panel, out):
    rep = lax.axis_index("rep")
    add_blocks(columns, tiles, panel, out, [lax.bitwise_xor(rep, d) for d in owners])


def sums(panel, adj_tiles, columns, owners, kind, name):
    reps = lax.axis_size("rep")
    rows, width = adj_tiles.shape[0] * BLOCK // reps * len(owners), panel.shape[1]
    return pl.pallas_call(
        functools.partial(sums_kernel, owners),
        out_shape=jax.ShapeDtypeStruct((rows, width), kind),
        in_specs=[VMEM, VMEM, VMEM],
        out_specs=VMEM,
        compiler_params=pltpu.CompilerParams(vmem_limit_bytes=32 * 1024 * 1024),
        cost_estimate=product_cost(adj_tiles, width, reps),
        name=name,
    )(columns, adj_tiles, panel)


def product_cost(adj_tiles, width, reps):
    size = adj_tiles.size // reps
    return pl.CostEstimate(flops=2 * size * width, bytes_accessed=2 * size, transcendentals=0)


def add_cores_kernel(own, core, *outs):
    rows = outs[0].shape[0]
    for j, out in enumerate(outs):
        here, there = pl.ds(j * rows, rows), pl.ds((j + 1) * rows, rows)
        out[...] = (own[here, :] + core[there, :].astype(jnp.float32)).astype(jnp.bfloat16)


def add_cores(own, core, rows):
    width = own.shape[1]
    return pl.pallas_call(
        add_cores_kernel,
        out_shape=[jax.ShapeDtypeStruct((rows, width), jnp.bfloat16)] * (own.shape[0] // rows),
        in_specs=[VMEM] * 2,
        out_specs=[VMEM] * (own.shape[0] // rows),
        compiler_params=pltpu.CompilerParams(vmem_limit_bytes=32 * 1024 * 1024),
        name="add_cores",
    )(own, core)


def tile_products(pieces, adj_tiles, columns, rows):
    reps = lax.axis_size("rep")
    panel, across = other_sums(pieces, adj_tiles, columns)
    core = lax.ppermute(across, "rep", [(i, i ^ 1) for i in range(reps)])
    own = sums(panel, adj_tiles, columns, range(2, reps, 2), jnp.float32, "own_far")
    parts = add_cores(own, core, rows)
    panel, parts = lax.optimization_barrier((panel, parts))
    near = sums(panel, adj_tiles, columns, [0], jnp.float32, "own_near")
    terms = [near, core]
    for j, part in enumerate(parts, 1):
        terms.append(lax.ppermute(part, "rep", [(i, i ^ (2 * j)) for i in range(reps)]))
    return terms


def add_terms(terms, rows):
    total = terms[0][pl.ds(0, rows), :]
    for term in terms[1:]:
        total = total + term[pl.ds(0, rows), :].astype(jnp.float32)
    return total


def contract(a, b, dims):
    return lax.dot_general(a, b, ((dims[:1], dims[1:]), ((), ())), preferred_element_type=jnp.float32)


def early_kernel(cot, w_out, by_slot, g_hidden, columns):
    g_hidden[...] = contract(cot[...], w_out[...], (1, 1))
    columns[...] = jnp.transpose(by_slot[...])


def early(cot_out, w_out, by_slot):
    rows, width = cot_out.shape
    units = w_out.shape[0]
    return pl.pallas_call(
        early_kernel,
        out_shape=[
            jax.ShapeDtypeStruct((rows, units), jnp.float32),
            jax.ShapeDtypeStruct(by_slot.shape[::-1], jnp.int32),
        ],
        in_specs=[VMEM] * 3,
        out_specs=[VMEM] * 2,
        compiler_params=pltpu.CompilerParams(vmem_limit_bytes=32 * 1024 * 1024),
        cost_estimate=pl.CostEstimate(flops=BESIDE, bytes_accessed=8 * rows * units, transcendentals=0),
        name="early",
    )(cot_out, w_out, by_slot)


def node_pre(terms, rows, w_in, b_in):
    agg_b = add_terms(terms, rows).astype(jnp.bfloat16)
    pre = contract(agg_b, w_in[...], (1, 0)) + b_in[...]
    return pre, 1.0 / (1.0 + jnp.exp(-pre))


def node_kernel(n_terms, *refs):
    terms = refs[:n_terms]
    g_hidden, w_in, b_in, g_out = refs[n_terms:]
    pre, sigma = node_pre(terms, g_out.shape[0], w_in, b_in)
    g_pre = (g_hidden[...] * sigma * (1.0 + pre * (1.0 - sigma))).astype(jnp.bfloat16)
    g_out[...] = contract(g_pre, w_in[...], (1, 1)).astype(jnp.bfloat16)


def node_update(terms, g_hidden, w_in, b_in):
    rows, units = g_hidden.shape
    width = w_in.shape[0]
    return pl.pallas_call(
        functools.partial(node_kernel, len(terms)),
        out_shape=jax.ShapeDtypeStruct((rows, width), jnp.bfloat16),
        in_specs=[VMEM] * (len(terms) + 3),
        out_specs=VMEM,
        compiler_params=pltpu.CompilerParams(vmem_limit_bytes=32 * 1024 * 1024),
        cost_estimate=pl.CostEstimate(
            flops=4 * rows * width * units, bytes_accessed=8 * rows * units, transcendentals=rows * units
        ),
        name="node_update",
    )(*terms, g_hidden, w_in, b_in.reshape(1, -1))


def project_kernel(n_terms, *refs):
    terms = refs[:n_terms]
    feats, w_in, b_in, w_out, b_out, out = refs[n_terms:]
    pre, sigma = node_pre(terms, out.shape[0], w_in, b_in)
    projected = contract((pre * sigma).astype(jnp.bfloat16), w_out[...], (1, 0)) + b_out[...]
    out[...] = (feats[...].astype(jnp.float32) + projected).astype(jnp.bfloat16)


def project(terms, node_feats, w_in, b_in, w_out, b_out):
    rows, width = node_feats.shape
    units = w_in.shape[1]
    return pl.pallas_call(
        functools.partial(project_kernel, len(terms)),
        out_shape=jax.ShapeDtypeStruct((rows, width), jnp.bfloat16),
        in_specs=[VMEM] * (len(terms) + 5),
        out_specs=VMEM,
        compiler_params=pltpu.CompilerParams(vmem_limit_bytes=32 * 1024 * 1024),
        cost_estimate=pl.CostEstimate(
            flops=4 * rows * width * units, bytes_accessed=2 * rows * units, transcendentals=rows * units
        ),
        name="project",
    )(*terms, node_feats, w_in, b_in.reshape(1, -1), w_out, b_out.reshape(1, -1))


def close_kernel(n_terms, *refs):
    cot, out = refs[n_terms:]
    total = add_terms(refs[:n_terms], out.shape[0])
    out[...] = (cot[...].astype(jnp.float32) + total).astype(jnp.bfloat16)


def close_grad(terms, cot_out):
    return pl.pallas_call(
        functools.partial(close_kernel, len(terms)),
        out_shape=jax.ShapeDtypeStruct(cot_out.shape, jnp.bfloat16),
        in_specs=[VMEM] * (len(terms) + 1),
        out_specs=VMEM,
        compiler_params=pltpu.CompilerParams(vmem_limit_bytes=32 * 1024 * 1024),
        name="close_grad",
    )(*terms, cot_out)


def local(node_feats, adj_tiles, col_index, w_in, b_in, w_out, b_out, cot_out):
    rows = node_feats.shape[0]
    g_hidden, columns = early(cot_out, w_out, jnp.transpose(col_index, (1, 2, 0))[0])
    terms = tile_products(gather_blocks(node_feats), adj_tiles, columns, rows)
    g_agg = node_update(terms, g_hidden, w_in, b_in)
    out_feats = project(terms, node_feats, w_in, b_in, w_out, b_out)
    terms = tile_products(gather_blocks(g_agg), adj_tiles, columns, rows)
    return (out_feats, close_grad(terms, cot_out))


def solution(mesh):
    placed = (
        P(("blk", "rep"), None),
        P("blk", "rep", None, None, None),
        P("blk", "rep", None),
        P(),
        P(),
        P(),
        P(),
        P(("blk", "rep"), None),
    )
    return jax.shard_map(
        local,
        mesh=mesh,
        in_specs=placed,
        out_specs=(P(("blk", "rep"), None), P(("blk", "rep"), None)),
        check_vma=False,
    )
```

```python
import functools

import jax
import jax.numpy as jnp
from jax import lax
from jax.experimental import pallas as pl
from jax.experimental.pallas import tpu as pltpu
from jax.sharding import PartitionSpec as P

BLOCK = 128
VMEM = pl.BlockSpec(memory_space=pltpu.VMEM)


BESIDE = 2 * 10**10
PAIRS = 4


def after(pair):
    return (3 * pair + 2) % (PAIRS + 1)


def before(pair):
    return (2 * pair + 1) % (PAIRS + 1)


def gather_blocks(rows):
    n = lax.axis_size("blk")
    if n != 2 * PAIRS:
        return [("all", lax.all_gather(rows, "blk", axis=0, tiled=True))]

    def beside(piece):
        return lax.ppermute(piece, "blk", [(i, i ^ 1) for i in range(n)])

    def step(piece, hop):
        return lax.ppermute(piece, "blk", [(i, 2 * hop(i // 2) + i % 2) for i in range(n)])

    first, second, own_beside = step(rows, after), step(rows, before), beside(rows)
    first_beside = beside(lax.optimization_barrier((first, own_beside))[0])
    third, third_beside = step(first, after), step(first_beside, after)
    second_beside = beside(second)
    return [
        ("own", rows),
        ("own beside", own_beside),
        ("second", second),
        ("second beside", second_beside),
        ("third", third),
        ("third beside", third_beside),
        ("first", first),
        ("first beside", first_beside),
    ]


def place_pieces(panel, blk, rows, names, pieces):
    got = dict(zip(names, pieces))
    if "all" in got:
        panel[...] = got["all"][...]
        return
    pair, side = blk // 2, lax.rem(blk, 2)
    came = {"own": pair, "first": before(pair), "second": after(pair), "third": before(before(pair))}
    for name, source in came.items():
        for which, other in ((name, 0), (name + " beside", 1)):
            start = (2 * source + lax.bitwise_xor(side, other)) * rows
            panel[pl.ds(pl.multiple_of(start, rows), rows), :] = got[which][...]


def add_blocks(columns, tiles, panel, out, owners):
    per_owner = out.shape[0] // (BLOCK * len(owners))
    slots_here = range(tiles.shape[2])
    for j, owner in enumerate(owners):
        numbers = columns[pl.ds(owner * per_owner, per_owner), :]
        for i in range(per_owner):
            starts = [pl.multiple_of(numbers[i, k] * BLOCK, BLOCK) for k in slots_here]
            left = jnp.concatenate([tiles[owner * per_owner + i, 0, k] for k in slots_here], axis=1)
            right = jnp.concatenate([panel[pl.ds(start, BLOCK), :] for start in starts], axis=0)
            summed = jnp.dot(left, right, preferred_element_type=jnp.float32)
            out[pl.ds((j * per_owner + i) * BLOCK, BLOCK), :] = summed.astype(out.dtype)


def other_kernel(names, reps, columns, tiles, *refs):
    pieces, panel, out = refs[: len(names)], refs[-2], refs[-1]
    blk, rep = lax.axis_index("blk"), lax.axis_index("rep")
    place_pieces(panel, blk, tiles.shape[0] * BLOCK // reps, names, pieces)
    add_blocks(columns, tiles, panel, out, [lax.bitwise_xor(rep, d) for d in range(1, reps, 2)])


def other_sums(gathered, adj_tiles, columns):
    reps = lax.axis_size("rep")
    names, pieces = zip(*gathered)
    width = pieces[0].shape[1]
    rows = adj_tiles.shape[0] * BLOCK // reps
    length = lax.axis_size("blk") * rows
    return pl.pallas_call(
        functools.partial(other_kernel, names, reps),
        out_shape=[
            jax.ShapeDtypeStruct((length, width), jnp.bfloat16),
            jax.ShapeDtypeStruct((rows * (reps // 2), width), jnp.bfloat16),
        ],
        in_specs=[VMEM, VMEM] + [VMEM] * len(pieces),
        out_specs=[VMEM] * 2,
        compiler_params=pltpu.CompilerParams(vmem_limit_bytes=32 * 1024 * 1024),
        cost_estimate=product_cost(adj_tiles, width, reps),
        name="other_sums",
    )(columns, adj_tiles, *pieces)


def sums_kernel(owners, columns, tiles, panel, out):
    rep = lax.axis_index("rep")
    add_blocks(columns, tiles, panel, out, [lax.bitwise_xor(rep, d) for d in owners])


def sums(panel, adj_tiles, columns, owners, kind, name):
    reps = lax.axis_size("rep")
    rows, width = adj_tiles.shape[0] * BLOCK // reps * len(owners), panel.shape[1]
    return pl.pallas_call(
        functools.partial(sums_kernel, owners),
        out_shape=jax.ShapeDtypeStruct((rows, width), kind),
        in_specs=[VMEM, VMEM, VMEM],
        out_specs=VMEM,
        compiler_params=pltpu.CompilerParams(vmem_limit_bytes=32 * 1024 * 1024),
        cost_estimate=product_cost(adj_tiles, width, reps),
        name=name,
    )(columns, adj_tiles, panel)


def product_cost(adj_tiles, width, reps):
    size = adj_tiles.size // reps
    return pl.CostEstimate(flops=2 * size * width, bytes_accessed=2 * size, transcendentals=0)


def add_cores_kernel(own, core, *outs):
    rows = outs[0].shape[0]
    for j, out in enumerate(outs):
        here, there = pl.ds(j * rows, rows), pl.ds((j + 1) * rows, rows)
        out[...] = (own[here, :] + core[there, :].astype(jnp.float32)).astype(jnp.bfloat16)


def add_cores(own, core, rows):
    width = own.shape[1]
    return pl.pallas_call(
        add_cores_kernel,
        out_shape=[jax.ShapeDtypeStruct((rows, width), jnp.bfloat16)] * (own.shape[0] // rows),
        in_specs=[VMEM] * 2,
        out_specs=[VMEM] * (own.shape[0] // rows),
        compiler_params=pltpu.CompilerParams(vmem_limit_bytes=32 * 1024 * 1024),
        name="add_cores",
    )(own, core)


def tile_products(pieces, adj_tiles, columns, rows):
    reps = lax.axis_size("rep")
    panel, across = other_sums(pieces, adj_tiles, columns)
    core = lax.ppermute(across, "rep", [(i, i ^ 1) for i in range(reps)])
    own = sums(panel, adj_tiles, columns, range(2, reps, 2), jnp.float32, "own_far")
    parts = add_cores(own, core, rows)
    panel, parts = lax.optimization_barrier((panel, parts))
    near = sums(panel, adj_tiles, columns, [0], jnp.float32, "own_near")
    terms = [near, core]
    for j, part in enumerate(parts, 1):
        terms.append(lax.ppermute(part, "rep", [(i, i ^ (2 * j)) for i in range(reps)]))
    return terms


def add_terms(terms, rows):
    total = terms[0][pl.ds(0, rows), :]
    for term in terms[1:]:
        total = total + term[pl.ds(0, rows), :].astype(jnp.float32)
    return total


def contract(a, b, dims):
    return lax.dot_general(a, b, ((dims[:1], dims[1:]), ((), ())), preferred_element_type=jnp.float32)


def by_row_kernel(by_slot, columns):
    columns[...] = jnp.transpose(by_slot[...])


def by_row(by_slot):
    return pl.pallas_call(
        by_row_kernel,
        out_shape=jax.ShapeDtypeStruct(by_slot.shape[::-1], jnp.int32),
        in_specs=[VMEM],
        out_specs=VMEM,
        compiler_params=pltpu.CompilerParams(vmem_limit_bytes=32 * 1024 * 1024),
        cost_estimate=pl.CostEstimate(flops=BESIDE, bytes_accessed=by_slot.size, transcendentals=0),
        name="by_row",
    )(by_slot)


def early_kernel(cot, w_out, g_hidden):
    g_hidden[...] = contract(cot[...], w_out[...], (1, 1))


def early(cot_out, w_out):
    rows, width = cot_out.shape
    units = w_out.shape[0]
    return pl.pallas_call(
        early_kernel,
        out_shape=jax.ShapeDtypeStruct((rows, units), jnp.float32),
        in_specs=[VMEM] * 2,
        out_specs=VMEM,
        compiler_params=pltpu.CompilerParams(vmem_limit_bytes=32 * 1024 * 1024),
        cost_estimate=pl.CostEstimate(
            flops=2 * rows * width * units, bytes_accessed=8 * rows * units, transcendentals=0
        ),
        name="early",
    )(cot_out, w_out)


def node_pre(terms, rows, w_in, b_in):
    agg_b = add_terms(terms, rows).astype(jnp.bfloat16)
    pre = contract(agg_b, w_in[...], (1, 0)) + b_in[...]
    return pre, 1.0 / (1.0 + jnp.exp(-pre))


def node_kernel(n_terms, *refs):
    terms = refs[:n_terms]
    g_hidden, w_in, b_in, g_out = refs[n_terms:]
    pre, sigma = node_pre(terms, g_out.shape[0], w_in, b_in)
    g_pre = (g_hidden[...] * sigma * (1.0 + pre * (1.0 - sigma))).astype(jnp.bfloat16)
    g_out[...] = contract(g_pre, w_in[...], (1, 1)).astype(jnp.bfloat16)


def node_update(terms, g_hidden, w_in, b_in):
    rows, units = g_hidden.shape
    width = w_in.shape[0]
    return pl.pallas_call(
        functools.partial(node_kernel, len(terms)),
        out_shape=jax.ShapeDtypeStruct((rows, width), jnp.bfloat16),
        in_specs=[VMEM] * (len(terms) + 3),
        out_specs=VMEM,
        compiler_params=pltpu.CompilerParams(vmem_limit_bytes=32 * 1024 * 1024),
        cost_estimate=pl.CostEstimate(
            flops=4 * rows * width * units, bytes_accessed=8 * rows * units, transcendentals=rows * units
        ),
        name="node_update",
    )(*terms, g_hidden, w_in, b_in.reshape(1, -1))


def project_kernel(n_terms, *refs):
    terms = refs[:n_terms]
    feats, w_in, b_in, w_out, b_out, out = refs[n_terms:]
    pre, sigma = node_pre(terms, out.shape[0], w_in, b_in)
    projected = contract((pre * sigma).astype(jnp.bfloat16), w_out[...], (1, 0)) + b_out[...]
    out[...] = (feats[...].astype(jnp.float32) + projected).astype(jnp.bfloat16)


def project(terms, node_feats, w_in, b_in, w_out, b_out):
    rows, width = node_feats.shape
    units = w_in.shape[1]
    return pl.pallas_call(
        functools.partial(project_kernel, len(terms)),
        out_shape=jax.ShapeDtypeStruct((rows, width), jnp.bfloat16),
        in_specs=[VMEM] * (len(terms) + 5),
        out_specs=VMEM,
        compiler_params=pltpu.CompilerParams(vmem_limit_bytes=32 * 1024 * 1024),
        cost_estimate=pl.CostEstimate(
            flops=4 * rows * width * units, bytes_accessed=2 * rows * units, transcendentals=rows * units
        ),
        name="project",
    )(*terms, node_feats, w_in, b_in.reshape(1, -1), w_out, b_out.reshape(1, -1))


def close_kernel(n_terms, *refs):
    cot, out = refs[n_terms:]
    total = add_terms(refs[:n_terms], out.shape[0])
    out[...] = (cot[...].astype(jnp.float32) + total).astype(jnp.bfloat16)


def close_grad(terms, cot_out):
    return pl.pallas_call(
        functools.partial(close_kernel, len(terms)),
        out_shape=jax.ShapeDtypeStruct(cot_out.shape, jnp.bfloat16),
        in_specs=[VMEM] * (len(terms) + 1),
        out_specs=VMEM,
        compiler_params=pltpu.CompilerParams(vmem_limit_bytes=32 * 1024 * 1024),
        name="close_grad",
    )(*terms, cot_out)


def local(node_feats, adj_tiles, col_index, w_in, b_in, w_out, b_out, cot_out):
    rows = node_feats.shape[0]
    columns = by_row(jnp.transpose(col_index, (1, 2, 0))[0])
    g_hidden = early(cot_out, lax.optimization_barrier((w_out, columns))[0])
    columns, g_hidden = lax.optimization_barrier((columns, g_hidden))
    terms = tile_products(gather_blocks(node_feats), adj_tiles, columns, rows)
    g_agg = node_update(terms, g_hidden, w_in, b_in)
    out_feats = project(terms, node_feats, w_in, b_in, w_out, b_out)
    terms = tile_products(gather_blocks(g_agg), adj_tiles, columns, rows)
    return (out_feats, close_grad(terms, cot_out))


def solution(mesh):
    placed = (
        P(("blk", "rep"), None),
        P("blk", "rep", None, None, None),
        P("blk", "rep", None),
        P(),
        P(),
        P(),
        P(),
        P(("blk", "rep"), None),
    )
    return jax.shard_map(
        local,
        mesh=mesh,
        in_specs=placed,
        out_specs=(P(("blk", "rep"), None), P(("blk", "rep"), None)),
        check_vma=False,
    )
```

```python
import functools

import jax
import jax.numpy as jnp
from jax import lax
from jax.experimental import pallas as pl
from jax.experimental.pallas import tpu as pltpu
from jax.sharding import PartitionSpec as P

BLOCK = 128
VMEM = pl.BlockSpec(memory_space=pltpu.VMEM)


BESIDE = 2 * 10**10
PAIRS = 4


def after(pair):
    return (3 * pair + 2) % (PAIRS + 1)


def before(pair):
    return (2 * pair + 1) % (PAIRS + 1)


def gather_blocks(rows):
    n = lax.axis_size("blk")
    if n != 2 * PAIRS:
        return [("all", lax.all_gather(rows, "blk", axis=0, tiled=True))]

    def beside(piece):
        return lax.ppermute(piece, "blk", [(i, i ^ 1) for i in range(n)])

    def step(piece, hop):
        return lax.ppermute(piece, "blk", [(i, 2 * hop(i // 2) + i % 2) for i in range(n)])

    def ordered(piece, earlier):
        return lax.optimization_barrier((piece, earlier))[0]

    first, second, own_beside = step(rows, after), step(rows, before), beside(rows)
    first_beside = beside(first)
    third, third_beside = step(ordered(first, own_beside), after), step(first_beside, after)
    second_beside = beside(ordered(second, first_beside))
    return [
        ("own", rows),
        ("own beside", own_beside),
        ("second", second),
        ("second beside", second_beside),
        ("third", third),
        ("third beside", third_beside),
        ("first", first),
        ("first beside", first_beside),
    ]


def place_pieces(panel, blk, rows, names, pieces):
    got = dict(zip(names, pieces))
    if "all" in got:
        panel[...] = got["all"][...]
        return
    pair, side = blk // 2, lax.rem(blk, 2)
    came = {"own": pair, "first": before(pair), "second": after(pair), "third": before(before(pair))}
    for name, source in came.items():
        for which, other in ((name, 0), (name + " beside", 1)):
            start = (2 * source + lax.bitwise_xor(side, other)) * rows
            panel[pl.ds(pl.multiple_of(start, rows), rows), :] = got[which][...]


def add_blocks(columns, tiles, panel, out, owners):
    per_owner = out.shape[0] // (BLOCK * len(owners))
    slots_here = range(tiles.shape[2])
    for j, owner in enumerate(owners):
        numbers = columns[pl.ds(owner * per_owner, per_owner), :]
        for i in range(per_owner):
            starts = [pl.multiple_of(numbers[i, k] * BLOCK, BLOCK) for k in slots_here]
            left = jnp.concatenate([tiles[owner * per_owner + i, 0, k] for k in slots_here], axis=1)
            right = jnp.concatenate([panel[pl.ds(start, BLOCK), :] for start in starts], axis=0)
            summed = jnp.dot(left, right, preferred_element_type=jnp.float32)
            out[pl.ds((j * per_owner + i) * BLOCK, BLOCK), :] = summed.astype(out.dtype)


def other_kernel(names, reps, columns, tiles, *refs):
    pieces, panel, out = refs[: len(names)], refs[-2], refs[-1]
    blk, rep = lax.axis_index("blk"), lax.axis_index("rep")
    place_pieces(panel, blk, tiles.shape[0] * BLOCK // reps, names, pieces)
    add_blocks(columns, tiles, panel, out, [lax.bitwise_xor(rep, d) for d in range(1, reps, 2)])


def other_sums(gathered, adj_tiles, columns):
    reps = lax.axis_size("rep")
    names, pieces = zip(*gathered)
    width = pieces[0].shape[1]
    rows = adj_tiles.shape[0] * BLOCK // reps
    length = lax.axis_size("blk") * rows
    return pl.pallas_call(
        functools.partial(other_kernel, names, reps),
        out_shape=[
            jax.ShapeDtypeStruct((length, width), jnp.bfloat16),
            jax.ShapeDtypeStruct((rows * (reps // 2), width), jnp.bfloat16),
        ],
        in_specs=[VMEM, VMEM] + [VMEM] * len(pieces),
        out_specs=[VMEM] * 2,
        compiler_params=pltpu.CompilerParams(vmem_limit_bytes=32 * 1024 * 1024),
        cost_estimate=product_cost(adj_tiles, width, reps),
        name="other_sums",
    )(columns, adj_tiles, *pieces)


def sums_kernel(owners, columns, tiles, panel, out):
    rep = lax.axis_index("rep")
    add_blocks(columns, tiles, panel, out, [lax.bitwise_xor(rep, d) for d in owners])


def sums(panel, adj_tiles, columns, owners, kind, name):
    reps = lax.axis_size("rep")
    rows, width = adj_tiles.shape[0] * BLOCK // reps * len(owners), panel.shape[1]
    return pl.pallas_call(
        functools.partial(sums_kernel, owners),
        out_shape=jax.ShapeDtypeStruct((rows, width), kind),
        in_specs=[VMEM, VMEM, VMEM],
        out_specs=VMEM,
        compiler_params=pltpu.CompilerParams(vmem_limit_bytes=32 * 1024 * 1024),
        cost_estimate=product_cost(adj_tiles, width, reps),
        name=name,
    )(columns, adj_tiles, panel)


def product_cost(adj_tiles, width, reps):
    size = adj_tiles.size // reps
    return pl.CostEstimate(flops=2 * size * width, bytes_accessed=2 * size, transcendentals=0)


def add_cores_kernel(own, core, *outs):
    rows = outs[0].shape[0]
    for j, out in enumerate(outs):
        here, there = pl.ds(j * rows, rows), pl.ds((j + 1) * rows, rows)
        out[...] = (own[here, :] + core[there, :].astype(jnp.float32)).astype(jnp.bfloat16)


def add_cores(own, core, rows):
    width = own.shape[1]
    return pl.pallas_call(
        add_cores_kernel,
        out_shape=[jax.ShapeDtypeStruct((rows, width), jnp.bfloat16)] * (own.shape[0] // rows),
        in_specs=[VMEM] * 2,
        out_specs=[VMEM] * (own.shape[0] // rows),
        compiler_params=pltpu.CompilerParams(vmem_limit_bytes=32 * 1024 * 1024),
        name="add_cores",
    )(own, core)


def tile_products(pieces, adj_tiles, columns, rows):
    reps = lax.axis_size("rep")
    panel, across = other_sums(pieces, adj_tiles, columns)
    core = lax.ppermute(across, "rep", [(i, i ^ 1) for i in range(reps)])
    own = sums(panel, adj_tiles, columns, range(2, reps, 2), jnp.float32, "own_far")
    parts = add_cores(own, core, rows)
    panel, parts = lax.optimization_barrier((panel, parts))
    near = sums(panel, adj_tiles, columns, [0], jnp.float32, "own_near")
    terms = [near, core]
    for j, part in enumerate(parts, 1):
        terms.append(lax.ppermute(part, "rep", [(i, i ^ (2 * j)) for i in range(reps)]))
    return terms


def add_terms(terms, rows):
    total = terms[0][pl.ds(0, rows), :]
    for term in terms[1:]:
        total = total + term[pl.ds(0, rows), :].astype(jnp.float32)
    return total


def contract(a, b, dims):
    return lax.dot_general(a, b, ((dims[:1], dims[1:]), ((), ())), preferred_element_type=jnp.float32)


def by_row_kernel(by_slot, columns):
    columns[...] = jnp.transpose(by_slot[...])


def by_row(by_slot):
    return pl.pallas_call(
        by_row_kernel,
        out_shape=jax.ShapeDtypeStruct(by_slot.shape[::-1], jnp.int32),
        in_specs=[VMEM],
        out_specs=VMEM,
        compiler_params=pltpu.CompilerParams(vmem_limit_bytes=32 * 1024 * 1024),
        cost_estimate=pl.CostEstimate(flops=BESIDE, bytes_accessed=by_slot.size, transcendentals=0),
        name="by_row",
    )(by_slot)


def early_kernel(cot, w_out, g_hidden):
    g_hidden[...] = contract(cot[...], w_out[...], (1, 1))


def early(cot_out, w_out):
    rows, width = cot_out.shape
    units = w_out.shape[0]
    return pl.pallas_call(
        early_kernel,
        out_shape=jax.ShapeDtypeStruct((rows, units), jnp.float32),
        in_specs=[VMEM] * 2,
        out_specs=VMEM,
        compiler_params=pltpu.CompilerParams(vmem_limit_bytes=32 * 1024 * 1024),
        cost_estimate=pl.CostEstimate(
            flops=2 * rows * width * units, bytes_accessed=8 * rows * units, transcendentals=0
        ),
        name="early",
    )(cot_out, w_out)


def node_pre(terms, rows, w_in, b_in):
    agg_b = add_terms(terms, rows).astype(jnp.bfloat16)
    pre = contract(agg_b, w_in[...], (1, 0)) + b_in[...]
    return pre, 1.0 / (1.0 + jnp.exp(-pre))


def node_kernel(n_terms, *refs):
    terms = refs[:n_terms]
    g_hidden, w_in, b_in, g_out = refs[n_terms:]
    pre, sigma = node_pre(terms, g_out.shape[0], w_in, b_in)
    g_pre = (g_hidden[...] * sigma * (1.0 + pre * (1.0 - sigma))).astype(jnp.bfloat16)
    g_out[...] = contract(g_pre, w_in[...], (1, 1)).astype(jnp.bfloat16)


def node_update(terms, g_hidden, w_in, b_in):
    rows, units = g_hidden.shape
    width = w_in.shape[0]
    return pl.pallas_call(
        functools.partial(node_kernel, len(terms)),
        out_shape=jax.ShapeDtypeStruct((rows, width), jnp.bfloat16),
        in_specs=[VMEM] * (len(terms) + 3),
        out_specs=VMEM,
        compiler_params=pltpu.CompilerParams(vmem_limit_bytes=32 * 1024 * 1024),
        cost_estimate=pl.CostEstimate(
            flops=4 * rows * width * units, bytes_accessed=8 * rows * units, transcendentals=rows * units
        ),
        name="node_update",
    )(*terms, g_hidden, w_in, b_in.reshape(1, -1))


def project_kernel(n_terms, *refs):
    terms = refs[:n_terms]
    feats, w_in, b_in, w_out, b_out, out = refs[n_terms:]
    pre, sigma = node_pre(terms, out.shape[0], w_in, b_in)
    projected = contract((pre * sigma).astype(jnp.bfloat16), w_out[...], (1, 0)) + b_out[...]
    out[...] = (feats[...].astype(jnp.float32) + projected).astype(jnp.bfloat16)


def project(terms, node_feats, w_in, b_in, w_out, b_out):
    rows, width = node_feats.shape
    units = w_in.shape[1]
    return pl.pallas_call(
        functools.partial(project_kernel, len(terms)),
        out_shape=jax.ShapeDtypeStruct((rows, width), jnp.bfloat16),
        in_specs=[VMEM] * (len(terms) + 5),
        out_specs=VMEM,
        compiler_params=pltpu.CompilerParams(vmem_limit_bytes=32 * 1024 * 1024),
        cost_estimate=pl.CostEstimate(
            flops=4 * rows * width * units, bytes_accessed=2 * rows * units, transcendentals=rows * units
        ),
        name="project",
    )(*terms, node_feats, w_in, b_in.reshape(1, -1), w_out, b_out.reshape(1, -1))


def close_kernel(n_terms, *refs):
    cot, out = refs[n_terms:]
    total = add_terms(refs[:n_terms], out.shape[0])
    out[...] = (cot[...].astype(jnp.float32) + total).astype(jnp.bfloat16)


def close_grad(terms, cot_out):
    return pl.pallas_call(
        functools.partial(close_kernel, len(terms)),
        out_shape=jax.ShapeDtypeStruct(cot_out.shape, jnp.bfloat16),
        in_specs=[VMEM] * (len(terms) + 1),
        out_specs=VMEM,
        compiler_params=pltpu.CompilerParams(vmem_limit_bytes=32 * 1024 * 1024),
        name="close_grad",
    )(*terms, cot_out)


def local(node_feats, adj_tiles, col_index, w_in, b_in, w_out, b_out, cot_out):
    rows = node_feats.shape[0]
    columns = by_row(jnp.transpose(col_index, (1, 2, 0))[0])
    g_hidden = early(cot_out, lax.optimization_barrier((w_out, columns))[0])
    columns, g_hidden = lax.optimization_barrier((columns, g_hidden))
    terms = tile_products(gather_blocks(node_feats), adj_tiles, columns, rows)
    g_agg = node_update(terms, g_hidden, w_in, b_in)
    out_feats = project(terms, node_feats, w_in, b_in, w_out, b_out)
    terms = tile_products(gather_blocks(g_agg), adj_tiles, columns, rows)
    return (out_feats, close_grad(terms, cot_out))


def solution(mesh):
    placed = (
        P(("blk", "rep"), None),
        P("blk", "rep", None, None, None),
        P("blk", "rep", None),
        P(),
        P(),
        P(),
        P(),
        P(("blk", "rep"), None),
    )
    return jax.shard_map(
        local,
        mesh=mesh,
        in_specs=placed,
        out_specs=(P(("blk", "rep"), None), P(("blk", "rep"), None)),
        check_vma=False,
    )
```

```python
import functools

import jax
import jax.numpy as jnp
from jax import lax
from jax.experimental import pallas as pl
from jax.experimental.pallas import tpu as pltpu
from jax.sharding import PartitionSpec as P

BLOCK = 128
VMEM = pl.BlockSpec(memory_space=pltpu.VMEM)


BESIDE = 2 * 10**10
PAIRS = 4


def after(pair):
    return (3 * pair + 2) % (PAIRS + 1)


def before(pair):
    return (2 * pair + 1) % (PAIRS + 1)


def gather_blocks(rows):
    n = lax.axis_size("blk")
    if n != 2 * PAIRS:
        return [("all", lax.all_gather(rows, "blk", axis=0, tiled=True))]

    def beside(piece):
        return lax.ppermute(piece, "blk", [(i, i ^ 1) for i in range(n)])

    def step(piece, hop):
        return lax.ppermute(piece, "blk", [(i, 2 * hop(i // 2) + i % 2) for i in range(n)])

    first, second, own_beside = step(rows, after), step(rows, before), beside(rows)
    first_beside = beside(lax.optimization_barrier((first, own_beside))[0])
    third, third_beside = step(first, after), step(first_beside, after)
    second_beside = beside(second)
    return [
        ("own", rows),
        ("own beside", own_beside),
        ("second", second),
        ("second beside", second_beside),
        ("third", third),
        ("third beside", third_beside),
        ("first", first),
        ("first beside", first_beside),
    ]


def place_pieces(panel, blk, rows, names, pieces):
    got = dict(zip(names, pieces))
    if "all" in got:
        panel[...] = got["all"][...]
        return
    pair, side = blk // 2, lax.rem(blk, 2)
    came = {"own": pair, "first": before(pair), "second": after(pair), "third": before(before(pair))}
    for name, source in came.items():
        for which, other in ((name, 0), (name + " beside", 1)):
            start = (2 * source + lax.bitwise_xor(side, other)) * rows
            panel[pl.ds(pl.multiple_of(start, rows), rows), :] = got[which][...]


def add_blocks(columns, tiles, panel, out, owners):
    per_owner = out.shape[0] // (BLOCK * len(owners))
    slots_here = range(tiles.shape[2])
    for j, owner in enumerate(owners):
        numbers = columns[pl.ds(owner * per_owner, per_owner), :]
        for i in range(per_owner):
            starts = [pl.multiple_of(numbers[i, k] * BLOCK, BLOCK) for k in slots_here]
            left = jnp.concatenate([tiles[owner * per_owner + i, 0, k] for k in slots_here], axis=1)
            right = jnp.concatenate([panel[pl.ds(start, BLOCK), :] for start in starts], axis=0)
            summed = jnp.dot(left, right, preferred_element_type=jnp.float32)
            out[pl.ds((j * per_owner + i) * BLOCK, BLOCK), :] = summed.astype(out.dtype)


def other_kernel(names, reps, columns, tiles, *refs):
    pieces, panel, out = refs[: len(names)], refs[-2], refs[-1]
    blk, rep = lax.axis_index("blk"), lax.axis_index("rep")
    place_pieces(panel, blk, tiles.shape[0] * BLOCK // reps, names, pieces)
    add_blocks(columns, tiles, panel, out, [lax.bitwise_xor(rep, d) for d in range(3, reps, 2)])


def other_sums(gathered, adj_tiles, columns):
    reps = lax.axis_size("rep")
    names, pieces = zip(*gathered)
    width = pieces[0].shape[1]
    rows = adj_tiles.shape[0] * BLOCK // reps
    length = lax.axis_size("blk") * rows
    return pl.pallas_call(
        functools.partial(other_kernel, names, reps),
        out_shape=[
            jax.ShapeDtypeStruct((length, width), jnp.bfloat16),
            jax.ShapeDtypeStruct((rows * (reps // 2 - 1), width), jnp.bfloat16),
        ],
        in_specs=[VMEM, VMEM] + [VMEM] * len(pieces),
        out_specs=[VMEM] * 2,
        compiler_params=pltpu.CompilerParams(vmem_limit_bytes=32 * 1024 * 1024),
        cost_estimate=product_cost(adj_tiles, width, reps),
        name="other_sums",
    )(columns, adj_tiles, *pieces)


def sums_kernel(owners, columns, tiles, panel, out):
    rep = lax.axis_index("rep")
    add_blocks(columns, tiles, panel, out, [lax.bitwise_xor(rep, d) for d in owners])


def sums(panel, adj_tiles, columns, owners, kind, name):
    reps = lax.axis_size("rep")
    rows, width = adj_tiles.shape[0] * BLOCK // reps * len(owners), panel.shape[1]
    return pl.pallas_call(
        functools.partial(sums_kernel, owners),
        out_shape=jax.ShapeDtypeStruct((rows, width), kind),
        in_specs=[VMEM, VMEM, VMEM],
        out_specs=VMEM,
        compiler_params=pltpu.CompilerParams(vmem_limit_bytes=32 * 1024 * 1024),
        cost_estimate=product_cost(adj_tiles, width, reps),
        name=name,
    )(columns, adj_tiles, panel)


def product_cost(adj_tiles, width, reps):
    size = adj_tiles.size // reps
    return pl.CostEstimate(flops=2 * size * width, bytes_accessed=2 * size, transcendentals=0)


def add_cores_kernel(own, core, *outs):
    rows = outs[0].shape[0]
    for j, out in enumerate(outs):
        part = pl.ds(j * rows, rows)
        out[...] = (own[part, :] + core[part, :].astype(jnp.float32)).astype(jnp.bfloat16)


def add_cores(own, core, rows):
    width = own.shape[1]
    return pl.pallas_call(
        add_cores_kernel,
        out_shape=[jax.ShapeDtypeStruct((rows, width), jnp.bfloat16)] * (own.shape[0] // rows),
        in_specs=[VMEM] * 2,
        out_specs=[VMEM] * (own.shape[0] // rows),
        compiler_params=pltpu.CompilerParams(vmem_limit_bytes=32 * 1024 * 1024),
        name="add_cores",
    )(own, core)


def tile_products(pieces, adj_tiles, columns, rows):
    reps = lax.axis_size("rep")
    other = [(i, i ^ 1) for i in range(reps)]
    panel, across = other_sums(pieces, adj_tiles, columns)
    core = lax.ppermute(across, "rep", other)
    own = sums(panel, adj_tiles, columns, range(2, reps, 2), jnp.float32, "own_far")
    parts = add_cores(own, core, rows)
    panel, parts = lax.optimization_barrier((panel, parts))
    far = []
    for j, part in enumerate(parts, 1):
        far.append(lax.ppermute(part, "rep", [(i, i ^ (2 * j)) for i in range(reps)]))
    near = sums(panel, adj_tiles, columns, [0], jnp.float32, "own_near")
    panel, near = lax.optimization_barrier((panel, near))
    beside = lax.ppermute(sums(panel, adj_tiles, columns, [1], jnp.bfloat16, "near_other"), "rep", other)
    terms = [near, *far, beside]
    return terms


def add_terms(terms, rows):
    total = terms[0][...].astype(jnp.float32)
    for term in terms[1:]:
        total = total + term[...].astype(jnp.float32)
    return total


def contract(a, b, dims):
    return lax.dot_general(a, b, ((dims[:1], dims[1:]), ((), ())), preferred_element_type=jnp.float32)


def by_row_kernel(by_slot, columns):
    columns[...] = jnp.transpose(by_slot[...])


def by_row(by_slot):
    return pl.pallas_call(
        by_row_kernel,
        out_shape=jax.ShapeDtypeStruct(by_slot.shape[::-1], jnp.int32),
        in_specs=[VMEM],
        out_specs=VMEM,
        compiler_params=pltpu.CompilerParams(vmem_limit_bytes=32 * 1024 * 1024),
        cost_estimate=pl.CostEstimate(flops=BESIDE, bytes_accessed=by_slot.size, transcendentals=0),
        name="by_row",
    )(by_slot)


def early_kernel(cot, w_out, g_hidden):
    g_hidden[...] = contract(cot[...], w_out[...], (1, 1))


def early(cot_out, w_out):
    rows, width = cot_out.shape
    units = w_out.shape[0]
    return pl.pallas_call(
        early_kernel,
        out_shape=jax.ShapeDtypeStruct((rows, units), jnp.float32),
        in_specs=[VMEM] * 2,
        out_specs=VMEM,
        compiler_params=pltpu.CompilerParams(vmem_limit_bytes=32 * 1024 * 1024),
        cost_estimate=pl.CostEstimate(
            flops=2 * rows * width * units, bytes_accessed=8 * rows * units, transcendentals=0
        ),
        name="early",
    )(cot_out, w_out)


def node_pre(terms, rows, w_in, b_in):
    agg_b = add_terms(terms, rows).astype(jnp.bfloat16)
    pre = contract(agg_b, w_in[...], (1, 0)) + b_in[...]
    return pre, 1.0 / (1.0 + jnp.exp(-pre))


def node_kernel(n_terms, *refs):
    terms = refs[:n_terms]
    g_hidden, w_in, b_in, g_out = refs[n_terms:]
    pre, sigma = node_pre(terms, g_out.shape[0], w_in, b_in)
    g_pre = (g_hidden[...] * sigma * (1.0 + pre * (1.0 - sigma))).astype(jnp.bfloat16)
    g_out[...] = contract(g_pre, w_in[...], (1, 1)).astype(jnp.bfloat16)


def node_update(terms, g_hidden, w_in, b_in):
    rows, units = g_hidden.shape
    width = w_in.shape[0]
    return pl.pallas_call(
        functools.partial(node_kernel, len(terms)),
        out_shape=jax.ShapeDtypeStruct((rows, width), jnp.bfloat16),
        in_specs=[VMEM] * (len(terms) + 3),
        out_specs=VMEM,
        compiler_params=pltpu.CompilerParams(vmem_limit_bytes=32 * 1024 * 1024),
        cost_estimate=pl.CostEstimate(
            flops=4 * rows * width * units, bytes_accessed=8 * rows * units, transcendentals=rows * units
        ),
        name="node_update",
    )(*terms, g_hidden, w_in, b_in.reshape(1, -1))


def project_kernel(n_terms, *refs):
    terms = refs[:n_terms]
    feats, w_in, b_in, w_out, b_out, out = refs[n_terms:]
    pre, sigma = node_pre(terms, out.shape[0], w_in, b_in)
    projected = contract((pre * sigma).astype(jnp.bfloat16), w_out[...], (1, 0)) + b_out[...]
    out[...] = (feats[...].astype(jnp.float32) + projected).astype(jnp.bfloat16)


def project(terms, node_feats, w_in, b_in, w_out, b_out):
    rows, width = node_feats.shape
    units = w_in.shape[1]
    return pl.pallas_call(
        functools.partial(project_kernel, len(terms)),
        out_shape=jax.ShapeDtypeStruct((rows, width), jnp.bfloat16),
        in_specs=[VMEM] * (len(terms) + 5),
        out_specs=VMEM,
        compiler_params=pltpu.CompilerParams(vmem_limit_bytes=32 * 1024 * 1024),
        cost_estimate=pl.CostEstimate(
            flops=4 * rows * width * units, bytes_accessed=2 * rows * units, transcendentals=rows * units
        ),
        name="project",
    )(*terms, node_feats, w_in, b_in.reshape(1, -1), w_out, b_out.reshape(1, -1))


def close_kernel(n_terms, *refs):
    cot, out = refs[n_terms:]
    total = add_terms(refs[:n_terms], out.shape[0])
    out[...] = (cot[...].astype(jnp.float32) + total).astype(jnp.bfloat16)


def close_grad(terms, cot_out):
    return pl.pallas_call(
        functools.partial(close_kernel, len(terms)),
        out_shape=jax.ShapeDtypeStruct(cot_out.shape, jnp.bfloat16),
        in_specs=[VMEM] * (len(terms) + 1),
        out_specs=VMEM,
        compiler_params=pltpu.CompilerParams(vmem_limit_bytes=32 * 1024 * 1024),
        name="close_grad",
    )(*terms, cot_out)


def local(node_feats, adj_tiles, col_index, w_in, b_in, w_out, b_out, cot_out):
    rows = node_feats.shape[0]
    columns = by_row(jnp.transpose(col_index, (1, 2, 0))[0])
    g_hidden = early(cot_out, lax.optimization_barrier((w_out, columns))[0])
    columns, g_hidden = lax.optimization_barrier((columns, g_hidden))
    terms = tile_products(gather_blocks(node_feats), adj_tiles, columns, rows)
    g_agg = node_update(terms, g_hidden, w_in, b_in)
    out_feats = project(terms, node_feats, w_in, b_in, w_out, b_out)
    terms = tile_products(gather_blocks(g_agg), adj_tiles, columns, rows)
    return (out_feats, close_grad(terms, cot_out))


def solution(mesh):
    placed = (
        P(("blk", "rep"), None),
        P("blk", "rep", None, None, None),
        P("blk", "rep", None),
        P(),
        P(),
        P(),
        P(),
        P(("blk", "rep"), None),
    )
    return jax.shard_map(
        local,
        mesh=mesh,
        in_specs=placed,
        out_specs=(P(("blk", "rep"), None), P(("blk", "rep"), None)),
        check_vma=False,
    )
```

```python
import functools

import jax
import jax.numpy as jnp
from jax import lax
from jax.experimental import pallas as pl
from jax.experimental.pallas import tpu as pltpu
from jax.sharding import PartitionSpec as P

BLOCK = 128
VMEM = pl.BlockSpec(memory_space=pltpu.VMEM)


BESIDE = 2 * 10**10
PAIRS = 4


def after(pair):
    return (3 * pair + 2) % (PAIRS + 1)


def before(pair):
    return (2 * pair + 1) % (PAIRS + 1)


def gather_blocks(rows):
    n = lax.axis_size("blk")
    if n != 2 * PAIRS:
        return [("all", lax.all_gather(rows, "blk", axis=0, tiled=True))]

    def beside(piece):
        return lax.ppermute(piece, "blk", [(i, i ^ 1) for i in range(n)])

    def step(piece, hop):
        return lax.ppermute(piece, "blk", [(i, 2 * hop(i // 2) + i % 2) for i in range(n)])

    first, second, own_beside = step(rows, after), step(rows, before), beside(rows)
    first_beside = beside(lax.optimization_barrier((first, own_beside))[0])
    third, third_beside = step(first, after), step(first_beside, after)
    second_beside = beside(second)
    return [
        ("own", rows),
        ("own beside", own_beside),
        ("second", second),
        ("second beside", second_beside),
        ("third", third),
        ("third beside", third_beside),
        ("first", first),
        ("first beside", first_beside),
    ]


def place_pieces(panel, blk, rows, names, pieces):
    got = dict(zip(names, pieces))
    if "all" in got:
        panel[...] = got["all"][...]
        return
    pair, side = blk // 2, lax.rem(blk, 2)
    came = {"own": pair, "first": before(pair), "second": after(pair), "third": before(before(pair))}
    for name, source in came.items():
        for which, other in ((name, 0), (name + " beside", 1)):
            start = (2 * source + lax.bitwise_xor(side, other)) * rows
            panel[pl.ds(pl.multiple_of(start, rows), rows), :] = got[which][...]


def add_blocks(columns, tiles, panel, out, owner):
    per_owner = out.shape[0] // BLOCK
    slots_here = range(tiles.shape[2])
    numbers = columns[pl.ds(owner * per_owner, per_owner), :]
    for i in range(per_owner):
        starts = [pl.multiple_of(numbers[i, k] * BLOCK, BLOCK) for k in slots_here]
        left = jnp.concatenate([tiles[owner * per_owner + i, 0, k] for k in slots_here], axis=1)
        right = jnp.concatenate([panel[pl.ds(start, BLOCK), :] for start in starts], axis=0)
        summed = jnp.dot(left, right, preferred_element_type=jnp.float32)
        out[pl.ds(i * BLOCK, BLOCK), :] = summed.astype(out.dtype)


def far_kernel(names, columns, tiles, *refs):
    pieces, panel, outs = refs[: len(names)], refs[len(names)], refs[len(names) + 1 :]
    blk, rep = lax.axis_index("blk"), lax.axis_index("rep")
    place_pieces(panel, blk, outs[0].shape[0], names, pieces)
    for d, out in enumerate(outs, 2):
        add_blocks(columns, tiles, panel, out, lax.bitwise_xor(rep, d))


def far_sums(gathered, adj_tiles, columns):
    reps = lax.axis_size("rep")
    names, pieces = zip(*gathered)
    width = pieces[0].shape[1]
    rows = adj_tiles.shape[0] * BLOCK // reps
    length = lax.axis_size("blk") * rows
    return pl.pallas_call(
        functools.partial(far_kernel, names),
        out_shape=[jax.ShapeDtypeStruct((length, width), jnp.bfloat16)]
        + [jax.ShapeDtypeStruct((rows, width), jnp.bfloat16)] * (reps - 2),
        in_specs=[VMEM, VMEM] + [VMEM] * len(pieces),
        out_specs=[VMEM] * (reps - 1),
        compiler_params=pltpu.CompilerParams(vmem_limit_bytes=32 * 1024 * 1024),
        cost_estimate=product_cost(adj_tiles, width, reps),
        name="far_sums",
    )(columns, adj_tiles, *pieces)


def near_kernel(d, columns, tiles, panel, out):
    add_blocks(columns, tiles, panel, out, lax.bitwise_xor(lax.axis_index("rep"), d))


def near_sums(panel, adj_tiles, columns, d, kind, name):
    reps = lax.axis_size("rep")
    rows, width = adj_tiles.shape[0] * BLOCK // reps, panel.shape[1]
    return pl.pallas_call(
        functools.partial(near_kernel, d),
        out_shape=jax.ShapeDtypeStruct((rows, width), kind),
        in_specs=[VMEM, VMEM, VMEM],
        out_specs=VMEM,
        compiler_params=pltpu.CompilerParams(vmem_limit_bytes=32 * 1024 * 1024),
        cost_estimate=product_cost(adj_tiles, width, reps),
        name=name,
    )(columns, adj_tiles, panel)


def product_cost(adj_tiles, width, reps):
    size = adj_tiles.size // reps
    return pl.CostEstimate(flops=2 * size * width, bytes_accessed=2 * size, transcendentals=0)


def tile_products(pieces, adj_tiles, columns):
    reps = lax.axis_size("rep")

    def send(part, d):
        return lax.ppermute(part, "rep", [(i, i ^ d) for i in range(reps)])

    panel, *parts = far_sums(pieces, adj_tiles, columns)
    far = [send(part, d) for d, part in enumerate(parts, 2)]
    near = near_sums(panel, adj_tiles, columns, 0, jnp.float32, "own_near")
    panel, near = lax.optimization_barrier((panel, near))
    beside = send(near_sums(panel, adj_tiles, columns, 1, jnp.bfloat16, "near_other"), 1)
    return [near, *far, beside]


def add_terms(terms, rows):
    total = terms[0][...].astype(jnp.float32)
    for term in terms[1:]:
        total = total + term[...].astype(jnp.float32)
    return total


def contract(a, b, dims):
    return lax.dot_general(a, b, ((dims[:1], dims[1:]), ((), ())), preferred_element_type=jnp.float32)


def by_row_kernel(by_slot, columns):
    columns[...] = jnp.transpose(by_slot[...])


def by_row(by_slot):
    return pl.pallas_call(
        by_row_kernel,
        out_shape=jax.ShapeDtypeStruct(by_slot.shape[::-1], jnp.int32),
        in_specs=[VMEM],
        out_specs=VMEM,
        compiler_params=pltpu.CompilerParams(vmem_limit_bytes=32 * 1024 * 1024),
        cost_estimate=pl.CostEstimate(flops=BESIDE, bytes_accessed=by_slot.size, transcendentals=0),
        name="by_row",
    )(by_slot)


def early_kernel(cot, w_out, g_hidden):
    g_hidden[...] = contract(cot[...], w_out[...], (1, 1))


def early(cot_out, w_out):
    rows, width = cot_out.shape
    units = w_out.shape[0]
    return pl.pallas_call(
        early_kernel,
        out_shape=jax.ShapeDtypeStruct((rows, units), jnp.float32),
        in_specs=[VMEM] * 2,
        out_specs=VMEM,
        compiler_params=pltpu.CompilerParams(vmem_limit_bytes=32 * 1024 * 1024),
        cost_estimate=pl.CostEstimate(
            flops=2 * rows * width * units, bytes_accessed=8 * rows * units, transcendentals=0
        ),
        name="early",
    )(cot_out, w_out)


def node_pre(terms, rows, w_in, b_in):
    agg_b = add_terms(terms, rows).astype(jnp.bfloat16)
    pre = contract(agg_b, w_in[...], (1, 0)) + b_in[...]
    return pre, 1.0 / (1.0 + jnp.exp(-pre))


def node_kernel(n_terms, *refs):
    terms = refs[:n_terms]
    g_hidden, w_in, b_in, g_out = refs[n_terms:]
    pre, sigma = node_pre(terms, g_out.shape[0], w_in, b_in)
    g_pre = (g_hidden[...] * sigma * (1.0 + pre * (1.0 - sigma))).astype(jnp.bfloat16)
    g_out[...] = contract(g_pre, w_in[...], (1, 1)).astype(jnp.bfloat16)


def node_update(terms, g_hidden, w_in, b_in):
    rows, units = g_hidden.shape
    width = w_in.shape[0]
    return pl.pallas_call(
        functools.partial(node_kernel, len(terms)),
        out_shape=jax.ShapeDtypeStruct((rows, width), jnp.bfloat16),
        in_specs=[VMEM] * (len(terms) + 3),
        out_specs=VMEM,
        compiler_params=pltpu.CompilerParams(vmem_limit_bytes=32 * 1024 * 1024),
        cost_estimate=pl.CostEstimate(
            flops=4 * rows * width * units, bytes_accessed=8 * rows * units, transcendentals=rows * units
        ),
        name="node_update",
    )(*terms, g_hidden, w_in, b_in.reshape(1, -1))


def project_kernel(n_terms, *refs):
    terms = refs[:n_terms]
    feats, w_in, b_in, w_out, b_out, out = refs[n_terms:]
    pre, sigma = node_pre(terms, out.shape[0], w_in, b_in)
    projected = contract((pre * sigma).astype(jnp.bfloat16), w_out[...], (1, 0)) + b_out[...]
    out[...] = (feats[...].astype(jnp.float32) + projected).astype(jnp.bfloat16)


def project(terms, node_feats, w_in, b_in, w_out, b_out):
    rows, width = node_feats.shape
    units = w_in.shape[1]
    return pl.pallas_call(
        functools.partial(project_kernel, len(terms)),
        out_shape=jax.ShapeDtypeStruct((rows, width), jnp.bfloat16),
        in_specs=[VMEM] * (len(terms) + 5),
        out_specs=VMEM,
        compiler_params=pltpu.CompilerParams(vmem_limit_bytes=32 * 1024 * 1024),
        cost_estimate=pl.CostEstimate(
            flops=4 * rows * width * units, bytes_accessed=2 * rows * units, transcendentals=rows * units
        ),
        name="project",
    )(*terms, node_feats, w_in, b_in.reshape(1, -1), w_out, b_out.reshape(1, -1))


def close_kernel(n_terms, *refs):
    cot, out = refs[n_terms:]
    total = add_terms(refs[:n_terms], out.shape[0])
    out[...] = (cot[...].astype(jnp.float32) + total).astype(jnp.bfloat16)


def close_grad(terms, cot_out):
    return pl.pallas_call(
        functools.partial(close_kernel, len(terms)),
        out_shape=jax.ShapeDtypeStruct(cot_out.shape, jnp.bfloat16),
        in_specs=[VMEM] * (len(terms) + 1),
        out_specs=VMEM,
        compiler_params=pltpu.CompilerParams(vmem_limit_bytes=32 * 1024 * 1024),
        name="close_grad",
    )(*terms, cot_out)


def local(node_feats, adj_tiles, col_index, w_in, b_in, w_out, b_out, cot_out):
    columns = by_row(jnp.transpose(col_index, (1, 2, 0))[0])
    g_hidden = early(cot_out, lax.optimization_barrier((w_out, columns))[0])
    columns, g_hidden = lax.optimization_barrier((columns, g_hidden))
    terms = tile_products(gather_blocks(node_feats), adj_tiles, columns)
    g_agg = node_update(terms, g_hidden, w_in, b_in)
    out_feats = project(terms, node_feats, w_in, b_in, w_out, b_out)
    terms = tile_products(gather_blocks(g_agg), adj_tiles, columns)
    return (out_feats, close_grad(terms, cot_out))


def solution(mesh):
    placed = (
        P(("blk", "rep"), None),
        P("blk", "rep", None, None, None),
        P("blk", "rep", None),
        P(),
        P(),
        P(),
        P(),
        P(("blk", "rep"), None),
    )
    return jax.shard_map(
        local,
        mesh=mesh,
        in_specs=placed,
        out_specs=(P(("blk", "rep"), None), P(("blk", "rep"), None)),
        check_vma=False,
    )
```

```python
import functools

import jax
import jax.numpy as jnp
from jax import lax
from jax.experimental import pallas as pl
from jax.experimental.pallas import tpu as pltpu
from jax.sharding import PartitionSpec as P

BLOCK = 128
VMEM = pl.BlockSpec(memory_space=pltpu.VMEM)


BESIDE = 2 * 10**10
PAIRS = 4


def after(pair):
    return (3 * pair + 2) % (PAIRS + 1)


def before(pair):
    return (2 * pair + 1) % (PAIRS + 1)


def gather_blocks(rows):
    n = lax.axis_size("blk")
    if n != 2 * PAIRS:
        return [("all", lax.all_gather(rows, "blk", axis=0, tiled=True))]

    def beside(piece):
        return lax.ppermute(piece, "blk", [(i, i ^ 1) for i in range(n)])

    def step(piece, hop):
        return lax.ppermute(piece, "blk", [(i, 2 * hop(i // 2) + i % 2) for i in range(n)])

    first, second, own_beside = step(rows, after), step(rows, before), beside(rows)
    first_beside = beside(first)
    third = step(lax.optimization_barrier((first, own_beside))[0], after)
    third_beside = step(first_beside, after)
    second_beside = beside(second)
    return [
        ("own", rows),
        ("own beside", own_beside),
        ("second", second),
        ("second beside", second_beside),
        ("third", third),
        ("third beside", third_beside),
        ("first", first),
        ("first beside", first_beside),
    ]


def place_pieces(panel, blk, rows, names, pieces):
    got = dict(zip(names, pieces))
    if "all" in got:
        panel[...] = got["all"][...]
        return
    pair, side = blk // 2, lax.rem(blk, 2)
    came = {"own": pair, "first": before(pair), "second": after(pair), "third": before(before(pair))}
    for name, source in came.items():
        for which, other in ((name, 0), (name + " beside", 1)):
            start = (2 * source + lax.bitwise_xor(side, other)) * rows
            panel[pl.ds(pl.multiple_of(start, rows), rows), :] = got[which][...]


def add_blocks(columns, tiles, panel, out, owners):
    per_owner = out.shape[0] // (BLOCK * len(owners))
    slots_here = range(tiles.shape[2])
    for j, owner in enumerate(owners):
        numbers = columns[pl.ds(owner * per_owner, per_owner), :]
        for i in range(per_owner):
            starts = [pl.multiple_of(numbers[i, k] * BLOCK, BLOCK) for k in slots_here]
            left = jnp.concatenate([tiles[owner * per_owner + i, 0, k] for k in slots_here], axis=1)
            right = jnp.concatenate([panel[pl.ds(start, BLOCK), :] for start in starts], axis=0)
            summed = jnp.dot(left, right, preferred_element_type=jnp.float32)
            out[pl.ds((j * per_owner + i) * BLOCK, BLOCK), :] = summed.astype(out.dtype)


def other_kernel(names, reps, columns, tiles, *refs):
    pieces, panel, out = refs[: len(names)], refs[-2], refs[-1]
    blk, rep = lax.axis_index("blk"), lax.axis_index("rep")
    place_pieces(panel, blk, tiles.shape[0] * BLOCK // reps, names, pieces)
    add_blocks(columns, tiles, panel, out, [lax.bitwise_xor(rep, d) for d in range(3, reps, 2)])


def other_sums(gathered, adj_tiles, columns):
    reps = lax.axis_size("rep")
    names, pieces = zip(*gathered)
    width = pieces[0].shape[1]
    rows = adj_tiles.shape[0] * BLOCK // reps
    length = lax.axis_size("blk") * rows
    return pl.pallas_call(
        functools.partial(other_kernel, names, reps),
        out_shape=[
            jax.ShapeDtypeStruct((length, width), jnp.bfloat16),
            jax.ShapeDtypeStruct((rows * (reps // 2 - 1), width), jnp.bfloat16),
        ],
        in_specs=[VMEM, VMEM] + [VMEM] * len(pieces),
        out_specs=[VMEM] * 2,
        compiler_params=pltpu.CompilerParams(vmem_limit_bytes=32 * 1024 * 1024),
        cost_estimate=product_cost(adj_tiles, width, reps),
        name="other_sums",
    )(columns, adj_tiles, *pieces)


def sums_kernel(owners, columns, tiles, panel, out):
    rep = lax.axis_index("rep")
    add_blocks(columns, tiles, panel, out, [lax.bitwise_xor(rep, d) for d in owners])


def sums(panel, adj_tiles, columns, owners, kind, name):
    reps = lax.axis_size("rep")
    rows, width = adj_tiles.shape[0] * BLOCK // reps * len(owners), panel.shape[1]
    return pl.pallas_call(
        functools.partial(sums_kernel, owners),
        out_shape=jax.ShapeDtypeStruct((rows, width), kind),
        in_specs=[VMEM, VMEM, VMEM],
        out_specs=VMEM,
        compiler_params=pltpu.CompilerParams(vmem_limit_bytes=32 * 1024 * 1024),
        cost_estimate=product_cost(adj_tiles, width, reps),
        name=name,
    )(columns, adj_tiles, panel)


def product_cost(adj_tiles, width, reps):
    size = adj_tiles.size // reps
    return pl.CostEstimate(flops=2 * size * width, bytes_accessed=2 * size, transcendentals=0)


def add_cores_kernel(own, core, *outs):
    rows = outs[0].shape[0]
    for j, out in enumerate(outs):
        part = pl.ds(j * rows, rows)
        out[...] = (own[part, :] + core[part, :].astype(jnp.float32)).astype(jnp.bfloat16)


def add_cores(own, core, rows):
    width = own.shape[1]
    return pl.pallas_call(
        add_cores_kernel,
        out_shape=[jax.ShapeDtypeStruct((rows, width), jnp.bfloat16)] * (own.shape[0] // rows),
        in_specs=[VMEM] * 2,
        out_specs=[VMEM] * (own.shape[0] // rows),
        compiler_params=pltpu.CompilerParams(vmem_limit_bytes=32 * 1024 * 1024),
        name="add_cores",
    )(own, core)


def tile_products(pieces, adj_tiles, columns, rows):
    reps = lax.axis_size("rep")
    other = [(i, i ^ 1) for i in range(reps)]
    panel, across = other_sums(pieces, adj_tiles, columns)
    core = lax.ppermute(across, "rep", other)
    own = sums(panel, adj_tiles, columns, range(2, reps, 2), jnp.float32, "own_far")
    parts = add_cores(own, core, rows)
    panel, parts = lax.optimization_barrier((panel, parts))
    far = []
    for j, part in enumerate(parts, 1):
        far.append(lax.ppermute(part, "rep", [(i, i ^ (2 * j)) for i in range(reps)]))
    near = sums(panel, adj_tiles, columns, [0], jnp.float32, "own_near")
    panel, near = lax.optimization_barrier((panel, near))
    beside = lax.ppermute(sums(panel, adj_tiles, columns, [1], jnp.bfloat16, "near_other"), "rep", other)
    terms = [near, *far, beside]
    return terms


def add_terms(terms, rows):
    total = terms[0][...].astype(jnp.float32)
    for term in terms[1:]:
        total = total + term[...].astype(jnp.float32)
    return total


def contract(a, b, dims):
    return lax.dot_general(a, b, ((dims[:1], dims[1:]), ((), ())), preferred_element_type=jnp.float32)


def by_row_kernel(by_slot, columns):
    columns[...] = jnp.transpose(by_slot[...])


def by_row(by_slot):
    return pl.pallas_call(
        by_row_kernel,
        out_shape=jax.ShapeDtypeStruct(by_slot.shape[::-1], jnp.int32),
        in_specs=[VMEM],
        out_specs=VMEM,
        compiler_params=pltpu.CompilerParams(vmem_limit_bytes=32 * 1024 * 1024),
        cost_estimate=pl.CostEstimate(flops=BESIDE, bytes_accessed=by_slot.size, transcendentals=0),
        name="by_row",
    )(by_slot)


def early_kernel(cot, w_out, g_hidden):
    g_hidden[...] = contract(cot[...], w_out[...], (1, 1))


def early(cot_out, w_out):
    rows, width = cot_out.shape
    units = w_out.shape[0]
    return pl.pallas_call(
        early_kernel,
        out_shape=jax.ShapeDtypeStruct((rows, units), jnp.float32),
        in_specs=[VMEM] * 2,
        out_specs=VMEM,
        compiler_params=pltpu.CompilerParams(vmem_limit_bytes=32 * 1024 * 1024),
        cost_estimate=pl.CostEstimate(
            flops=2 * rows * width * units, bytes_accessed=8 * rows * units, transcendentals=0
        ),
        name="early",
    )(cot_out, w_out)


def node_pre(terms, rows, w_in, b_in):
    agg_b = add_terms(terms, rows).astype(jnp.bfloat16)
    pre = contract(agg_b, w_in[...], (1, 0)) + b_in[...]
    return pre, 1.0 / (1.0 + jnp.exp(-pre))


def node_kernel(n_terms, *refs):
    terms = refs[:n_terms]
    g_hidden, w_in, b_in, g_out = refs[n_terms:]
    pre, sigma = node_pre(terms, g_out.shape[0], w_in, b_in)
    g_pre = (g_hidden[...] * sigma * (1.0 + pre * (1.0 - sigma))).astype(jnp.bfloat16)
    g_out[...] = contract(g_pre, w_in[...], (1, 1)).astype(jnp.bfloat16)


def node_update(terms, g_hidden, w_in, b_in):
    rows, units = g_hidden.shape
    width = w_in.shape[0]
    return pl.pallas_call(
        functools.partial(node_kernel, len(terms)),
        out_shape=jax.ShapeDtypeStruct((rows, width), jnp.bfloat16),
        in_specs=[VMEM] * (len(terms) + 3),
        out_specs=VMEM,
        compiler_params=pltpu.CompilerParams(vmem_limit_bytes=32 * 1024 * 1024),
        cost_estimate=pl.CostEstimate(
            flops=4 * rows * width * units, bytes_accessed=8 * rows * units, transcendentals=rows * units
        ),
        name="node_update",
    )(*terms, g_hidden, w_in, b_in.reshape(1, -1))


def project_kernel(n_terms, *refs):
    terms = refs[:n_terms]
    feats, w_in, b_in, w_out, b_out, out = refs[n_terms:]
    pre, sigma = node_pre(terms, out.shape[0], w_in, b_in)
    projected = contract((pre * sigma).astype(jnp.bfloat16), w_out[...], (1, 0)) + b_out[...]
    out[...] = (feats[...].astype(jnp.float32) + projected).astype(jnp.bfloat16)


def project(terms, node_feats, w_in, b_in, w_out, b_out):
    rows, width = node_feats.shape
    units = w_in.shape[1]
    return pl.pallas_call(
        functools.partial(project_kernel, len(terms)),
        out_shape=jax.ShapeDtypeStruct((rows, width), jnp.bfloat16),
        in_specs=[VMEM] * (len(terms) + 5),
        out_specs=VMEM,
        compiler_params=pltpu.CompilerParams(vmem_limit_bytes=32 * 1024 * 1024),
        cost_estimate=pl.CostEstimate(
            flops=4 * rows * width * units, bytes_accessed=2 * rows * units, transcendentals=rows * units
        ),
        name="project",
    )(*terms, node_feats, w_in, b_in.reshape(1, -1), w_out, b_out.reshape(1, -1))


def close_kernel(n_terms, *refs):
    cot, out = refs[n_terms:]
    total = add_terms(refs[:n_terms], out.shape[0])
    out[...] = (cot[...].astype(jnp.float32) + total).astype(jnp.bfloat16)


def close_grad(terms, cot_out):
    return pl.pallas_call(
        functools.partial(close_kernel, len(terms)),
        out_shape=jax.ShapeDtypeStruct(cot_out.shape, jnp.bfloat16),
        in_specs=[VMEM] * (len(terms) + 1),
        out_specs=VMEM,
        compiler_params=pltpu.CompilerParams(vmem_limit_bytes=32 * 1024 * 1024),
        name="close_grad",
    )(*terms, cot_out)


def local(node_feats, adj_tiles, col_index, w_in, b_in, w_out, b_out, cot_out):
    rows = node_feats.shape[0]
    columns = by_row(jnp.transpose(col_index, (1, 2, 0))[0])
    g_hidden = early(cot_out, lax.optimization_barrier((w_out, columns))[0])
    columns, g_hidden = lax.optimization_barrier((columns, g_hidden))
    terms = tile_products(gather_blocks(node_feats), adj_tiles, columns, rows)
    g_agg = node_update(terms, g_hidden, w_in, b_in)
    out_feats = project(terms, node_feats, w_in, b_in, w_out, b_out)
    terms = tile_products(gather_blocks(g_agg), adj_tiles, columns, rows)
    return (out_feats, close_grad(terms, cot_out))


def solution(mesh):
    placed = (
        P(("blk", "rep"), None),
        P("blk", "rep", None, None, None),
        P("blk", "rep", None),
        P(),
        P(),
        P(),
        P(),
        P(("blk", "rep"), None),
    )
    return jax.shard_map(
        local,
        mesh=mesh,
        in_specs=placed,
        out_specs=(P(("blk", "rep"), None), P(("blk", "rep"), None)),
        check_vma=False,
    )
```

```python
import functools

import jax
import jax.numpy as jnp
from jax import lax
from jax.experimental import pallas as pl
from jax.experimental.pallas import tpu as pltpu
from jax.sharding import PartitionSpec as P

BLOCK = 128
VMEM = pl.BlockSpec(memory_space=pltpu.VMEM)


BESIDE = 2 * 10**10
PAIRS = 4


def after(pair):
    return (3 * pair + 2) % (PAIRS + 1)


def before(pair):
    return (2 * pair + 1) % (PAIRS + 1)


def gather_blocks(rows):
    n = lax.axis_size("blk")
    if n != 2 * PAIRS:
        return [("all", lax.all_gather(rows, "blk", axis=0, tiled=True))]

    def beside(piece):
        return lax.ppermute(piece, "blk", [(i, i ^ 1) for i in range(n)])

    def step(piece, hop):
        return lax.ppermute(piece, "blk", [(i, 2 * hop(i // 2) + i % 2) for i in range(n)])

    first, second, own_beside = step(rows, after), step(rows, before), beside(rows)
    first_beside = beside(first)
    third = step(lax.optimization_barrier((first, own_beside))[0], after)
    third_beside = step(first_beside, after)
    second_beside = beside(second)
    return [
        ("own", rows),
        ("own beside", own_beside),
        ("second", second),
        ("second beside", second_beside),
        ("third", third),
        ("third beside", third_beside),
        ("first", first),
        ("first beside", first_beside),
    ]


def place_pieces(panel, blk, rows, names, pieces):
    got = dict(zip(names, pieces))
    if "all" in got:
        panel[...] = got["all"][...]
        return
    pair, side = blk // 2, lax.rem(blk, 2)
    came = {"own": pair, "first": before(pair), "second": after(pair), "third": before(before(pair))}
    for name, source in came.items():
        for which, other in ((name, 0), (name + " beside", 1)):
            start = (2 * source + lax.bitwise_xor(side, other)) * rows
            panel[pl.ds(pl.multiple_of(start, rows), rows), :] = got[which][...]


def add_blocks(columns, tiles, panel, out, owners):
    per_owner = out.shape[0] // (BLOCK * len(owners))
    slots_here = range(tiles.shape[2])
    for j, owner in enumerate(owners):
        numbers = columns[pl.ds(owner * per_owner, per_owner), :]
        for i in range(per_owner):
            starts = [pl.multiple_of(numbers[i, k] * BLOCK, BLOCK) for k in slots_here]
            left = jnp.concatenate([tiles[owner * per_owner + i, 0, k] for k in slots_here], axis=1)
            right = jnp.concatenate([panel[pl.ds(start, BLOCK), :] for start in starts], axis=0)
            summed = jnp.dot(left, right, preferred_element_type=jnp.float32)
            out[pl.ds((j * per_owner + i) * BLOCK, BLOCK), :] = summed.astype(out.dtype)


def other_kernel(names, reps, columns, tiles, *refs):
    pieces, panel, out = refs[: len(names)], refs[-2], refs[-1]
    blk, rep = lax.axis_index("blk"), lax.axis_index("rep")
    place_pieces(panel, blk, tiles.shape[0] * BLOCK // reps, names, pieces)
    add_blocks(columns, tiles, panel, out, [lax.bitwise_xor(rep, d) for d in range(3, reps, 2)])


def other_sums(gathered, adj_tiles, columns):
    reps = lax.axis_size("rep")
    names, pieces = zip(*gathered)
    width = pieces[0].shape[1]
    rows = adj_tiles.shape[0] * BLOCK // reps
    length = lax.axis_size("blk") * rows
    return pl.pallas_call(
        functools.partial(other_kernel, names, reps),
        out_shape=[
            jax.ShapeDtypeStruct((length, width), jnp.bfloat16),
            jax.ShapeDtypeStruct((rows * (reps // 2 - 1), width), jnp.bfloat16),
        ],
        in_specs=[VMEM, VMEM] + [VMEM] * len(pieces),
        out_specs=[VMEM] * 2,
        compiler_params=pltpu.CompilerParams(vmem_limit_bytes=32 * 1024 * 1024),
        cost_estimate=product_cost(adj_tiles, width, reps),
        name="other_sums",
    )(columns, adj_tiles, *pieces)


def sums_kernel(owners, columns, tiles, panel, out):
    rep = lax.axis_index("rep")
    add_blocks(columns, tiles, panel, out, [lax.bitwise_xor(rep, d) for d in owners])


def sums(panel, adj_tiles, columns, owners, kind, name):
    reps = lax.axis_size("rep")
    rows, width = adj_tiles.shape[0] * BLOCK // reps * len(owners), panel.shape[1]
    return pl.pallas_call(
        functools.partial(sums_kernel, owners),
        out_shape=jax.ShapeDtypeStruct((rows, width), kind),
        in_specs=[VMEM, VMEM, VMEM],
        out_specs=VMEM,
        compiler_params=pltpu.CompilerParams(vmem_limit_bytes=32 * 1024 * 1024),
        cost_estimate=product_cost(adj_tiles, width, reps),
        name=name,
    )(columns, adj_tiles, panel)


def product_cost(adj_tiles, width, reps):
    size = adj_tiles.size // reps
    return pl.CostEstimate(flops=2 * size * width, bytes_accessed=2 * size, transcendentals=0)


def add_cores_kernel(own, core, *outs):
    rows = outs[0].shape[0]
    for j, out in enumerate(outs):
        part = pl.ds(j * rows, rows)
        out[...] = (own[part, :] + core[part, :].astype(jnp.float32)).astype(jnp.bfloat16)


def add_cores(own, core, rows):
    width = own.shape[1]
    return pl.pallas_call(
        add_cores_kernel,
        out_shape=[jax.ShapeDtypeStruct((rows, width), jnp.bfloat16)] * (own.shape[0] // rows),
        in_specs=[VMEM] * 2,
        out_specs=[VMEM] * (own.shape[0] // rows),
        compiler_params=pltpu.CompilerParams(vmem_limit_bytes=32 * 1024 * 1024),
        name="add_cores",
    )(own, core)


def tile_products(pieces, adj_tiles, columns, rows):
    reps = lax.axis_size("rep")
    other = [(i, i ^ 1) for i in range(reps)]
    panel, across = other_sums(pieces, adj_tiles, columns)
    core = lax.ppermute(across, "rep", other)
    own = sums(panel, adj_tiles, columns, range(2, reps, 2), jnp.float32, "own_far")
    parts = add_cores(own, core, rows)
    panel, parts = lax.optimization_barrier((panel, parts))
    far = []
    for j, part in enumerate(parts, 1):
        far.append(lax.ppermute(part, "rep", [(i, i ^ (2 * j)) for i in range(reps)]))
    near = sums(panel, adj_tiles, columns, [0], jnp.float32, "own_near")
    panel, near = lax.optimization_barrier((panel, near))
    beside = lax.ppermute(sums(panel, adj_tiles, columns, [1], jnp.bfloat16, "near_other"), "rep", other)
    terms = [near, *far, beside]
    return terms


def add_terms(terms, rows):
    total = terms[0][...].astype(jnp.float32)
    for term in terms[1:]:
        total = total + term[...].astype(jnp.float32)
    return total


def contract(a, b, dims):
    return lax.dot_general(a, b, ((dims[:1], dims[1:]), ((), ())), preferred_element_type=jnp.float32)


def by_row_kernel(by_slot, columns):
    columns[...] = jnp.zeros_like(columns)
    columns[pl.ds(0, by_slot.shape[1]), :] = jnp.transpose(by_slot[...])


def by_row(by_slot):
    per_row, rows = by_slot.shape
    return pl.pallas_call(
        by_row_kernel,
        out_shape=jax.ShapeDtypeStruct((rows + 8, per_row), jnp.int32),
        in_specs=[VMEM],
        out_specs=VMEM,
        compiler_params=pltpu.CompilerParams(vmem_limit_bytes=32 * 1024 * 1024),
        cost_estimate=pl.CostEstimate(flops=BESIDE, bytes_accessed=by_slot.size, transcendentals=0),
        name="by_row",
    )(by_slot)


def early_kernel(cot, w_out, g_hidden):
    g_hidden[...] = contract(cot[...], w_out[...], (1, 1))


def early(cot_out, w_out):
    rows, width = cot_out.shape
    units = w_out.shape[0]
    return pl.pallas_call(
        early_kernel,
        out_shape=jax.ShapeDtypeStruct((rows, units), jnp.float32),
        in_specs=[VMEM] * 2,
        out_specs=VMEM,
        compiler_params=pltpu.CompilerParams(vmem_limit_bytes=32 * 1024 * 1024),
        cost_estimate=pl.CostEstimate(
            flops=2 * rows * width * units, bytes_accessed=8 * rows * units, transcendentals=0
        ),
        name="early",
    )(cot_out, w_out)


def node_pre(terms, rows, w_in, b_in):
    agg_b = add_terms(terms, rows).astype(jnp.bfloat16)
    pre = contract(agg_b, w_in[...], (1, 0)) + b_in[...]
    return pre, 1.0 / (1.0 + jnp.exp(-pre))


def node_kernel(n_terms, *refs):
    terms = refs[:n_terms]
    g_hidden, w_in, b_in, g_out = refs[n_terms:]
    pre, sigma = node_pre(terms, g_out.shape[0], w_in, b_in)
    g_pre = (g_hidden[...] * sigma * (1.0 + pre * (1.0 - sigma))).astype(jnp.bfloat16)
    g_out[...] = contract(g_pre, w_in[...], (1, 1)).astype(jnp.bfloat16)


def node_update(terms, g_hidden, w_in, b_in):
    rows, units = g_hidden.shape
    width = w_in.shape[0]
    return pl.pallas_call(
        functools.partial(node_kernel, len(terms)),
        out_shape=jax.ShapeDtypeStruct((rows, width), jnp.bfloat16),
        in_specs=[VMEM] * (len(terms) + 3),
        out_specs=VMEM,
        compiler_params=pltpu.CompilerParams(vmem_limit_bytes=32 * 1024 * 1024),
        cost_estimate=pl.CostEstimate(
            flops=4 * rows * width * units, bytes_accessed=8 * rows * units, transcendentals=rows * units
        ),
        name="node_update",
    )(*terms, g_hidden, w_in, b_in.reshape(1, -1))


def project_kernel(n_terms, *refs):
    terms = refs[:n_terms]
    feats, w_in, b_in, w_out, b_out, out = refs[n_terms:]
    pre, sigma = node_pre(terms, out.shape[0], w_in, b_in)
    projected = contract((pre * sigma).astype(jnp.bfloat16), w_out[...], (1, 0)) + b_out[...]
    out[...] = (feats[...].astype(jnp.float32) + projected).astype(jnp.bfloat16)


def project(terms, node_feats, w_in, b_in, w_out, b_out):
    rows, width = node_feats.shape
    units = w_in.shape[1]
    return pl.pallas_call(
        functools.partial(project_kernel, len(terms)),
        out_shape=jax.ShapeDtypeStruct((rows, width), jnp.bfloat16),
        in_specs=[VMEM] * (len(terms) + 5),
        out_specs=VMEM,
        compiler_params=pltpu.CompilerParams(vmem_limit_bytes=32 * 1024 * 1024),
        cost_estimate=pl.CostEstimate(
            flops=4 * rows * width * units, bytes_accessed=2 * rows * units, transcendentals=rows * units
        ),
        name="project",
    )(*terms, node_feats, w_in, b_in.reshape(1, -1), w_out, b_out.reshape(1, -1))


def close_kernel(n_terms, *refs):
    cot, out = refs[n_terms:]
    total = add_terms(refs[:n_terms], out.shape[0])
    out[...] = (cot[...].astype(jnp.float32) + total).astype(jnp.bfloat16)


def close_grad(terms, cot_out):
    return pl.pallas_call(
        functools.partial(close_kernel, len(terms)),
        out_shape=jax.ShapeDtypeStruct(cot_out.shape, jnp.bfloat16),
        in_specs=[VMEM] * (len(terms) + 1),
        out_specs=VMEM,
        compiler_params=pltpu.CompilerParams(vmem_limit_bytes=32 * 1024 * 1024),
        name="close_grad",
    )(*terms, cot_out)


def local(node_feats, adj_tiles, col_index, w_in, b_in, w_out, b_out, cot_out):
    rows = node_feats.shape[0]
    columns = by_row(jnp.transpose(col_index, (1, 2, 0))[0])
    g_hidden = early(cot_out, lax.optimization_barrier((w_out, columns))[0])
    columns, g_hidden = lax.optimization_barrier((columns, g_hidden))
    terms = tile_products(gather_blocks(node_feats), adj_tiles, columns, rows)
    g_agg = node_update(terms, g_hidden, w_in, b_in)
    out_feats = project(terms, node_feats, w_in, b_in, w_out, b_out)
    terms = tile_products(gather_blocks(g_agg), adj_tiles, columns, rows)
    return (out_feats, close_grad(terms, cot_out))


def solution(mesh):
    placed = (
        P(("blk", "rep"), None),
        P("blk", "rep", None, None, None),
        P("blk", "rep", None),
        P(),
        P(),
        P(),
        P(),
        P(("blk", "rep"), None),
    )
    return jax.shard_map(
        local,
        mesh=mesh,
        in_specs=placed,
        out_specs=(P(("blk", "rep"), None), P(("blk", "rep"), None)),
        check_vma=False,
    )
```

```python
import functools

import jax
import jax.numpy as jnp
from jax import lax
from jax.experimental import pallas as pl
from jax.experimental.pallas import tpu as pltpu
from jax.sharding import PartitionSpec as P

BLOCK = 128
VMEM = pl.BlockSpec(memory_space=pltpu.VMEM)


BESIDE = 2 * 10**10
PAIRS = 4


def after(pair):
    return (3 * pair + 2) % (PAIRS + 1)


def before(pair):
    return (2 * pair + 1) % (PAIRS + 1)


def gather_blocks(rows):
    n = lax.axis_size("blk")
    if n != 2 * PAIRS:
        return [("all", lax.all_gather(rows, "blk", axis=0, tiled=True))]

    def beside(piece):
        return lax.ppermute(piece, "blk", [(i, i ^ 1) for i in range(n)])

    def step(piece, hop):
        return lax.ppermute(piece, "blk", [(i, 2 * hop(i // 2) + i % 2) for i in range(n)])

    first, second, own_beside = step(rows, after), step(rows, before), beside(rows)
    first_beside = beside(first)
    third = step(lax.optimization_barrier((first, own_beside))[0], after)
    third_beside = step(first_beside, after)
    second_beside = beside(second)
    return [
        ("own", rows),
        ("own beside", own_beside),
        ("second", second),
        ("second beside", second_beside),
        ("third", third),
        ("third beside", third_beside),
        ("first", first),
        ("first beside", first_beside),
    ]


def place_pieces(panel, blk, rows, names, pieces):
    got = dict(zip(names, pieces))
    if "all" in got:
        panel[...] = got["all"][...]
        return
    pair, side = blk // 2, lax.rem(blk, 2)
    came = {"own": pair, "first": before(pair), "second": after(pair), "third": before(before(pair))}
    for name, source in came.items():
        for which, other in ((name, 0), (name + " beside", 1)):
            start = (2 * source + lax.bitwise_xor(side, other)) * rows
            panel[pl.ds(pl.multiple_of(start, rows), rows), :] = got[which][...]


def add_blocks(columns, tiles, panel, out, owners):
    per_owner = out.shape[0] // (BLOCK * len(owners))
    slots_here = range(tiles.shape[2])
    for j, owner in enumerate(owners):
        numbers = columns[pl.ds(owner * per_owner, per_owner), :]
        for i in range(per_owner):
            starts = [pl.multiple_of(numbers[i, k] * BLOCK, BLOCK) for k in slots_here]
            left = jnp.concatenate([tiles[owner * per_owner + i, 0, k] for k in slots_here], axis=1)
            right = jnp.concatenate([panel[pl.ds(start, BLOCK), :] for start in starts], axis=0)
            summed = jnp.dot(left, right, preferred_element_type=jnp.float32)
            out[pl.ds((j * per_owner + i) * BLOCK, BLOCK), :] = summed.astype(out.dtype)


def other_kernel(names, reps, columns, tiles, *refs):
    pieces, panel, out = refs[: len(names)], refs[-2], refs[-1]
    blk, rep = lax.axis_index("blk"), lax.axis_index("rep")
    place_pieces(panel, blk, tiles.shape[0] * BLOCK // reps, names, pieces)
    add_blocks(columns, tiles, panel, out, [lax.bitwise_xor(rep, d) for d in range(3, reps, 2)])


def other_sums(gathered, adj_tiles, columns):
    reps = lax.axis_size("rep")
    names, pieces = zip(*gathered)
    width = pieces[0].shape[1]
    rows = adj_tiles.shape[0] * BLOCK // reps
    length = lax.axis_size("blk") * rows
    return pl.pallas_call(
        functools.partial(other_kernel, names, reps),
        out_shape=[
            jax.ShapeDtypeStruct((length, width), jnp.bfloat16),
            jax.ShapeDtypeStruct((rows * (reps // 2 - 1), width), jnp.bfloat16),
        ],
        in_specs=[VMEM, VMEM] + [VMEM] * len(pieces),
        out_specs=[VMEM] * 2,
        compiler_params=pltpu.CompilerParams(vmem_limit_bytes=32 * 1024 * 1024),
        cost_estimate=product_cost(adj_tiles, width, reps),
        name="other_sums",
    )(columns, adj_tiles, *pieces)


def sums_kernel(owners, columns, tiles, panel, out):
    rep = lax.axis_index("rep")
    add_blocks(columns, tiles, panel, out, [lax.bitwise_xor(rep, d) for d in owners])


def sums(panel, adj_tiles, columns, owners, kind, name):
    reps = lax.axis_size("rep")
    rows, width = adj_tiles.shape[0] * BLOCK // reps * len(owners), panel.shape[1]
    return pl.pallas_call(
        functools.partial(sums_kernel, owners),
        out_shape=jax.ShapeDtypeStruct((rows, width), kind),
        in_specs=[VMEM, VMEM, VMEM],
        out_specs=VMEM,
        compiler_params=pltpu.CompilerParams(vmem_limit_bytes=32 * 1024 * 1024),
        cost_estimate=product_cost(adj_tiles, width, reps),
        name=name,
    )(columns, adj_tiles, panel)


def product_cost(adj_tiles, width, reps):
    size = adj_tiles.size // reps
    return pl.CostEstimate(flops=2 * size * width, bytes_accessed=2 * size, transcendentals=0)


def add_cores_kernel(own, core, *outs):
    rows = outs[0].shape[0]
    for j, out in enumerate(outs):
        part = pl.ds(j * rows, rows)
        out[...] = (own[part, :] + core[part, :].astype(jnp.float32)).astype(jnp.bfloat16)


def add_cores(own, core, rows):
    width = own.shape[1]
    return pl.pallas_call(
        add_cores_kernel,
        out_shape=[jax.ShapeDtypeStruct((rows, width), jnp.bfloat16)] * (own.shape[0] // rows),
        in_specs=[VMEM] * 2,
        out_specs=[VMEM] * (own.shape[0] // rows),
        compiler_params=pltpu.CompilerParams(vmem_limit_bytes=32 * 1024 * 1024),
        name="add_cores",
    )(own, core)


def tile_products(pieces, adj_tiles, columns, rows):
    reps = lax.axis_size("rep")
    other = [(i, i ^ 1) for i in range(reps)]
    panel, across = other_sums(pieces, adj_tiles, columns)
    core = lax.ppermute(across, "rep", other)
    own = sums(panel, adj_tiles, columns, range(2, reps, 2), jnp.float32, "own_far")
    parts = add_cores(own, core, rows)
    panel, parts = lax.optimization_barrier((panel, parts))
    far = []
    for j, part in enumerate(parts, 1):
        far.append(lax.ppermute(part, "rep", [(i, i ^ (2 * j)) for i in range(reps)]))
    near = sums(panel, adj_tiles, columns, [0], jnp.float32, "own_near")
    panel, near = lax.optimization_barrier((panel, near))
    beside = lax.ppermute(sums(panel, adj_tiles, columns, [1], jnp.bfloat16, "near_other"), "rep", other)
    terms = [near, *far, beside]
    return terms


def add_terms(terms, rows):
    total = terms[0][...].astype(jnp.float32)
    for term in terms[1:]:
        total = total + term[...].astype(jnp.float32)
    return total


def contract(a, b, dims):
    return lax.dot_general(a, b, ((dims[:1], dims[1:]), ((), ())), preferred_element_type=jnp.float32)


def by_row_kernel(by_slot, columns):
    columns[...] = jnp.zeros_like(columns)
    columns[pl.ds(0, by_slot.shape[1]), :] = jnp.transpose(by_slot[...])


def by_row(by_slot):
    per_row, rows = by_slot.shape
    return pl.pallas_call(
        by_row_kernel,
        out_shape=jax.ShapeDtypeStruct((rows + 8, per_row), jnp.int32),
        in_specs=[VMEM],
        out_specs=VMEM,
        compiler_params=pltpu.CompilerParams(vmem_limit_bytes=32 * 1024 * 1024),
        cost_estimate=pl.CostEstimate(flops=BESIDE, bytes_accessed=by_slot.size, transcendentals=0),
        name="by_row",
    )(by_slot)


def early_kernel(cot, w_out, g_hidden):
    g_hidden[...] = contract(cot[...], w_out[...], (1, 1))


def early(cot_out, w_out):
    rows, width = cot_out.shape
    units = w_out.shape[0]
    return pl.pallas_call(
        early_kernel,
        out_shape=jax.ShapeDtypeStruct((rows, units), jnp.float32),
        in_specs=[VMEM] * 2,
        out_specs=VMEM,
        compiler_params=pltpu.CompilerParams(vmem_limit_bytes=32 * 1024 * 1024),
        cost_estimate=pl.CostEstimate(
            flops=2 * rows * width * units, bytes_accessed=8 * rows * units, transcendentals=0
        ),
        name="early",
    )(cot_out, w_out)


def node_pre(terms, rows, w_in, b_in):
    agg_b = add_terms(terms, rows).astype(jnp.bfloat16)
    pre = contract(agg_b, w_in[...], (1, 0)) + b_in[...]
    return pre, 0.5 * jnp.tanh(0.5 * pre) + 0.5


def node_kernel(n_terms, *refs):
    terms = refs[:n_terms]
    g_hidden, w_in, b_in, g_out = refs[n_terms:]
    pre, sigma = node_pre(terms, g_out.shape[0], w_in, b_in)
    g_pre = (g_hidden[...] * sigma * (1.0 + pre * (1.0 - sigma))).astype(jnp.bfloat16)
    g_out[...] = contract(g_pre, w_in[...], (1, 1)).astype(jnp.bfloat16)


def node_update(terms, g_hidden, w_in, b_in):
    rows, units = g_hidden.shape
    width = w_in.shape[0]
    return pl.pallas_call(
        functools.partial(node_kernel, len(terms)),
        out_shape=jax.ShapeDtypeStruct((rows, width), jnp.bfloat16),
        in_specs=[VMEM] * (len(terms) + 3),
        out_specs=VMEM,
        compiler_params=pltpu.CompilerParams(vmem_limit_bytes=32 * 1024 * 1024),
        cost_estimate=pl.CostEstimate(
            flops=4 * rows * width * units, bytes_accessed=8 * rows * units, transcendentals=rows * units
        ),
        name="node_update",
    )(*terms, g_hidden, w_in, b_in.reshape(1, -1))


def project_kernel(n_terms, *refs):
    terms = refs[:n_terms]
    feats, w_in, b_in, w_out, b_out, out = refs[n_terms:]
    pre, sigma = node_pre(terms, out.shape[0], w_in, b_in)
    projected = contract((pre * sigma).astype(jnp.bfloat16), w_out[...], (1, 0)) + b_out[...]
    out[...] = (feats[...].astype(jnp.float32) + projected).astype(jnp.bfloat16)


def project(terms, node_feats, w_in, b_in, w_out, b_out):
    rows, width = node_feats.shape
    units = w_in.shape[1]
    return pl.pallas_call(
        functools.partial(project_kernel, len(terms)),
        out_shape=jax.ShapeDtypeStruct((rows, width), jnp.bfloat16),
        in_specs=[VMEM] * (len(terms) + 5),
        out_specs=VMEM,
        compiler_params=pltpu.CompilerParams(vmem_limit_bytes=32 * 1024 * 1024),
        cost_estimate=pl.CostEstimate(
            flops=4 * rows * width * units, bytes_accessed=2 * rows * units, transcendentals=rows * units
        ),
        name="project",
    )(*terms, node_feats, w_in, b_in.reshape(1, -1), w_out, b_out.reshape(1, -1))


def close_kernel(n_terms, *refs):
    cot, out = refs[n_terms:]
    total = add_terms(refs[:n_terms], out.shape[0])
    out[...] = (cot[...].astype(jnp.float32) + total).astype(jnp.bfloat16)


def close_grad(terms, cot_out):
    return pl.pallas_call(
        functools.partial(close_kernel, len(terms)),
        out_shape=jax.ShapeDtypeStruct(cot_out.shape, jnp.bfloat16),
        in_specs=[VMEM] * (len(terms) + 1),
        out_specs=VMEM,
        compiler_params=pltpu.CompilerParams(vmem_limit_bytes=32 * 1024 * 1024),
        name="close_grad",
    )(*terms, cot_out)


def local(node_feats, adj_tiles, col_index, w_in, b_in, w_out, b_out, cot_out):
    rows = node_feats.shape[0]
    columns = by_row(jnp.transpose(col_index, (1, 2, 0))[0])
    g_hidden = early(cot_out, lax.optimization_barrier((w_out, columns))[0])
    columns, g_hidden = lax.optimization_barrier((columns, g_hidden))
    terms = tile_products(gather_blocks(node_feats), adj_tiles, columns, rows)
    g_agg = node_update(terms, g_hidden, w_in, b_in)
    out_feats = project(terms, node_feats, w_in, b_in, w_out, b_out)
    terms = tile_products(gather_blocks(g_agg), adj_tiles, columns, rows)
    return (out_feats, close_grad(terms, cot_out))


def solution(mesh):
    placed = (
        P(("blk", "rep"), None),
        P("blk", "rep", None, None, None),
        P("blk", "rep", None),
        P(),
        P(),
        P(),
        P(),
        P(("blk", "rep"), None),
    )
    return jax.shard_map(
        local,
        mesh=mesh,
        in_specs=placed,
        out_specs=(P(("blk", "rep"), None), P(("blk", "rep"), None)),
        check_vma=False,
    )
```
